128 devices in a mesh: fsdp: 16 (over y, x_lo, core), seq: 8 (over z, x_hi).
Axes of the slice: x: 4 (x_hi: 2, x_lo: 2; x = x_hi * 2 + x_lo), y: 4, z: 4, core: 2. Of those that a mesh axis runs over, the one named last changes fastest.
Arguments:
- hidden: float32 [16, 1024, 1536], P('fsdp', 'seq'), may hold values from -6 to 6
- cotangent: float32 [16, 1024, 1536], P('fsdp', 'seq'), may hold values from -6 to 6
- routes: int32 [16, 1024, 6], P('fsdp', 'seq'), may hold values from 0 to 7, all different within a row
- head_params: float32 [3, 48], replicated, may hold values from -5 to 3.41
- head_first: float32 [3, 48], replicated
- head_second: float32 [3, 48], replicated
- small_params: float32 [22784], P(('fsdp', 'seq')), may hold values from -1.5 to 1.5
- small_first: float32 [22784], P(('fsdp', 'seq'))
- small_second: float32 [22784], P(('fsdp', 'seq'))
- proj_weight: float32 [1536, 6448], P(('fsdp', 'seq')), may hold values from -0.15625 to 0.15625
- proj_first: float32 [1536, 6448], P(('fsdp', 'seq'))
- proj_second: float32 [1536, 6448], P(('fsdp', 'seq'))
- out_weight: float32 [3072, 1536], P(('fsdp', 'seq')), may hold values from -0.109375 to 0.109375
- out_first: float32 [3072, 1536], P(('fsdp', 'seq'))
- out_second: float32 [3072, 1536], P(('fsdp', 'seq'))
- router_weight: float32 [1536, 8], P(('fsdp', 'seq')), may hold values from -0.078125 to 0.078125
- router_first: float32 [1536, 8], P(('fsdp', 'seq'))
- router_second: float32 [1536, 8], P(('fsdp', 'seq'))
- experts_up: float32 [1536, 8, 1024], P('fsdp', 'seq'), may hold values from -0.15625 to 0.15625
- experts_up_first: float32 [1536, 8, 1024], P('fsdp', 'seq')
- experts_up_second: float32 [1536, 8, 1024], P('fsdp', 'seq')
- experts_down: float32 [512, 8, 1536], P('fsdp', 'seq'), may hold values from -1 to 1
- experts_down_first: float32 [512, 8, 1536], P('fsdp', 'seq')
- experts_down_second: float32 [512, 8, 1536], P('fsdp', 'seq')
- shared_up: float32 [1536, 2048], P(('fsdp', 'seq')), may hold values from -0.15625 to 0.15625
- shared_up_first: float32 [1536, 2048], P(('fsdp', 'seq'))
- shared_up_second: float32 [1536, 2048], P(('fsdp', 'seq'))
- shared_down: float32 [1024, 1536], P(('fsdp', 'seq')), may hold values from -0.375 to 0.375
- shared_down_first: float32 [1024, 1536], P(('fsdp', 'seq'))
- shared_down_second: float32 [1024, 1536], P(('fsdp', 'seq'))
Outputs:
- block_out: float32 [16, 1024, 1536], P('fsdp', 'seq')
- hidden_grad: float32 [16, 1024, 1536], P('fsdp', 'seq')
- head_params_new: float32 [3, 48], replicated
- head_first_new: float32 [3, 48], replicated
- head_second_new: float32 [3, 48], replicated
- small_params_new: float32 [22784], P(('fsdp', 'seq'))
- small_first_new: float32 [22784], P(('fsdp', 'seq'))
- small_second_new: float32 [22784], P(('fsdp', 'seq'))
- proj_weight_new: float32 [1536, 6448], P(('fsdp', 'seq'))
- proj_first_new: float32 [1536, 6448], P(('fsdp', 'seq'))
- proj_second_new: float32 [1536, 6448], P(('fsdp', 'seq'))
- out_weight_new: float32 [3072, 1536], P(('fsdp', 'seq'))
- out_first_new: float32 [3072, 1536], P(('fsdp', 'seq'))
- out_second_new: float32 [3072, 1536], P(('fsdp', 'seq'))
- router_weight_new: float32 [1536, 8], P(('fsdp', 'seq'))
- router_first_new: float32 [1536, 8], P(('fsdp', 'seq'))
- router_second_new: float32 [1536, 8], P(('fsdp', 'seq'))
- experts_up_new: float32 [1536, 8, 1024], P('fsdp', 'seq')
- experts_up_first_new: float32 [1536, 8, 1024], P('fsdp', 'seq')
- experts_up_second_new: float32 [1536, 8, 1024], P('fsdp', 'seq')
- experts_down_new: float32 [512, 8, 1536], P('fsdp', 'seq')
- experts_down_first_new: float32 [512, 8, 1536], P('fsdp', 'seq')
- experts_down_second_new: float32 [512, 8, 1536], P('fsdp', 'seq')
- shared_up_new: float32 [1536, 2048], P(('fsdp', 'seq'))
- shared_up_first_new: float32 [1536, 2048], P(('fsdp', 'seq'))
- shared_up_second_new: float32 [1536, 2048], P(('fsdp', 'seq'))
- shared_down_new: float32 [1024, 1536], P(('fsdp', 'seq'))
- shared_down_first_new: float32 [1024, 1536], P(('fsdp', 'seq'))
- shared_down_second_new: float32 [1024, 1536], P(('fsdp', 'seq'))
The draws below stay inside these ranges and needn't reach their ends.
Inputs may be any that keep to these rules, and one draw needn't show every extreme that they name: `routes`: each position names 6 different experts, and every expert is named somewhere.
All inputs are finite; a program needn't handle non-finite values.
Results may differ from the reference program's by a relative error of at most 0.02.
Values may be sent and summed in bfloat16 or wider, within the bound.
A program may use at most 256 MiB of HBM per device.

```python
import math
import jax
import jax.numpy as jnp
from jax import lax

D = 1536
HEADS = 48
HDIM = 64
STATE = 128
CONV = 4
FF_EXP = 512
FF_SH = 1024
TOPK = 6
EXPERTS = 8
SEQ_LEN = 1024
STEP = 5
INNER = 3072
CHANNELS = 3328
PROJ = 6448
SMALL = 22784
BATCH = 16
TOKENS = 16384


def make_first_state(key, array_shape, factor):
    spread = factor * math.sqrt(TOKENS) * (1.0 - 0.9) / 0.9
    return spread * jax.random.truncated_normal(key, -3.0, 3.0, array_shape, jnp.float32)


def make_second_state(key, array_shape, factor):
    base_level = factor * factor * TOKENS * 2.0 * (1.0 - 0.95) / 0.95
    return base_level * jnp.exp(jax.random.uniform(key, array_shape, jnp.float32, -math.log(2.0), math.log(2.0)))


def draw_head_params(key, part):
    key = jax.random.fold_in(key, 1)
    subkeys = jax.random.split(key, 3)
    offsets = jax.random.uniform(subkeys[0], (HEADS,), jnp.float32, -5.0, -3.0)
    log_rates = jax.random.uniform(subkeys[1], (HEADS,), jnp.float32, math.log(0.05), math.log(30.0))
    skip_gains = jax.random.uniform(subkeys[2], (HEADS,), jnp.float32, 0.5, 1.5)
    return jnp.stack([offsets, log_rates, skip_gains])


def draw_head_first(key, part):
    key = jax.random.fold_in(key, 2)
    return make_first_state(key, (3, HEADS), 20.0)


def draw_head_second(key, part):
    key = jax.random.fold_in(key, 3)
    return make_second_state(key, (3, HEADS), 20.0)


def draw_small_params(key, part):
    key = jax.random.fold_in(key, 4)
    subkeys = jax.random.split(key, 3)
    gain_values = jax.random.uniform(subkeys[0], (2 * D + INNER,), jnp.float32, 0.6, 1.4)
    biases = 0.3 * jax.random.truncated_normal(subkeys[1], -3.0, 3.0, (CHANNELS,), jnp.float32)
    taps_all = 0.5 * jax.random.truncated_normal(subkeys[2], -3.0, 3.0, (CONV * CHANNELS,), jnp.float32)
    return jnp.concatenate([gain_values, biases, taps_all])


def draw_small_first(key, part):
    key = jax.random.fold_in(key, 5)
    return make_first_state(key, (SMALL,), 3.0)


def draw_small_second(key, part):
    key = jax.random.fold_in(key, 6)
    return make_second_state(key, (SMALL,), 3.0)


def draw_proj_first(key, part):
    key = jax.random.fold_in(key, 7)
    return make_first_state(key, (D, PROJ), 2.0)


def draw_proj_second(key, part):
    key = jax.random.fold_in(key, 8)
    return make_second_state(key, (D, PROJ), 2.0)


def draw_out_first(key, part):
    key = jax.random.fold_in(key, 9)
    return make_first_state(key, (INNER, D), 2.0)


def draw_out_second(key, part):
    key = jax.random.fold_in(key, 10)
    return make_second_state(key, (INNER, D), 2.0)


def draw_router_first(key, part):
    key = jax.random.fold_in(key, 11)
    return make_first_state(key, (D, EXPERTS), 30.0)


def draw_router_second(key, part):
    key = jax.random.fold_in(key, 12)
    return make_second_state(key, (D, EXPERTS), 30.0)


def draw_experts_up_first(key, part):
    key = jax.random.fold_in(key, 13)
    return make_first_state(key, (D, EXPERTS, 2 * FF_EXP), 1.0)


def draw_experts_up_second(key, part):
    key = jax.random.fold_in(key, 14)
    return make_second_state(key, (D, EXPERTS, 2 * FF_EXP), 1.0)


def draw_experts_down_first(key, part):
    key = jax.random.fold_in(key, 15)
    return make_first_state(key, (FF_EXP, EXPERTS, D), 0.2)


def draw_experts_down_second(key, part):
    key = jax.random.fold_in(key, 16)
    return make_second_state(key, (FF_EXP, EXPERTS, D), 0.2)


def draw_shared_up_first(key, part):
    key = jax.random.fold_in(key, 17)
    return make_first_state(key, (D, 2 * FF_SH), 2.0)


def draw_shared_up_second(key, part):
    key = jax.random.fold_in(key, 18)
    return make_second_state(key, (D, 2 * FF_SH), 2.0)


def draw_shared_down_first(key, part):
    key = jax.random.fold_in(key, 19)
    return make_first_state(key, (FF_SH, D), 1.0)


def draw_shared_down_second(key, part):
    key = jax.random.fold_in(key, 20)
    return make_second_state(key, (FF_SH, D), 1.0)


def block_levels(rng, shape, pieces, low, high):
    def one(dim, shards_of):
        draws = jax.random.uniform(jax.random.fold_in(jax.random.fold_in(rng, 6), dim), (shards_of,), jnp.float32, low / len(pieces), high / len(pieces))
        return jnp.repeat(jnp.exp(draws), shape[dim] // shards_of).reshape((-1,) + (1,) * (len(shape) - dim - 1))

    gain = one(*pieces[0])
    for cut in pieces[1:]:
        gain = gain * one(*cut)
    return gain


def distinct(rng, rows, count, top, lift):
    order = jax.random.permutation(jax.random.fold_in(rng, 1), count)
    pull = order
    for power in range(3):
        pull = pull * pull // count
    pull = pull * lift // count
    lots = jax.random.randint(jax.random.fold_in(rng, 2), (rows, count), 0, 4096) + pull
    holders = jax.random.permutation(jax.random.fold_in(rng, 3), rows)[jnp.arange(count) % rows]
    lots = jnp.where(jnp.arange(rows)[:, None] == holders[None, :], 1 << 14, lots)
    priority = lots * count + jnp.arange(count)
    return lax.top_k(priority.astype(jnp.int32), top)[1].astype(jnp.int32)


def noise(stream_key, extent, deviation, limit, shards=(), kind=jnp.bfloat16):
    values = deviation * jax.random.normal(stream_key, extent, jnp.float32)
    if shards:
        values = values * block_levels(stream_key, extent, shards, -0.22, 0.18)
    return jnp.clip(values, -limit, limit).astype(kind)


def setup_inputs(seed: int = 0) -> dict:
    seeds = jax.random.split(jax.random.key(seed), 31)
    hidden = noise(seeds[0], (BATCH, SEQ_LEN, D), 1.0, 6.0, ((0, 16), (1, 8)), jnp.float32)
    cotangent = noise(seeds[1], (BATCH, SEQ_LEN, D), 1.0, 6.0, ((0, 16), (1, 8)), jnp.float32)
    routes = distinct(seeds[2], BATCH * SEQ_LEN, EXPERTS, TOPK, 0).reshape((BATCH, SEQ_LEN, TOPK))
    head_params = draw_head_params(jax.random.fold_in(seeds[30], 71), 0)
    head_first = draw_head_first(jax.random.fold_in(seeds[30], 71), 0)
    head_second = draw_head_second(jax.random.fold_in(seeds[30], 71), 0)
    small_params = draw_small_params(jax.random.fold_in(seeds[30], 71), 0)
    small_first = draw_small_first(jax.random.fold_in(seeds[30], 71), 0)
    small_second = draw_small_second(jax.random.fold_in(seeds[30], 71), 0)
    proj_weight = noise(seeds[9], (D, PROJ), D ** -0.5, 0.15625, ((0, 128),), jnp.float32)
    proj_first = draw_proj_first(jax.random.fold_in(seeds[30], 71), 0)
    proj_second = draw_proj_second(jax.random.fold_in(seeds[30], 71), 0)
    out_weight = noise(seeds[12], (INNER, D), INNER ** -0.5, 0.109375, ((0, 128),), jnp.float32)
    out_first = draw_out_first(jax.random.fold_in(seeds[30], 71), 0)
    out_second = draw_out_second(jax.random.fold_in(seeds[30], 71), 0)
    router_weight = noise(seeds[15], (D, EXPERTS), (4 * D) ** -0.5, 0.078125, ((0, 128),), jnp.float32)
    router_first = draw_router_first(jax.random.fold_in(seeds[30], 71), 0)
    router_second = draw_router_second(jax.random.fold_in(seeds[30], 71), 0)
    experts_up = noise(seeds[18], (D, EXPERTS, 2 * FF_EXP), D ** -0.5, 0.15625, ((0, 16), (1, 8)), jnp.float32)
    experts_up_first = draw_experts_up_first(jax.random.fold_in(seeds[30], 71), 0)
    experts_up_second = draw_experts_up_second(jax.random.fold_in(seeds[30], 71), 0)
    experts_down = noise(seeds[21], (FF_EXP, EXPERTS, D), (FF_EXP // 16) ** -0.5, 1.0, ((0, 16), (1, 8)), jnp.float32)
    experts_down_first = draw_experts_down_first(jax.random.fold_in(seeds[30], 71), 0)
    experts_down_second = draw_experts_down_second(jax.random.fold_in(seeds[30], 71), 0)
    shared_up = noise(seeds[24], (D, 2 * FF_SH), D ** -0.5, 0.15625, ((0, 128),), jnp.float32)
    shared_up_first = draw_shared_up_first(jax.random.fold_in(seeds[30], 71), 0)
    shared_up_second = draw_shared_up_second(jax.random.fold_in(seeds[30], 71), 0)
    shared_down = noise(seeds[27], (FF_SH, D), (FF_SH // 4) ** -0.5, 0.375, ((0, 128),), jnp.float32)
    shared_down_first = draw_shared_down_first(jax.random.fold_in(seeds[30], 71), 0)
    shared_down_second = draw_shared_down_second(jax.random.fold_in(seeds[30], 71), 0)
    return dict(hidden=hidden, cotangent=cotangent, routes=routes, head_params=head_params, head_first=head_first, head_second=head_second, small_params=small_params, small_first=small_first, small_second=small_second, proj_weight=proj_weight, proj_first=proj_first, proj_second=proj_second, out_weight=out_weight, out_first=out_first, out_second=out_second, router_weight=router_weight, router_first=router_first, router_second=router_second, experts_up=experts_up, experts_up_first=experts_up_first, experts_up_second=experts_up_second, experts_down=experts_down, experts_down_first=experts_down_first, experts_down_second=experts_down_second, shared_up=shared_up, shared_up_first=shared_up_first, shared_up_second=shared_up_second, shared_down=shared_down, shared_down_first=shared_down_first, shared_down_second=shared_down_second)


NORM_EPSILON = 1e-05
BETA_FIRST = 0.9
BETA_SECOND = 0.95
ADAM_EPSILON = 1e-08
RATE_MATRIX = 0.04
RATE_DOWN = 0.1
RATE_SMALL = 0.3
RATE_HEAD = 1.0
WEIGHT_DECAY = 0.1
HIGHEST = lax.Precision.HIGHEST

@jax.custom_vjp
def low(v):
    return lax.optimization_barrier(v.astype(jnp.bfloat16)).astype(jnp.float32)

@jax.custom_vjp
def low_back(v):
    return v

def low_keep(v):
    return (low(v), None)

def low_pass(kept, grad):
    return (grad,)

def back_keep(v):
    return (v, None)

def back_low(kept, grad):
    return (low(grad),)
low.defvjp(low_keep, low_pass)
low_back.defvjp(back_keep, back_low)

def rms_scale(values, gain_vec):
    return values * lax.rsqrt(lax.optimization_barrier(jnp.mean(values * values, axis=-1, keepdims=True)) + NORM_EPSILON) * gain_vec

def conv_silu(inputs, kernel, offsets):
    length = inputs.shape[-2]
    kernel_size = kernel.shape[0]
    padded = jnp.pad(inputs, [(0, 0)] * (inputs.ndim - 2) + [(kernel_size - 1, 0), (0, 0)])
    running = offsets
    for offset_index in range(kernel_size):
        running = running + kernel[offset_index] * lax.slice_in_dim(padded, offset_index, offset_index + length, axis=inputs.ndim - 2)
    return jax.nn.silu(running)

def silu_gate(values, half_width):
    return jax.nn.silu(values[..., :half_width]) * values[..., half_width:]

def route_combine(logit_values, onehot):
    picked = lax.optimization_barrier(jnp.sum(logit_values[:, None, :] * onehot, axis=-1))
    route_probs = jax.nn.softmax(picked, axis=-1)
    return lax.optimization_barrier(jnp.sum(route_probs[:, :, None] * onehot, axis=1))

def split_small(small_vec):
    cut_three = 2 * D + INNER
    cut_four = cut_three + CHANNELS
    return (small_vec[:D], small_vec[D:2 * D], small_vec[2 * D:cut_three], small_vec[cut_three:cut_four], small_vec[cut_four:].reshape(CONV, CHANNELS))

def head_apply(operands, scores_in):
    cum_head, rate_head, x_head = operands
    lower_mask = jnp.tril(jnp.ones((SEQ_LEN, SEQ_LEN), dtype=bool))
    decay_matrix = jnp.exp(jnp.where(lower_mask, cum_head[:, None] - cum_head[None, :], 0.0))
    weight_matrix = jnp.where(lower_mask, scores_in * decay_matrix, 0.0) * rate_head[None, :]
    return low_back(jnp.dot(low(weight_matrix), x_head, precision=HIGHEST))

def layer(inputs, onehot, head_params, small_params, proj_weight, out_weight, router_weight, experts_up, experts_down, shared_up, shared_down):
    gain_first, gain_second, gain_mixer, conv_bias, conv_kernel = split_small(low(small_params))
    normed = low(rms_scale(inputs, gain_first))
    projected = low_back(low(jnp.dot(normed, low(proj_weight), precision=HIGHEST)))
    gate_z = projected[:, :INNER]
    conv_input = projected[:, INNER:INNER + CHANNELS]
    rate_raw = projected[:, INNER + CHANNELS:]
    activated = low(conv_silu(conv_input, conv_kernel, conv_bias))
    x_act = activated[:, :INNER]
    b_state = activated[:, INNER:INNER + STATE]
    c_state = activated[:, INNER + STATE:]
    step_sizes = jax.nn.softplus(rate_raw + head_params[0])
    cumulative = jnp.cumsum(step_sizes * -jnp.exp(head_params[1]), axis=0)
    scores = jnp.dot(c_state, b_state.T, precision=HIGHEST)
    checked = jax.checkpoint(head_apply)
    per_head = lax.map(lambda operands: checked(operands, scores), (cumulative.T, step_sizes.T, jnp.transpose(x_act.reshape(SEQ_LEN, HEADS, HDIM), (1, 0, 2))))
    mixed_out = jnp.transpose(per_head, (1, 0, 2)).reshape(SEQ_LEN, INNER)
    mixed_out = mixed_out + x_act * jnp.repeat(head_params[2], HDIM)
    gated_out = low_back(low(mixed_out * jax.nn.silu(gate_z)))
    gated_normed = low(rms_scale(gated_out, gain_mixer))
    mixer_out = low_back(jnp.dot(gated_normed, low(out_weight), precision=HIGHEST))
    middle = inputs + mixer_out
    normed_two = low(rms_scale(middle, gain_second))
    logits = low_back(jnp.dot(normed_two, low(router_weight), precision=HIGHEST))
    combine = route_combine(logits, onehot)
    expert_gu = low_back(jnp.einsum('td,def->etf', normed_two, low(experts_up), precision=HIGHEST))
    expert_act = low(silu_gate(expert_gu, FF_EXP))
    expert_out = low_back(jnp.einsum('etf,fed->etd', expert_act, low(experts_down), precision=HIGHEST))
    routed = jnp.einsum('te,etd->td', combine, expert_out, precision=HIGHEST)
    shared_gu = low_back(jnp.dot(normed_two, low(shared_up), precision=HIGHEST))
    shared_act = low(silu_gate(shared_gu, FF_SH))
    shared_out = low_back(jnp.dot(shared_act, low(shared_down), precision=HIGHEST))
    return middle + routed + shared_out

def adam_update(weight, old_first, old_second, gradient, step_rate, decay_rate):
    first_new = BETA_FIRST * old_first + (1.0 - BETA_FIRST) * gradient
    second_new = BETA_SECOND * old_second + (1.0 - BETA_SECOND) * gradient * gradient
    first_hat = first_new / (1.0 - BETA_FIRST ** STEP)
    second_hat = second_new / (1.0 - BETA_SECOND ** STEP)
    weight_new = weight - step_rate * (first_hat / (jnp.sqrt(second_hat) + ADAM_EPSILON) + decay_rate * weight)
    return (weight_new, first_new, second_new)

def reference(hidden, cotangent, routes, head_params, head_first, head_second, small_params, small_first, small_second, proj_weight, proj_first, proj_second, out_weight, out_first, out_second, router_weight, router_first, router_second, experts_up, experts_up_first, experts_up_second, experts_down, experts_down_first, experts_down_second, shared_up, shared_up_first, shared_up_second, shared_down, shared_down_first, shared_down_second):
    weights = (head_params, small_params, proj_weight, out_weight, router_weight, experts_up, experts_down, shared_up, shared_down)
    onehots = (routes[..., None] == jnp.arange(EXPERTS, dtype=jnp.int32)).astype(jnp.float32)

    def per_sequence(totals, operands):
        inputs, cotangent_seq, onehot = operands
        block_seq, pullback = jax.vjp(lambda values, *params: layer(values, onehot, *params), inputs, *weights)
        gradients = pullback(cotangent_seq)
        return (tuple((running + gradient for running, gradient in zip(totals, gradients[1:]))), (block_seq, gradients[0]))
    zero_grads = tuple((jnp.zeros_like(weight) for weight in weights))
    totals, (block_out, hidden_grad) = lax.scan(per_sequence, zero_grads, (hidden, cotangent, onehots))
    head_new = adam_update(head_params, head_first, head_second, totals[0], RATE_HEAD, 0.0)
    small_new = adam_update(small_params, small_first, small_second, totals[1], RATE_SMALL, 0.0)
    proj_new = adam_update(proj_weight, proj_first, proj_second, totals[2], RATE_MATRIX, WEIGHT_DECAY)
    out_new = adam_update(out_weight, out_first, out_second, totals[3], RATE_MATRIX, WEIGHT_DECAY)
    router_new = adam_update(router_weight, router_first, router_second, totals[4], RATE_MATRIX, WEIGHT_DECAY)
    up_new = adam_update(experts_up, experts_up_first, experts_up_second, totals[5], RATE_MATRIX, WEIGHT_DECAY)
    down_new = adam_update(experts_down, experts_down_first, experts_down_second, totals[6], RATE_DOWN, WEIGHT_DECAY)
    shared_up_new = adam_update(shared_up, shared_up_first, shared_up_second, totals[7], RATE_MATRIX, WEIGHT_DECAY)
    shared_down_new = adam_update(shared_down, shared_down_first, shared_down_second, totals[8], RATE_MATRIX, WEIGHT_DECAY)
    return (block_out, hidden_grad, head_new[0], head_new[1], head_new[2], small_new[0], small_new[1], small_new[2], proj_new[0], proj_new[1], proj_new[2], out_new[0], out_new[1], out_new[2], router_new[0], router_new[1], router_new[2], up_new[0], up_new[1], up_new[2], down_new[0], down_new[1], down_new[2], shared_up_new[0], shared_up_new[1], shared_up_new[2], shared_down_new[0], shared_down_new[1], shared_down_new[2])
```

```python
import functools

import jax
import jax.numpy as jnp
from jax import lax
from jax.experimental import pallas as pl
from jax.experimental.pallas import tpu as pltpu
from jax.sharding import PartitionSpec as P

D = 1536
HEADS = 48
HDIM = 64
STATE = 128
CONV = 4
FF_EXP = 512
FF_SH = 1024
TOPK = 6
EXPERTS = 8
STEP = 5
INNER = 3072
CHANNELS = 3328
SMALL = 22784
GROUPS = 8
SHARDS = 16
HEADS_HERE = HEADS // GROUPS
INNER_HERE = INNER // GROUPS
SH_HERE = FF_SH // GROUPS
SEQ_LEN = 1024
PIECE = SEQ_LEN // GROUPS
CONV_HERE = INNER_HERE + 2 * STATE
PROJ_HERE = INNER_HERE + CONV_HERE + 128
SMALL_COLS = 15


NORM_EPSILON = 1e-05
BETA_FIRST = 0.9
BETA_SECOND = 0.95
ADAM_EPSILON = 1e-08
RATE_MATRIX = 0.04
RATE_DOWN = 0.1
RATE_SMALL = 0.3
RATE_HEAD = 1.0
WEIGHT_DECAY = 0.1
HIGHEST = lax.Precision.HIGHEST
LOW = jnp.bfloat16
FULL = jnp.float32
MESH = pl.DeviceIdType.MESH


def hi_lo(values):
    high = values.astype(LOW)
    return high, (values - high.astype(FULL)).astype(LOW)


BUSY = pl.CostEstimate(flops=30_000_000_000, bytes_accessed=4_000_000, transcendentals=0)


def seq_axis():
    me = lax.axis_index("seq")
    side, level = lax.rem(me, 2), lax.div(me, 2)

    def slot(up, other):
        return lax.rem(level + up + 4, 4) * 2 + (1 - side if other else side)

    return me, slot, lambda up, other: {"seq": slot(up, other)}


def fsdp_axis():
    me = lax.axis_index("fsdp")
    core, rest = lax.rem(me, 2), lax.div(me, 2)
    side, level = lax.rem(rest, 2), lax.div(rest, 2)

    def slot(up, other):
        return lax.rem(level + up + 4, 4) * 2 + (1 - side if other else side)

    return core, slot, lambda up, other: {"fsdp": slot(up, other) * 2 + core}, {"fsdp": rest * 2 + 1 - core}


def meet(devices):
    barrier = pltpu.get_barrier_semaphore()
    for device in devices:
        pl.semaphore_signal(barrier, inc=1, device_id=device, device_id_type=MESH)
    pl.semaphore_wait(barrier, len(devices))


def ring_peers(device):
    return [device(0, True), device(1, False), device(-1, False)]


def sender(send_sem, recv_sem, started):
    def send(source, target, device):
        index = len(started)
        copy = pltpu.make_async_remote_copy(
            src_ref=source,
            dst_ref=target,
            send_sem=send_sem.at[index],
            recv_sem=recv_sem.at[index],
            device_id=device,
            device_id_type=MESH,
        )
        copy.start()
        started.append(copy)
        return copy

    return send


def take_turns(*programs):
    waiting = list(programs)
    while waiting:
        for program in list(waiting):
            if next(program, None) is None:
                waiting.remove(program)


def follow(order, ring, shards):
    for which in order:
        for program in [ring] if which == "z" else shards:
            next(program, None)


def ring_gather(source, place, slot, device, send, arrived, split=True):
    rows = source.shape[0]
    halves = ((pl.ds(0, rows // 2),), (pl.ds(rows // 2, rows // 2),)) if split else ((), None)
    own = place(slot(0, False), ())
    to_side = send(source, own, device(0, True))
    up = send(source, own, device(1, False))
    down = send(source, own, device(-1, False))
    arrived(source, own)
    yield True
    far, two = [], []

    def pass_on(copy, up, other, index):
        copy.wait_recv()
        if halves[index] is not None:
            part = place(slot(-up, other), halves[index])
            far.append(send(part, part, device(up, False)))
        block = place(slot(-up, other), ())
        arrived(block, block)

    def far_here(index, other):
        if halves[index % 2] is not None:
            far.pop(0).wait_recv()
            part = place(slot(2, other), halves[index % 2])
            arrived(part, part)

    pass_on(up, 1, False, 0)
    yield True
    pass_on(down, -1, False, 1)
    yield True
    to_side.wait_recv()
    block = place(slot(0, True), ())
    two.append(send(block, block, device(1, False)))
    two.append(send(block, block, device(-1, False)))
    arrived(block, block)
    yield True
    for index in range(2):
        far_here(index, False)
        yield True
    pass_on(two[0], 1, True, 0)
    yield True
    pass_on(two[1], -1, True, 1)
    yield True
    for index in range(2):
        far_here(index, True)
        yield True


def nothing(source, target):
    return None


def side_start(side_ref, side_out, per_peer, send_sem, recv_sem, local_sem):
    me = lax.axis_index("seq")
    copies = []
    for step in range(1, GROUPS):
        other = lax.rem(me + step, GROUPS)
        copy = pltpu.make_async_remote_copy(
            src_ref=side_ref.at[other] if per_peer else side_ref,
            dst_ref=side_out.at[me],
            send_sem=send_sem.at[step],
            recv_sem=recv_sem.at[step],
            device_id={"seq": other},
            device_id_type=MESH,
        )
        copy.start()
        copies.append(copy)
    keep = pltpu.make_async_copy(side_ref.at[me] if per_peer else side_ref, side_out.at[me], local_sem)
    keep.start()
    return copies, keep


def side_end(copies, keep):
    for copy in copies:
        copy.wait_recv()
    for copy in copies:
        copy.wait_send()
    keep.wait()


def all_peers():
    me = lax.axis_index("seq")
    return [{"seq": lax.rem(me + step, GROUPS)} for step in range(1, GROUPS)]


def gather_kernel(x_ref, side_ref, out_ref, side_out, send_sem, recv_sem, local_sem, s_send, s_recv, s_local):
    me, slot, device = seq_axis()
    meet(all_peers())
    started = []
    send = sender(send_sem, recv_sem, started)
    program = ring_gather(x_ref, lambda at, cut: out_ref.at[(at, *cut)], slot, device, send, nothing)
    next(program)
    sides = side_start(side_ref, side_out, False, s_send, s_recv, s_local)
    keep = pltpu.make_async_copy(x_ref, out_ref.at[me], local_sem)
    keep.start()
    take_turns(program)
    side_end(*sides)
    for copy in started:
        copy.wait_send()
    keep.wait()


def any_spec():
    return pl.BlockSpec(memory_space=pl.ANY)


def vmem_spec():
    return pl.BlockSpec(memory_space=pltpu.VMEM)


def dma_sems(count):
    return pltpu.SemaphoreType.DMA((count,))


def seq_gather(piece, side, name, collective_id):
    rows, width = piece.shape
    gathered, sides = pl.pallas_call(
        gather_kernel,
        out_shape=(
            jax.ShapeDtypeStruct((GROUPS, rows, width), piece.dtype),
            jax.ShapeDtypeStruct((GROUPS, 8, 128), FULL),
        ),
        in_specs=[any_spec()] * 2,
        out_specs=(any_spec(), any_spec()),
        scratch_shapes=[
            dma_sems(9),
            dma_sems(9),
            pltpu.SemaphoreType.DMA,
            dma_sems(GROUPS),
            dma_sems(GROUPS),
            pltpu.SemaphoreType.DMA,
        ],
        compiler_params=pltpu.CompilerParams(collective_id=collective_id, has_side_effects=True),
        cost_estimate=BUSY,
        name=name,
    )(piece, side)
    return gathered.reshape(GROUPS * rows, width), sides


def shard_gather(source, target, send_sem, recv_sem, started, crossing, split=True):
    core, slot, device, twin = fsdp_axis()
    send = sender(send_sem, recv_sem, started)

    def place(at, cut):
        return target.at[(at * 2 + core, *cut)]

    def arrived(origin, block):
        crossing.append(send(origin, block, twin))

    return ring_gather(source, place, slot, device, send, arrived, split)


START_COUNT = 2


def start_kernel(x_ref, *rest):
    sources, x_out, targets = rest[:START_COUNT], rest[START_COUNT], rest[START_COUNT + 1 : 2 * START_COUNT + 1]
    x_send, x_recv, keeps, *sems = rest[2 * START_COUNT + 1 :]
    me, slot, device = seq_axis()
    core, f_slot, f_device, twin = fsdp_axis()
    meet(ring_peers(device) + ring_peers(f_device) + [twin])
    mine = f_slot(0, False) * 2 + core
    x_started, started, crossing, kept = [], [], [], []
    x_sender = sender(x_send, x_recv, x_started)
    program = ring_gather(x_ref, lambda at, cut: x_out.at[(at, *cut)], slot, device, x_sender, nothing)
    shards = []
    for index, (source, target) in enumerate(zip(sources, targets)):
        copies = []
        started.append(copies)
        shards.append(
            shard_gather(
                source, target, sems[2 * index], sems[2 * index + 1], copies, crossing, source.shape[0] % 32 == 0
            )
        )
        keep = pltpu.make_async_copy(source, target.at[mine], keeps.at[index])
        keep.start()
        kept.append(keep)
    keep = pltpu.make_async_copy(x_ref, x_out.at[me], keeps.at[START_COUNT])
    keep.start()
    kept.append(keep)
    follow("yzyyyzzyyzyyyyzzzzzz", program, shards)
    take_turns(program, *shards)
    for copy in crossing:
        copy.wait_recv()
    for copies in (x_started, *started):
        for copy in copies:
            copy.wait_send()
    for keep in kept:
        keep.wait()


def start_gather(piece, *shards):
    rows, width = piece.shape
    out = pl.pallas_call(
        start_kernel,
        out_shape=(jax.ShapeDtypeStruct((GROUPS, rows, width), LOW),)
        + tuple(jax.ShapeDtypeStruct((SHARDS, *shard.shape), LOW) for shard in shards),
        in_specs=[any_spec()] * (1 + START_COUNT),
        out_specs=(any_spec(),) * (1 + START_COUNT),
        scratch_shapes=[dma_sems(9)] * 2 + [dma_sems(START_COUNT + 1)] + [dma_sems(19)] * (2 * START_COUNT),
        compiler_params=pltpu.CompilerParams(collective_id=2, has_side_effects=True),
        cost_estimate=BUSY,
        name="rows_first",
    )(piece, *shards)
    return [out[0].reshape(GROUPS * rows, width)] + [
        full.reshape(SHARDS * shard.shape[0], -1) for full, shard in zip(out[1:], shards)
    ]


def ring_scatter(block, slot, device, send, result, buffers):
    in_low, in_high, sum_up, sum_down, land_low, land_high, part_out, part_in = buffers
    rows = part_out.shape[0]
    half = rows // 2
    first, second = pl.ds(0, half), pl.ds(half, half)
    everything = pl.ds(0, rows)
    landing = {}

    def begin(turn, other):
        far = block(2, other)
        copies = [
            send(far(first), in_low.at[turn], device(1, False)),
            send(far(second), in_high.at[turn], device(-1, False)),
        ]
        landing[turn] = [
            send(block(1, other)(second), land_low.at[turn, second], device(1, False)),
            send(block(-1, other)(first), land_high.at[turn, first], device(-1, False)),
        ]
        return copies

    def middle(turn, other, copies):
        copies[0].wait_recv()
        sum_up[turn] = (in_low[turn].astype(FULL) + block(1, other)(first)[...].astype(FULL)).astype(LOW)
        landing[turn].append(send(sum_up.at[turn], land_low.at[turn, first], device(1, False)))
        copies[1].wait_recv()
        sum_down[turn] = (in_high[turn].astype(FULL) + block(-1, other)(second)[...].astype(FULL)).astype(LOW)
        landing[turn].append(send(sum_down.at[turn], land_high.at[turn, second], device(-1, False)))

    def total(turn, other):
        for copy in landing[turn]:
            copy.wait_recv()
        return (
            block(0, other)(everything)[...].astype(FULL)
            + land_low[turn].astype(FULL)
            + land_high[turn].astype(FULL)
        )

    copies = begin(0, True)
    yield True
    middle(0, True, copies)
    yield True
    copies = begin(1, False)
    yield True
    part_out[...] = total(0, True).astype(LOW)
    to_side = send(part_out, part_in, device(0, True))
    yield True
    middle(1, False, copies)
    yield True
    result[...] = total(1, False)
    yield True
    to_side.wait_recv()
    result[...] += part_in[...].astype(FULL)


def scatter_buffers(rows, width):
    half = rows // 2
    return (
        [pltpu.VMEM((2, half, width), LOW)] * 4
        + [pltpu.VMEM((2, rows, width), LOW)] * 2
        + [pltpu.VMEM((rows, width), LOW)] * 2
    )


def block_of(x_ref, slot):
    def block(up, other):
        return lambda cut: x_ref.at[slot(up, other), cut]

    return block


def mixed_kernel(x_ref, side_ref, u_ref, d_ref, out_ref, side_out, u_out, d_out, *rest):
    buffers, (send_sem, recv_sem, s_send, s_recv, s_local) = rest[:8], rest[8:13]
    u_send, u_recv, d_send, d_recv, keeps = rest[13:]
    me, slot, device = seq_axis()
    core, f_slot, f_device, twin = fsdp_axis()
    meet(all_peers() + ring_peers(f_device) + [twin])
    started, u_started, d_started, crossing = [], [], [], []
    send = sender(send_sem, recv_sem, started)
    program = ring_scatter(block_of(x_ref, slot), slot, device, send, out_ref, buffers)
    next(program)
    sides = side_start(side_ref, side_out, True, s_send, s_recv, s_local)
    mine = f_slot(0, False) * 2 + core
    kept = []
    for index, (source, block) in enumerate(((u_ref, u_out.at[mine]), (d_ref, d_out.at[mine]))):
        keep = pltpu.make_async_copy(source, block, keeps.at[index])
        keep.start()
        kept.append(keep)
    shards = [
        shard_gather(u_ref, u_out, u_send, u_recv, u_started, crossing),
        shard_gather(d_ref, d_out, d_send, d_recv, d_started, crossing),
    ]
    follow("yzyyzyyyzyyzyyzz", program, shards)
    take_turns(program, *shards)
    side_end(*sides)
    for copy in crossing:
        copy.wait_recv()
    for copy in started + u_started + d_started:
        copy.wait_send()
    for keep in kept:
        keep.wait()


def mixed_scatter(parts, side, up_piece, down_piece):
    groups, rows, width = parts.shape
    summed, sides, up_all, down_all = pl.pallas_call(
        mixed_kernel,
        out_shape=(
            jax.ShapeDtypeStruct((rows, width), FULL),
            jax.ShapeDtypeStruct((GROUPS, 8, 128), FULL),
            jax.ShapeDtypeStruct((SHARDS, *up_piece.shape), LOW),
            jax.ShapeDtypeStruct((SHARDS, *down_piece.shape), LOW),
        ),
        in_specs=[vmem_spec(), vmem_spec(), any_spec(), any_spec()],
        out_specs=(vmem_spec(), vmem_spec(), any_spec(), any_spec()),
        scratch_shapes=scatter_buffers(rows, width)
        + [dma_sems(13), dma_sems(13), dma_sems(GROUPS), dma_sems(GROUPS), pltpu.SemaphoreType.DMA]
        + [dma_sems(19)] * 4
        + [dma_sems(2)],
        compiler_params=pltpu.CompilerParams(
            collective_id=4, has_side_effects=True, vmem_limit_bytes=40 << 20
        ),
        cost_estimate=BUSY,
        name="mixer_out",
    )(parts, side, up_piece, down_piece)
    return summed, sides, up_all.reshape(-1, up_piece.shape[1]), down_all.reshape(-1, down_piece.shape[1])


def shard_scratch(grads):
    depth, columns = grads.shape[1:]
    return (
        scatter_buffers(depth, columns)
        + [pltpu.VMEM((GROUPS, depth, columns), LOW)]
        + [dma_sems(13), dma_sems(13), dma_sems(8), dma_sems(8)]
    )


SHARD_SCRATCH = 13


def shard_scatters(arrays, started):
    core, slot, device, twin = fsdp_axis()
    order = [(2, True), (1, True), (-1, True), (2, False), (1, False), (-1, False), (0, True), (0, False)]
    programs, senders = [], []
    for pick, target, scratch in arrays:
        buffers, (core_in, send_sem, recv_sem, c_send, c_recv) = scratch[:8], scratch[8:]
        crossing, copies, arriving = [], [], {}
        started.extend([crossing, copies])
        senders.append((pick, core_in, sender(c_send, c_recv, crossing), arriving))

        def block(up, other, pick=pick, core_in=core_in, arriving=arriving):
            at = slot(up, other)
            if (up, other) in arriving:
                arriving.pop((up, other)).wait_recv()
                core_in[at] = (core_in[at].astype(FULL) + pick(at * 2 + core)[...].astype(FULL)).astype(LOW)
            return lambda cut: core_in.at[at, cut]

        programs.append(ring_scatter(block, slot, device, sender(send_sem, recv_sem, copies), target, buffers))
    for key in order:
        for pick, core_in, send_core, arriving in senders:
            at = slot(*key)
            arriving[key] = send_core(pick(at * 2 + 1 - core), core_in.at[at], twin)
    return programs


def blocks_of(ref):
    return lambda at: ref.at[at]


def shard_peers():
    core, slot, device, twin = fsdp_axis()
    return ring_peers(device) + [twin]


def last_kernel(g_ref, p_ref, w_ref, a_ref, x_out, w_out, a_out, x_ref, *rest):
    x_buffers, (x_send, x_recv) = rest[:8], rest[8:10]
    me, slot, device = seq_axis()
    done = set()

    def part_of(up, other):
        at = slot(up, other)
        if (up, other) not in done:
            done.add((up, other))
            here = pl.ds(pl.multiple_of(at * PIECE, PIECE), PIECE)
            for part in range(D // 512):
                cols = slice(part * 512, (part + 1) * 512)
                x_ref[at, :, cols] = dot_rhs_t(g_ref[here, :], p_ref[cols, :]).astype(LOW)
        return lambda cut: x_ref.at[at, cut]

    meet(ring_peers(device) + shard_peers())
    x_started, started = [], []
    program = ring_scatter(part_of, slot, device, sender(x_send, x_recv, x_started), x_out, x_buffers)
    main, small = shard_scatters(
        [
            (blocks_of(w_ref), w_out, rest[10 : 10 + SHARD_SCRATCH]),
            (blocks_of(a_ref), a_out, rest[10 + SHARD_SCRATCH :]),
        ],
        started,
    )
    follow("zyzyzyyzyzyzyz", program, [main, small])
    take_turns(program, main, small)
    for copies in (x_started, *started):
        for copy in copies:
            copy.wait_send()


def last_scatter(proj_grad, weights, grads, small):
    rows, width = PIECE, D
    return pl.pallas_call(
        last_kernel,
        out_shape=(
            jax.ShapeDtypeStruct((rows, width), FULL),
            jax.ShapeDtypeStruct(grads.shape[1:], FULL),
            jax.ShapeDtypeStruct(small.shape[1:], FULL),
        ),
        in_specs=[vmem_spec()] * 4,
        out_specs=(vmem_spec(),) * 3,
        scratch_shapes=[pltpu.VMEM((GROUPS, rows, width), LOW)]
        + scatter_buffers(rows, width)
        + [dma_sems(13), dma_sems(13)]
        + shard_scratch(grads)
        + shard_scratch(small),
        compiler_params=pltpu.CompilerParams(
            collective_id=8, has_side_effects=True, vmem_limit_bytes=40 << 20
        ),
        cost_estimate=BUSY,
        name="rows_last",
    )(proj_grad, weights, grads, small)


def middle_kernel(x_ref, side_ref, u_ref, x_out, side_out, u_out, *rest):
    x_send, x_recv, x_local, s_send, s_recv, s_local = rest[:6]
    me, slot, device = seq_axis()
    meet(all_peers() + shard_peers())
    x_started, started = [], []
    send = sender(x_send, x_recv, x_started)
    program = ring_gather(x_ref, lambda at, cut: x_out.at[(at, *cut)], slot, device, send, nothing)
    next(program)
    [shard] = shard_scatters([(blocks_of(u_ref), u_out, rest[6:])], started)
    sides = side_start(side_ref, side_out, False, s_send, s_recv, s_local)
    keep = pltpu.make_async_copy(x_ref, x_out.at[me], x_local)
    keep.start()
    follow("yyyzzyzyzzyyzzzz", program, [shard])
    take_turns(program, shard)
    side_end(*sides)
    for copies in (x_started, *started):
        for copy in copies:
            copy.wait_send()
    keep.wait()


def middle_gather(piece, side, up_grads):
    rows, width = piece.shape
    gathered, sides, up_sum = pl.pallas_call(
        middle_kernel,
        out_shape=(
            jax.ShapeDtypeStruct((GROUPS, rows, width), piece.dtype),
            jax.ShapeDtypeStruct((GROUPS, 8, 128), FULL),
            jax.ShapeDtypeStruct(up_grads.shape[1:], FULL),
        ),
        in_specs=[any_spec(), any_spec(), vmem_spec()],
        out_specs=(any_spec(), any_spec(), vmem_spec()),
        scratch_shapes=[
            dma_sems(9),
            dma_sems(9),
            pltpu.SemaphoreType.DMA,
            dma_sems(GROUPS),
            dma_sems(GROUPS),
            pltpu.SemaphoreType.DMA,
        ]
        + shard_scratch(up_grads),
        compiler_params=pltpu.CompilerParams(
            collective_id=7, has_side_effects=True, vmem_limit_bytes=48 << 20
        ),
        cost_estimate=BUSY,
        name="rows_mixer",
    )(piece, side, up_grads)
    return gathered.reshape(GROUPS * rows, width), sides, up_sum


UNITS = FF_EXP + SH_HERE
HIDDEN_COLS = 2 * UNITS


def experts_kernel(
    x_ref,
    side_ref,
    cot_any,
    up_any,
    shared_any,
    down_any,
    shared_down_any,
    back_out,
    side_back,
    block_any,
    up_grad_any,
    down_grad_any,
    shared_grad_any,
    cot_ref,
    up_ref,
    shared_ref,
    down_ref,
    shared_down_ref,
    block_ref,
    up_grad_ref,
    down_grad_ref,
    shared_grad_ref,
    rows_ref,
    sides_in,
    parts_ref,
    gu_ref,
    act_ref,
    side_send,
    *rest,
):
    buffers, rest = rest[:8], rest[8:]
    g_send, g_recv, g_local, s_send, s_recv, s_local, r_send, r_recv, b_send, b_recv, b_local, moves = rest
    me, slot, device = seq_axis()
    moving = []

    def move(source, target):
        copy = pltpu.make_async_copy(source, target, moves.at[len(moving)])
        copy.start()
        moving.append(copy)

    for source, target in (
        (up_any, up_ref),
        (down_any, down_ref),
        (cot_any, cot_ref),
        (shared_any, shared_ref),
        (shared_down_any, shared_down_ref),
    ):
        move(source, target)
    meet(all_peers())
    started = []
    gather = ring_gather(
        x_ref, lambda at, cut: rows_ref.at[(at, *cut)], slot, device, sender(g_send, g_recv, started), nothing
    )
    next(gather)
    sides = side_start(side_ref, sides_in, False, s_send, s_recv, s_local)
    keep = pltpu.make_async_copy(x_ref, rows_ref.at[me], g_local)
    keep.start()
    keep.wait()
    for copy in moving:
        copy.wait()
    side_end(*sides)

    def unit_step(hidden, cot, weights, downs, width, gu_at, half, scale):
        gate = dot(hidden, weights[:, gu_at : gu_at + width])
        lift = dot(hidden, weights[:, gu_at + half : gu_at + half + width])
        back = dot_rhs_t(cot, downs)
        gate_sig = sigmoid(gate)
        gate_silu = gate * gate_sig
        act = (gate_silu * lift).astype(LOW).astype(FULL)
        product = back * act
        if scale is not None:
            scale = jnp.concatenate([scale] * (width // 128), axis=1)
            act = act * scale
            back = back * scale
        gate_grad = back * lift * (gate_sig * (1.0 + gate * (1.0 - gate_sig)))
        return product, act.astype(LOW), gate_grad.astype(LOW), (back * gate_silu).astype(LOW)

    def joined(blocks):
        return blocks[0] if len(blocks) == 1 else jnp.concatenate(blocks, axis=0)

    def process(*keys):
        slots = [slot(*key) for key in keys]
        rows = [pl.ds(pl.multiple_of(at * PIECE, PIECE), PIECE) for at in slots]

        def put(ref, cols, values):
            for index, here in enumerate(rows):
                ref[here, cols] = values[index * PIECE : (index + 1) * PIECE]

        hidden = joined([rows_ref[at] for at in slots])
        cot = joined([cot_ref[at] for at in slots])
        scale = joined([jnp.broadcast_to(sides_in[at, pl.ds(me, 1), :], (128, 128)).T for at in slots])
        folded = None
        for begin in range(0, FF_EXP, 256):
            cols = slice(begin, begin + 256)
            product, act, gate_grad, lift_grad = unit_step(
                hidden, cot, up_ref, down_ref[cols, :], 256, begin, FF_EXP, scale
            )
            put(act_ref, cols, act)
            put(gu_ref, cols, gate_grad)
            put(gu_ref, slice(FF_EXP + begin, FF_EXP + begin + 256), lift_grad)
            product = product[:, :128] + product[:, 128:]
            folded = product if folded is None else folded + product
        unused, act, gate_grad, lift_grad = unit_step(
            hidden, cot, shared_ref, shared_down_ref[...], SH_HERE, 0, SH_HERE, None
        )
        put(act_ref, slice(FF_EXP, UNITS), act)
        put(gu_ref, slice(2 * FF_EXP, 2 * FF_EXP + SH_HERE), gate_grad)
        put(gu_ref, slice(2 * FF_EXP + SH_HERE, HIDDEN_COLS), lift_grad)
        sums = lax.dot_general(
            jnp.ones((8, 128), FULL),
            folded,
            (((1,), (1,)), ((), ())),
            precision=HIGHEST,
            preferred_element_type=FULL,
        )
        for index, at in enumerate(slots):
            side_send[at] = sums[:, index * PIECE : (index + 1) * PIECE]
        grads = joined([gu_ref[here, :] for here in rows])
        for begin in range(0, D, 512):
            cols = slice(begin, begin + 512)
            total = dot_rhs_t(grads[:, : 2 * FF_EXP], up_ref[cols, :])
            total = (total + dot_rhs_t(grads[:, 2 * FF_EXP :], shared_ref[cols, :])).astype(LOW)
            for index, at in enumerate(slots):
                parts_ref[at, :, cols] = total[index * PIECE : (index + 1) * PIECE]

    process((0, False))
    next(gather)
    next(gather)
    process((-1, False), (1, False))
    next(gather)
    next(gather)
    next(gather)
    process((0, True), (2, False))
    next(gather)
    next(gather)
    process((-1, True), (1, True))
    take_turns(gather)
    process((2, True))

    summed = []
    scatter = ring_scatter(
        block_of(parts_ref, slot), slot, device, sender(r_send, r_recv, summed), back_out, buffers
    )
    next(scatter)
    backs = side_start(side_send, side_back, True, b_send, b_recv, b_local)

    def block_step(at, carry):
        rows = pl.ds(pl.multiple_of(at * PIECE, PIECE), PIECE)
        for begin in range(0, D, 512):
            cols = slice(begin, begin + 512)
            total = dot(act_ref[rows, :FF_EXP], down_ref[:, cols])
            total = total + dot(act_ref[rows, FF_EXP:], shared_down_ref[:, cols])
            block_ref[at, :, cols] = total.astype(LOW)
        return carry

    def up_step(part, carry):
        rows = pl.ds(pl.multiple_of(part * 256, 256), 256)
        left = rows_ref[:, :, rows].reshape(SEQ_LEN, 256).T
        for begin in range(0, HIDDEN_COLS, 640):
            cols = slice(begin, begin + 640)
            up_grad_ref[rows, cols] = dot(left, gu_ref[:, cols]).astype(LOW)
        return carry

    lax.fori_loop(0, 4, block_step, 0)
    next(scatter)
    next(scatter)
    lax.fori_loop(4, 8, block_step, 0)
    moving.clear()
    move(block_ref, block_any)
    next(scatter)
    lax.fori_loop(0, 3, up_step, 0)
    next(scatter)
    lax.fori_loop(3, 6, up_step, 0)
    move(up_grad_ref, up_grad_any)
    next(scatter)
    for row in range(0, UNITS, 128):
        left = act_ref[:, row : row + 128].T
        for begin in range(0, D, 512):
            cols = slice(begin, begin + 512)
            grads = dot(left, cot_ref[:, :, cols].reshape(SEQ_LEN, 512)).astype(LOW)
            if row < FF_EXP:
                down_grad_ref[row : row + 128, cols] = grads
            else:
                shared_grad_ref[:, cols] = grads
    move(down_grad_ref, down_grad_any)
    move(shared_grad_ref, shared_grad_any)
    take_turns(scatter)
    for copy in moving:
        copy.wait()
    side_end(*backs)
    for copy in started + summed:
        copy.wait_send()


def experts(piece, side, rows_cot, up, shared, down, shared_down):
    return pl.pallas_call(
        experts_kernel,
        out_shape=(
            jax.ShapeDtypeStruct((PIECE, D), FULL),
            jax.ShapeDtypeStruct((GROUPS, 8, 128), FULL),
            jax.ShapeDtypeStruct((GROUPS, PIECE, D), LOW),
            jax.ShapeDtypeStruct((D, HIDDEN_COLS), LOW),
            jax.ShapeDtypeStruct((FF_EXP, D), LOW),
            jax.ShapeDtypeStruct((SH_HERE, D), LOW),
        ),
        in_specs=[vmem_spec()] * 2 + [any_spec()] * 5,
        out_specs=(vmem_spec(),) * 2 + (any_spec(),) * 4,
        scratch_shapes=[
            pltpu.VMEM((GROUPS, PIECE, D), LOW),
            pltpu.VMEM((D, 2 * FF_EXP), LOW),
            pltpu.VMEM((D, 2 * SH_HERE), LOW),
            pltpu.VMEM((FF_EXP, D), LOW),
            pltpu.VMEM((SH_HERE, D), LOW),
            pltpu.VMEM((GROUPS, PIECE, D), LOW),
            pltpu.VMEM((D, HIDDEN_COLS), LOW),
            pltpu.VMEM((FF_EXP, D), LOW),
            pltpu.VMEM((SH_HERE, D), LOW),
            pltpu.VMEM((GROUPS, PIECE, D), LOW),
            pltpu.VMEM((GROUPS, 8, 128), FULL),
            pltpu.VMEM((GROUPS, PIECE, D), LOW),
            pltpu.VMEM((SEQ_LEN, HIDDEN_COLS), LOW),
            pltpu.VMEM((SEQ_LEN, UNITS), LOW),
            pltpu.VMEM((GROUPS, 8, 128), FULL),
        ]
        + scatter_buffers(PIECE, D)
        + [dma_sems(9), dma_sems(9), pltpu.SemaphoreType.DMA]
        + [dma_sems(GROUPS), dma_sems(GROUPS), pltpu.SemaphoreType.DMA]
        + [dma_sems(13), dma_sems(13)]
        + [dma_sems(GROUPS), dma_sems(GROUPS), pltpu.SemaphoreType.DMA]
        + [dma_sems(5)],
        compiler_params=pltpu.CompilerParams(
            collective_id=5, has_side_effects=True, vmem_limit_bytes=56 << 20
        ),
        cost_estimate=BUSY,
        name="experts",
    )(piece, side, rows_cot, up, shared, down, shared_down)


def swap_start(x_ref, out_ref, send_sem, recv_sem, local_sem):
    return side_start(x_ref, out_ref, True, send_sem, recv_sem, local_sem)


def columns_kernel(x_ref, x_out, x_send, x_recv, x_local):
    meet(all_peers())
    side_end(*swap_start(x_ref, x_out, x_send, x_recv, x_local))


def columns_out(blocks):
    return pl.pallas_call(
        columns_kernel,
        out_shape=jax.ShapeDtypeStruct(blocks.shape, blocks.dtype),
        in_specs=[any_spec()],
        out_specs=any_spec(),
        scratch_shapes=[dma_sems(GROUPS), dma_sems(GROUPS), pltpu.SemaphoreType.DMA],
        compiler_params=pltpu.CompilerParams(collective_id=1, has_side_effects=True),
        cost_estimate=BUSY,
        name="columns_out",
    )(blocks)


def back_kernel(x_ref, u_ref, side_ref, x_out, u_out, side_out, *sems):
    meet(all_peers())
    swaps = [
        swap_start(x_ref, x_out, *sems[:3]),
        swap_start(u_ref, u_out, *sems[3:6]),
        swap_start(side_ref, side_out, *sems[6:]),
    ]
    for swap in swaps:
        side_end(*swap)


def columns_back(blocks, shared, side):
    return pl.pallas_call(
        back_kernel,
        out_shape=(
            jax.ShapeDtypeStruct(blocks.shape, blocks.dtype),
            jax.ShapeDtypeStruct(shared.shape, shared.dtype),
            jax.ShapeDtypeStruct(side.shape, side.dtype),
        ),
        in_specs=[any_spec()] * 3,
        out_specs=(any_spec(),) * 3,
        scratch_shapes=[dma_sems(GROUPS), dma_sems(GROUPS), pltpu.SemaphoreType.DMA] * 3,
        compiler_params=pltpu.CompilerParams(collective_id=10, has_side_effects=True),
        cost_estimate=BUSY,
        name="columns_back",
    )(blocks, shared, side)


TILE = 256
TILES = SEQ_LEN // TILE
PAIRS = HEADS_HERE // 2


def scan_lanes(values, backward):
    length = values.shape[1]
    lane = lax.broadcasted_iota(jnp.int32, values.shape, 1)
    step = 1
    while step < length:
        if backward:
            values = values + jnp.where(lane < length - step, pltpu.roll(values, length - step, 1), 0.0)
        else:
            values = values + jnp.where(lane >= step, pltpu.roll(values, step, 1), 0.0)
        step *= 2
    return values


def sigmoid(values):
    return 1.0 / (1.0 + jnp.exp(-values))


def conv_taps(padded, taps, at):
    total = taps[0:1, at] * padded[5 : 5 + SEQ_LEN]
    for tap in range(1, CONV):
        total = total + taps[tap : tap + 1, at] * padded[5 + tap : 5 + tap + SEQ_LEN]
    return total


def scores_and_columns(b_state, c_state, cum_rows, scores, columns):
    for low in range(TILES):
        for far in range(low + 1):
            scores[low * TILE : (low + 1) * TILE, far * TILE : (far + 1) * TILE] = dot_rhs_t(
                c_state[low * TILE : (low + 1) * TILE], b_state[far * TILE : (far + 1) * TILE]
            )
    turned = jnp.concatenate([cum_rows, jnp.zeros((120, SEQ_LEN), FULL)], axis=0).T
    for head in range(HEADS_HERE):
        columns[head] = jnp.broadcast_to(turned[:, head : head + 1], (SEQ_LEN, 128))


def decay_tile(columns, cum_ref, head, low, far):
    column = columns[head, low * TILE : (low + 1) * TILE]
    row = cum_ref[pl.ds(head, 1), far * TILE : (far + 1) * TILE]
    return jnp.exp(jnp.minimum(jnp.concatenate([column] * (TILE // 128), axis=1) - row, 0.0))


def lower_tile():
    shape = (TILE, TILE)
    return lax.broadcasted_iota(jnp.int32, shape, 0) >= lax.broadcasted_iota(jnp.int32, shape, 1)


def mixer_forward_kernel(
    unit_any,
    first_ref,
    weight_any,
    out_weight_ref,
    taps_ref,
    bias_ref,
    head_ref,
    gain_ref,
    skip_ref,
    cot_ref,
    shared_ref,
    shared_down_ref,
    proj_any,
    act_any,
    mixed_any,
    gated_any,
    part_any,
    side_ref,
    cum_ref,
    step_ref,
    cot_out,
    shared_out,
    shared_down_out,
    unit_ref,
    weight_ref,
    proj_ref,
    act_ref,
    mixed_ref,
    gated_ref,
    part_ref,
    padded,
    scores,
    columns,
    scaled_ref,
    c_send,
    c_recv,
    c_local,
    moves,
    u_send,
    u_recv,
    d_send,
    d_recv,
    keeps,
):
    moving = []

    def move(source, target):
        copy = pltpu.make_async_copy(source, target, moves.at[len(moving)])
        copy.start()
        moving.append(copy)

    move(weight_any, weight_ref)
    move(unit_any, unit_ref)
    me, slot, device = seq_axis()
    core, f_slot, f_device, twin = fsdp_axis()
    meet(ring_peers(device) + ring_peers(f_device) + [twin])
    mine = f_slot(0, False) * 2 + core
    started, u_started, d_started, crossing, kept = [], [], [], [], []
    program = ring_gather(
        cot_ref, lambda at, cut: cot_out.at[(at, *cut)], slot, device, sender(c_send, c_recv, started), nothing
    )
    next(program)
    keep = pltpu.make_async_copy(cot_ref, cot_out.at[me], c_local)
    keep.start()
    shards = [
        shard_gather(shared_ref, shared_out, u_send, u_recv, u_started, crossing),
        shard_gather(shared_down_ref, shared_down_out, d_send, d_recv, d_started, crossing, False),
    ]
    for index, (source, block) in enumerate(
        ((shared_ref, shared_out.at[mine]), (shared_down_ref, shared_down_out.at[mine]))
    ):
        kept.append(pltpu.make_async_copy(source, block, keeps.at[index]))
        kept[-1].start()
    follow("y", program, shards)
    for copy in moving:
        copy.wait()
    moving.clear()

    def rows_step(tile, carry):
        here = pl.ds(pl.multiple_of(tile * TILE, TILE), TILE)
        normed = (unit_ref[here, :].astype(FULL) * first_ref[...]).astype(LOW)
        for part in range(PROJ_HERE // 384):
            at = slice(part * 384, (part + 1) * 384)
            proj_ref[here, at] = dot(normed, weight_ref[:, at]).astype(LOW)
        return carry

    lax.fori_loop(0, TILES, rows_step, 0)
    move(proj_ref, proj_any)
    follow("yyyzz", program, shards)
    padded[0:8] = jnp.zeros((8, 128), FULL)
    for part in range(CONV_HERE // 128):
        at = slice(part * 128, (part + 1) * 128)
        padded[8:] = proj_ref[:, INNER_HERE + part * 128 : INNER_HERE + (part + 1) * 128].astype(FULL)
        before = bias_ref[0:1, at] + conv_taps(padded, taps_ref, at)
        act_ref[:, at] = (before * sigmoid(before)).astype(LOW)
    rates = proj_ref[:, INNER_HERE + CONV_HERE :].astype(FULL).T[:8] + head_ref[0][:, :1]
    step_ref[...] = jnp.maximum(rates, 0.0) + jnp.log1p(jnp.exp(-jnp.abs(rates)))
    cum_ref[...] = scan_lanes(step_ref[...] * head_ref[1][:, :1], False)
    scores_and_columns(
        act_ref[:, INNER_HERE : INNER_HERE + STATE],
        act_ref[:, INNER_HERE + STATE :],
        cum_ref[...],
        scores,
        columns,
    )
    move(act_ref, act_any)
    follow("yyz", program, shards)

    def pair_step(pair, carry):
        at = pl.ds(pl.multiple_of(pair * 128, 128), 128)
        for low in range(TILES):
            here = slice(low * TILE, (low + 1) * TILE)
            sums = [None, None]
            for far in range(low + 1):
                there = slice(far * TILE, (far + 1) * TILE)
                for half in range(2):
                    head = pair * 2 + half
                    weight = scores[here, there] * decay_tile(columns, cum_ref, head, low, far)
                    weight = weight * step_ref[pl.ds(head, 1), there]
                    if far == low:
                        weight = jnp.where(lower_tile(), weight, 0.0)
                    term = dot(weight.astype(LOW), act_ref[there, at])
                    sums[half] = term if far == 0 else sums[half] + term
            first = lax.broadcasted_iota(jnp.int32, (TILE, 128), 1) < HDIM
            x_tile = act_ref[here, at].astype(FULL)
            mixed = jnp.where(first, sums[0], sums[1]) + skip_ref[0:1, at] * x_tile
            gate = proj_ref[here, at].astype(FULL)
            gated = (mixed * (gate * sigmoid(gate))).astype(LOW)
            mixed_ref[here, at] = mixed
            gated_ref[here, at] = gated
            scaled_ref[here, at] = (gated.astype(FULL) * gain_ref[0:1, at]).astype(LOW)
        return carry

    lax.fori_loop(0, PAIRS, pair_step, 0)
    move(mixed_ref, mixed_any)
    move(gated_ref, gated_any)
    follow("yyyyzzzz", program, shards)

    def out_step(tile, carry):
        here = pl.ds(pl.multiple_of(tile * TILE, TILE), TILE)
        for part in range(D // 512):
            at = slice(part * 512, (part + 1) * 512)
            part_ref[here, at] = dot(scaled_ref[here, :], out_weight_ref[:, at]).astype(LOW)
        return carry

    lax.fori_loop(0, TILES, out_step, 0)
    move(part_ref, part_any)
    wide = gated_ref[...].astype(FULL)
    squares = lax.dot_general(
        jnp.ones((8, INNER_HERE), FULL),
        wide * wide,
        (((1,), (1,)), ((), ())),
        precision=HIGHEST,
        preferred_element_type=FULL,
    )
    for piece in range(GROUPS):
        side_ref[piece] = squares[:, piece * PIECE : (piece + 1) * PIECE]
    take_turns(program, *shards)
    for copy in moving + kept:
        copy.wait()
    for copy in crossing:
        copy.wait_recv()
    for copy in started + u_started + d_started:
        copy.wait_send()
    keep.wait()


def mixer_forward(unit_rows, gain_first, weights, out_weights, taps, bias, head_cols, gain, skip, piece, shared, shared_down):
    return pl.pallas_call(
        mixer_forward_kernel,
        out_shape=(
            jax.ShapeDtypeStruct((SEQ_LEN, PROJ_HERE), LOW),
            jax.ShapeDtypeStruct((SEQ_LEN, CONV_HERE), LOW),
            jax.ShapeDtypeStruct((SEQ_LEN, INNER_HERE), FULL),
            jax.ShapeDtypeStruct((SEQ_LEN, INNER_HERE), LOW),
            jax.ShapeDtypeStruct((SEQ_LEN, D), LOW),
            jax.ShapeDtypeStruct((GROUPS, 8, PIECE), FULL),
            jax.ShapeDtypeStruct((8, SEQ_LEN), FULL),
            jax.ShapeDtypeStruct((8, SEQ_LEN), FULL),
            jax.ShapeDtypeStruct((GROUPS, PIECE, D), LOW),
            jax.ShapeDtypeStruct((SHARDS, *shared.shape), LOW),
            jax.ShapeDtypeStruct((SHARDS, *shared_down.shape), LOW),
        ),
        in_specs=[any_spec(), vmem_spec(), any_spec()] + [vmem_spec()] * 6 + [any_spec()] * 3,
        out_specs=(any_spec(),) * 5 + (vmem_spec(),) * 3 + (any_spec(),) * 3,
        scratch_shapes=[
            pltpu.VMEM((SEQ_LEN, D), LOW),
            pltpu.VMEM((D, PROJ_HERE), LOW),
            pltpu.VMEM((SEQ_LEN, PROJ_HERE), LOW),
            pltpu.VMEM((SEQ_LEN, CONV_HERE), LOW),
            pltpu.VMEM((SEQ_LEN, INNER_HERE), FULL),
            pltpu.VMEM((SEQ_LEN, INNER_HERE), LOW),
            pltpu.VMEM((SEQ_LEN, D), LOW),
            pltpu.VMEM((SEQ_LEN + 8, 128), FULL),
            pltpu.VMEM((SEQ_LEN, SEQ_LEN), FULL),
            pltpu.VMEM((HEADS_HERE, SEQ_LEN, 128), FULL),
            pltpu.VMEM((SEQ_LEN, INNER_HERE), LOW),
            dma_sems(9),
            dma_sems(9),
            pltpu.SemaphoreType.DMA,
            dma_sems(6),
        ]
        + [dma_sems(19)] * 4
        + [dma_sems(2)],
        compiler_params=pltpu.CompilerParams(
            collective_id=3, has_side_effects=True, vmem_limit_bytes=52 << 20
        ),
        cost_estimate=BUSY,
        name="mixer_forward",
    )(unit_rows, gain_first, weights, out_weights, taps, bias, head_cols, gain, skip, piece, shared, shared_down)


def mixer_backward_kernel(
    grad_ref,
    proj_ref,
    act_ref,
    mixed_ref,
    cum_ref,
    step_ref,
    taps_ref,
    bias_ref,
    head_ref,
    skip_ref,
    block_ref,
    down_ref,
    owned_ref,
    out_ref,
    conv_ref,
    skip_grad_ref,
    head_grad_ref,
    block_out,
    down_out,
    owned_out,
    padded,
    trailing,
    scores,
    score_grad,
    columns,
    mixed_low,
    act_grad,
    size_rows,
    flow_rows,
    row_sums,
    mixed_back,
    *rest,
):
    me, slot, device = seq_axis()
    meet(ring_peers(device) + shard_peers())
    started = [[]]
    shards = shard_scatters(
        [
            (blocks_of(down_ref), down_out, rest[10 : 10 + SHARD_SCRATCH]),
            (blocks_of(owned_ref), owned_out, rest[10 + SHARD_SCRATCH :]),
        ],
        started,
    )
    send = sender(rest[8], rest[9], started[0])
    program = ring_scatter(block_of(block_ref, slot), slot, device, send, block_out, rest[:8])
    next(program)
    scores_and_columns(
        act_ref[:, INNER_HERE : INNER_HERE + STATE],
        act_ref[:, INNER_HERE + STATE :],
        cum_ref[...],
        scores,
        columns,
    )
    size_rows[...] = jnp.zeros((8, SEQ_LEN), FULL)
    flow_rows[...] = jnp.zeros((8, SEQ_LEN), FULL)
    for part in range(PAIRS):
        at = slice(part * 128, (part + 1) * 128)
        gate = proj_ref[:, at].astype(FULL)
        gate_sig = sigmoid(gate)
        grad = grad_ref[:, at].astype(FULL)
        mixed_grad = grad * (gate * gate_sig)
        out_ref[:, at] = (grad * mixed_ref[:, at] * (gate_sig * (1.0 + gate * (1.0 - gate_sig)))).astype(LOW)
        x_tile = act_ref[:, at].astype(FULL)
        skip_grad_ref[:, at] = jnp.broadcast_to(jnp.sum(mixed_grad * x_tile, axis=0, keepdims=True), (8, 128))
        mixed_low[:, at] = mixed_grad.astype(LOW)
        act_grad[:, at] = skip_ref[0:1, at] * mixed_grad
    follow("zzy", program, shards)

    def pair_step(pair):
        at = slice(pair * 128, (pair + 1) * 128)
        first = lax.broadcasted_iota(jnp.int32, (TILE, 128), 1) < HDIM
        for half in range(2):
            head = pair * 2 + half
            mine = first if half == 0 else jnp.logical_not(first)
            for low in range(TILES):
                here = slice(low * TILE, (low + 1) * TILE)
                grad = jnp.where(mine, mixed_low[here, at], jnp.zeros((TILE, 128), LOW))
                turned = mixed_low[here, at].T[half * HDIM : (half + 1) * HDIM]
                sums = jnp.zeros((TILE, 128), FULL)
                for far in range(low + 1):
                    there = slice(far * TILE, (far + 1) * TILE)
                    decay = decay_tile(columns, cum_ref, head, low, far)
                    if far == low:
                        decay = jnp.where(lower_tile(), decay, 0.0)
                    step = step_ref[pl.ds(head, 1), there]
                    scaled = dot_rhs_t(grad, act_ref[there, at]) * decay
                    product = scaled * scores[here, there]
                    size_rows[pl.ds(head, 1), there] += jnp.sum(product, axis=0, keepdims=True)
                    flow = product * step
                    for part in range(TILE // 128):
                        sums = sums + flow[:, part * 128 : (part + 1) * 128]
                    add = scaled * step
                    if half == 0 and pair == 0:
                        score_grad[here, there] = add
                    else:
                        score_grad[here, there] += add
                    weight = (scores[here, there] * decay * step).astype(LOW)
                    mixed_back[half * HDIM : (half + 1) * HDIM, there] += dot(turned, weight)
                row_sums[...] = sums
                flow_rows[pl.ds(head, 1), here] = lax.dot_general(
                    jnp.ones((8, 128), FULL),
                    row_sums[...],
                    (((1,), (1,)), ((), ())),
                    precision=HIGHEST,
                    preferred_element_type=FULL,
                )[:1]

    for pair in range(PAIRS):
        mixed_back[...] = jnp.zeros((128, SEQ_LEN), FULL)
        pair_step(pair)
        act_grad[:, pair * 128 : (pair + 1) * 128] += mixed_back[...].T
        follow(("yyz", "yz", "y")[pair], program, shards)

    b_at, c_at = INNER_HERE, INNER_HERE + STATE
    mixed_back[...] = jnp.zeros((128, SEQ_LEN), FULL)
    for low in range(TILES):
        here = slice(low * TILE, (low + 1) * TILE)
        for far in range(low + 1):
            there = slice(far * TILE, (far + 1) * TILE)
            high, rest = hi_lo(score_grad[here, there])
            b_tile, c_tile = act_ref[there, b_at:c_at], act_ref[here, c_at:]
            c_term = dot(high, b_tile) + dot(rest, b_tile)
            if far == 0:
                c_turned = c_tile.T
            mixed_back[:, there] += dot(c_turned, high) + dot(c_turned, rest)
            if far == 0:
                act_grad[here, c_at:] = c_term
            else:
                act_grad[here, c_at:] += c_term
    act_grad[:, b_at:c_at] = mixed_back[...].T

    step, size = step_ref[...], size_rows[...]
    decay_rate = head_ref[1][:, :1]
    back = scan_lanes(flow_rows[...] - step * size, True)
    rates = proj_ref[:, INNER_HERE + CONV_HERE :].astype(FULL).T[:8] + head_ref[0][:, :1]
    rate_grad = (size + back * decay_rate) * sigmoid(rates)
    real = lax.broadcasted_iota(jnp.int32, (8, SEQ_LEN), 0) < HEADS_HERE
    rate_grad = jnp.where(real, rate_grad, 0.0)
    head_grad_ref[0] = jnp.broadcast_to(jnp.sum(rate_grad, axis=1, keepdims=True), (8, 128))
    head_grad_ref[1] = jnp.broadcast_to(jnp.sum(back * step * decay_rate, axis=1, keepdims=True), (8, 128))
    turned = jnp.concatenate([rate_grad, jnp.zeros((120, SEQ_LEN), FULL)], axis=0).T
    out_ref[:, INNER_HERE + CONV_HERE :] = turned.astype(LOW)

    padded[0:8] = jnp.zeros((8, 128), FULL)
    trailing[SEQ_LEN:] = jnp.zeros((8, 128), FULL)
    for part in range(CONV_HERE // 128):
        at = slice(part * 128, (part + 1) * 128)
        wide = slice(INNER_HERE + part * 128, INNER_HERE + (part + 1) * 128)
        padded[8:] = proj_ref[:, wide].astype(FULL)
        before = bias_ref[0:1, at] + conv_taps(padded, taps_ref, at)
        gate = sigmoid(before)
        grad = act_grad[:, at] * (gate * (1.0 + before * (1.0 - gate)))
        trailing[:SEQ_LEN] = grad
        conv_ref[CONV : CONV + 1, at] = jnp.sum(grad, axis=0, keepdims=True)
        total = None
        for tap in range(CONV):
            conv_ref[tap : tap + 1, at] = jnp.sum(
                trailing[:SEQ_LEN] * padded[5 + tap : 5 + tap + SEQ_LEN], axis=0, keepdims=True
            )
            shift = CONV - 1 - tap
            term = taps_ref[tap : tap + 1, at] * trailing[shift : shift + SEQ_LEN]
            total = term if total is None else total + term
        out_ref[:, wide] = total.astype(LOW)
    conv_ref[CONV + 1 :] = jnp.zeros((3, CONV_HERE), FULL)
    take_turns(program, *shards)
    for copies in started:
        for copy in copies:
            copy.wait_send()


def mixer_backward(grad, projected, act, mixed, cum, step, taps, bias, head_cols, skip, blocks, downs, owned):
    return pl.pallas_call(
        mixer_backward_kernel,
        out_shape=(
            jax.ShapeDtypeStruct((SEQ_LEN, PROJ_HERE), LOW),
            jax.ShapeDtypeStruct((8, CONV_HERE), FULL),
            jax.ShapeDtypeStruct((8, INNER_HERE), FULL),
            jax.ShapeDtypeStruct((2, 8, 128), FULL),
            jax.ShapeDtypeStruct((PIECE, D), FULL),
            jax.ShapeDtypeStruct((32, D), FULL),
            jax.ShapeDtypeStruct((32, D), FULL),
        ),
        in_specs=[vmem_spec()] * 13,
        out_specs=(vmem_spec(),) * 7,
        scratch_shapes=[
            pltpu.VMEM((SEQ_LEN + 8, 128), FULL),
            pltpu.VMEM((SEQ_LEN + 8, 128), FULL),
            pltpu.VMEM((SEQ_LEN, SEQ_LEN), FULL),
            pltpu.VMEM((SEQ_LEN, SEQ_LEN), FULL),
            pltpu.VMEM((HEADS_HERE, SEQ_LEN, 128), FULL),
            pltpu.VMEM((SEQ_LEN, INNER_HERE), LOW),
            pltpu.VMEM((SEQ_LEN, CONV_HERE), FULL),
            pltpu.VMEM((8, SEQ_LEN), FULL),
            pltpu.VMEM((8, SEQ_LEN), FULL),
            pltpu.VMEM((TILE, 128), FULL),
            pltpu.VMEM((128, SEQ_LEN), FULL),
        ]
        + scatter_buffers(PIECE, D)
        + [dma_sems(13), dma_sems(13)]
        + shard_scratch(downs)
        + shard_scratch(owned),
        compiler_params=pltpu.CompilerParams(
            collective_id=9, has_side_effects=True, vmem_limit_bytes=52 << 20
        ),
        cost_estimate=BUSY,
        name="mixer_backward",
    )(grad, projected, act, mixed, cum, step, taps, bias, head_cols, skip, blocks, downs, owned)


def adam_update(weight, old_first, old_second, gradient, step_rate, decay_rate):
    first_new = BETA_FIRST * old_first + (1.0 - BETA_FIRST) * gradient
    second_new = BETA_SECOND * old_second + (1.0 - BETA_SECOND) * gradient * gradient
    first_hat = first_new / (1.0 - BETA_FIRST**STEP)
    second_hat = second_new / (1.0 - BETA_SECOND**STEP)
    weight_new = weight - step_rate * (
        first_hat / (jnp.sqrt(second_hat) + ADAM_EPSILON) + decay_rate * weight
    )
    return (weight_new, first_new, second_new)


def update_kernel(dense_ref, shared_ref, aux_ref, owned_ref, up_ref, down_ref, gain_ref, *refs):
    olds = [refs[3 * index : 3 * index + 3] for index in range(9)]
    news = [refs[27 + 3 * index : 27 + 3 * index + 3] for index in range(9)]

    def step(index, gradient, rate, decay, at=()):
        old, new = olds[index], news[index]
        values = adam_update(old[0][at], old[1][at], old[2][at], gradient, rate, decay)
        for ref, value in zip(new, values):
            ref[at] = value

    rows = slice(None)
    state, rates = None, None
    place_row = lax.broadcasted_iota(jnp.int32, (128, 128), 0)
    place_col = lax.broadcasted_iota(jnp.int32, (128, 128), 1)
    for group in range(GROUPS):
        block = dense_ref[group].astype(FULL)
        for half in range(2):
            begin = half * INNER + group * INNER_HERE
            gradient = block[:, half * INNER_HERE : (half + 1) * INNER_HERE] * gain_ref[...]
            step(0, gradient, RATE_MATRIX, WEIGHT_DECAY, (rows, slice(begin, begin + INNER_HERE)))
            begin = half * FF_SH + group * SH_HERE
            gradient = shared_ref[group, :, half * SH_HERE : (half + 1) * SH_HERE].astype(FULL)
            step(1, gradient, RATE_MATRIX, WEIGHT_DECAY, (rows, slice(begin, begin + SH_HERE)))
        part = block[:, 2 * INNER_HERE : 2 * INNER_HERE + 2 * STATE]
        state = part if group == 0 else state + part
        moved = jnp.logical_and(place_row < HEADS_HERE, place_col == place_row + group * HEADS_HERE)
        part = dot(dense_ref[group, :, INNER_HERE + CONV_HERE : PROJ_HERE], moved.astype(LOW))
        rates = part if group == 0 else rates + part
    state, rates = state * gain_ref[...], rates * gain_ref[...]
    step(0, state, RATE_MATRIX, WEIGHT_DECAY, (rows, slice(2 * INNER, 2 * INNER + 2 * STATE)))
    step(0, rates[:, :HEADS], RATE_MATRIX, WEIGHT_DECAY, (rows, slice(INNER + CHANNELS, INNER + CHANNELS + HEADS)))
    step(2, owned_ref[:24], RATE_MATRIX, WEIGHT_DECAY, (slice(0, 24),))
    step(3, owned_ref[24:], RATE_MATRIX, WEIGHT_DECAY, (slice(0, 8),))

    def expert_step(index, sums, width, rate):
        def turn(count, carry):
            for row in range(8):
                at = count * 8 + row
                step(index, sums[pl.ds(at, 1), :width], rate, WEIGHT_DECAY, (at,))
            return carry

        lax.fori_loop(0, sums.shape[0] // 8, turn, 0)

    expert_step(4, up_ref, 2 * FF_EXP, RATE_MATRIX)
    expert_step(5, down_ref, D, RATE_DOWN)
    aux = aux_ref[0]
    for group in range(1, GROUPS):
        aux = aux + aux_ref[group]
    small = jnp.concatenate([aux[0:1], aux[1:2]], axis=1)[:, :178]
    step(6, small, RATE_SMALL, 0.0, (slice(0, 1),))
    step(7, aux[2:3, :96], RATE_MATRIX, WEIGHT_DECAY, (slice(0, 1),))
    step(8, aux[3:6, :HEADS], RATE_HEAD, 0.0, (slice(0, 3),))


def update(sums, triples):
    olds = [values for triple in triples for values in triple]
    news = pl.pallas_call(
        update_kernel,
        out_shape=tuple(jax.ShapeDtypeStruct(values.shape, FULL) for values in olds),
        in_specs=[vmem_spec()] * (7 + len(olds)),
        out_specs=(vmem_spec(),) * len(olds),
        compiler_params=pltpu.CompilerParams(vmem_limit_bytes=52 << 20),
        name="update",
    )(*sums, *olds)
    return [news[3 * index : 3 * index + 3] for index in range(len(triples))]


def route_combine(logit_values, onehot):
    picked = jnp.sum(logit_values[:, None, :] * onehot, axis=-1)
    route_probs = jax.nn.softmax(picked, axis=-1)
    return jnp.sum(route_probs[:, :, None] * onehot, axis=1)


def inverse_rms(values):
    return lax.rsqrt(jnp.mean(values * values, axis=-1, keepdims=True) + NORM_EPSILON)


def norm_back(values, inverse, gain, grad):
    shared = grad * gain
    inner = jnp.mean(values * shared, axis=-1, keepdims=True)
    grad_in = inverse * shared - values * (inverse * inverse * inverse * inner)
    return grad_in, jnp.sum(values * inverse * grad, axis=0)


def silu_slope(values, gate):
    return gate * (1.0 + values * (1.0 - gate))


def dot(left, right):
    return jnp.dot(left, right, preferred_element_type=FULL)


def dot_lhs_t(left, right):
    return lax.dot_general(left, right, (((0,), (0,)), ((), ())), preferred_element_type=FULL)


def dot_rhs_t(left, right):
    return lax.dot_general(left, right, (((1,), (1,)), ((), ())), preferred_element_type=FULL)


def side_rows(values):
    return jnp.pad(values, ((0, 0), (0, 7), (0, 0)))


def piece_order(forward):
    order = []
    for shard in range(SHARDS):
        for group in range(GROUPS):
            owner = shard * GROUPS + group
            user = ((shard % 2) * GROUPS + group) * GROUPS + shard // 2
            order.append((owner, user) if forward else (user, owner))
    return order


def local(
    hidden,
    cotangent,
    routes,
    head_params,
    head_first,
    head_second,
    small_params,
    small_first,
    small_second,
    proj_weight,
    proj_first,
    proj_second,
    out_weight,
    out_first,
    out_second,
    router_weight,
    router_first,
    router_second,
    experts_up,
    experts_up_first,
    experts_up_second,
    experts_down,
    experts_down_first,
    experts_down_second,
    shared_up,
    shared_up_first,
    shared_up_second,
    shared_down,
    shared_down_first,
    shared_down_second,
):
    group_index = lax.axis_index("seq")
    both = ("fsdp", "seq")
    inputs = hidden[0]
    out_grad = cotangent[0]

    proj_low = proj_weight.astype(LOW)
    misc = jnp.concatenate(
        [router_weight.astype(LOW), jnp.pad(small_params.astype(LOW), (0, 2)).reshape(12, SMALL_COLS)],
        axis=1,
    )
    columns = jnp.concatenate(
        [
            proj_low[:, :INNER].reshape(12, GROUPS, INNER_HERE),
            proj_low[:, INNER : 2 * INNER].reshape(12, GROUPS, INNER_HERE),
            jnp.broadcast_to(proj_low[:, None, 2 * INNER : INNER + CHANNELS], (12, GROUPS, 2 * STATE)),
            proj_low[:, INNER + CHANNELS :].reshape(12, GROUPS, HEADS_HERE),
            jnp.broadcast_to(misc[:, None], (12, GROUPS, 8 + SMALL_COLS)),
            jnp.zeros((12, GROUPS, 128 - HEADS_HERE - 8 - SMALL_COLS), LOW),
            shared_up.astype(LOW).reshape(12, 2, GROUPS, SH_HERE)[:, 0],
            shared_up.astype(LOW).reshape(12, 2, GROUPS, SH_HERE)[:, 1],
        ],
        axis=2,
    )
    columns = columns_out(columns.transpose(1, 0, 2)).reshape(96, -1)
    owned = jnp.concatenate([out_weight.astype(LOW), shared_down.astype(LOW)], axis=0)
    owned = lax.ppermute(owned, both, piece_order(True))

    first_inverse = inverse_rms(inputs)
    unit_rows, weights, out_here = start_gather(
        (inputs * first_inverse).astype(LOW), columns[:, :PROJ_HERE], owned[:24]
    )

    misc_at = INNER_HERE + CONV_HERE + HEADS_HERE
    misc = weights[:, misc_at : misc_at + EXPERTS + SMALL_COLS]
    router_full = misc[:, :EXPERTS]
    small_vec = (
        misc[:, EXPERTS:].reshape(SHARDS * GROUPS, 12 * SMALL_COLS)[:, :178].reshape(SMALL).astype(FULL)
    )
    gain_first, gain_second = small_vec[:D], small_vec[D : 2 * D]
    gain_mixer = lax.dynamic_slice_in_dim(small_vec, 2 * D + group_index * INNER_HERE, INNER_HERE)
    bias_all = small_vec[2 * D + INNER : 2 * D + INNER + CHANNELS]
    kernel_all = small_vec[2 * D + INNER + CHANNELS :].reshape(CONV, CHANNELS)
    conv_bias = jnp.concatenate(
        [lax.dynamic_slice_in_dim(bias_all, group_index * INNER_HERE, INNER_HERE), bias_all[INNER:]]
    )
    conv_kernel = jnp.concatenate(
        [
            lax.dynamic_slice_in_dim(kernel_all, group_index * INNER_HERE, INNER_HERE, 1),
            kernel_all[:, INNER:],
        ],
        axis=1,
    )
    head_local = lax.dynamic_slice_in_dim(head_params, group_index * HEADS_HERE, HEADS_HERE, 1)

    head_cols = jnp.stack([head_local[0], -jnp.exp(head_local[1])])
    head_cols = jnp.broadcast_to(jnp.pad(head_cols, ((0, 0), (0, 2)))[:, :, None], (2, 8, 128))
    skip_wide = jnp.repeat(head_local[2], HDIM)[None]
    projected, act, mixed, gated, out_part, square_side, cum_rows, step_rows, rows_cot, shared_here, shared_down_here = mixer_forward(
        unit_rows,
        gain_first[None],
        weights,
        out_here,
        conv_kernel,
        conv_bias[None],
        head_cols,
        gain_mixer[None],
        skip_wide,
        out_grad.astype(LOW),
        columns[:, PROJ_HERE:],
        owned[24:],
    )
    shared_here, shared_down_here = shared_here.reshape(D, 2 * SH_HERE), shared_down_here.reshape(SH_HERE, D)
    rows_cot = rows_cot.reshape(SEQ_LEN, D)
    raw_out, squares, up_here, down_here = mixed_scatter(
        out_part.reshape(GROUPS, PIECE, D),
        square_side,
        experts_up.reshape(96, 2 * FF_EXP).astype(LOW),
        experts_down.reshape(32, D).astype(LOW),
    )
    mixer_inverse = lax.rsqrt(jnp.sum(squares[:, 0], axis=0)[:, None] / INNER + NORM_EPSILON)
    middle = inputs + mixer_inverse * raw_out

    second_inverse = inverse_rms(middle)
    normed_two = (middle * second_inverse * gain_second).astype(LOW)
    logits = dot(normed_two, router_full)
    onehot = (routes[0][:, :, None] == jnp.arange(EXPERTS, dtype=jnp.int32)).astype(FULL)
    combine, route_pull = jax.vjp(lambda values: route_combine(values, onehot), logits)
    back_sum, combine_sides, block_part, up_total_grad, down_total_grad, shared_down_total_grad = experts(
        normed_two, combine.T, rows_cot.reshape(GROUPS, PIECE, D), up_here, shared_here, down_here, shared_down_here
    )

    logits_grad = route_pull(combine_sides[:, 0].T)[0].astype(LOW)
    normed_two_grad = back_sum + dot_rhs_t(logits_grad, router_full)
    router_grad = dot_lhs_t(normed_two, logits_grad)
    middle_from_norm, gain_second_grad = norm_back(middle, second_inverse, gain_second, normed_two_grad)
    middle_grad = out_grad + middle_from_norm
    mixer_grad = middle_grad.astype(LOW)
    mixer_inner = jnp.sum(mixer_grad.astype(FULL) * raw_out, axis=1, keepdims=True) / INNER
    mixer_fix = mixer_inverse * mixer_inverse * mixer_inverse * mixer_inner
    rows_mixer, stats, up_sum = middle_gather(
        mixer_grad,
        jnp.pad(jnp.concatenate([mixer_inverse, mixer_fix], axis=1).T, ((0, 6), (0, 0))),
        up_total_grad.reshape(SHARDS, 96, 2 * FF_EXP + 2 * SH_HERE),
    )

    rows_inverse = stats[:, 0].reshape(SEQ_LEN, 1)
    rows_fix = stats[:, 1].reshape(SEQ_LEN, 1)
    gated = gated.astype(FULL)
    gated_normed = (gated * rows_inverse * gain_mixer).astype(LOW)
    out_total_grad = dot_lhs_t(gated_normed, rows_mixer).astype(LOW)
    gated_normed_grad = dot_rhs_t(rows_mixer, out_here)
    gain_mixer_grad = jnp.sum(gated * rows_inverse * gated_normed_grad, axis=0)
    gated_grad = (rows_inverse * gain_mixer * gated_normed_grad - gated * rows_fix).astype(LOW)
    owned_grad = jnp.concatenate(
        [out_total_grad.reshape(SHARDS, 24, D), shared_down_total_grad.reshape(SHARDS, 8, D)], axis=1
    )

    proj_grad, conv_grads, skip_sums, head_sums, block_sum, down_sum, owned_sum = mixer_backward(
        gated_grad,
        projected,
        act,
        mixed,
        cum_rows,
        step_rows,
        conv_kernel,
        conv_bias[None],
        head_cols,
        skip_wide,
        block_part,
        down_total_grad.reshape(SHARDS, 32, D),
        owned_grad,
    )
    owned_sum = lax.ppermute(owned_sum.astype(LOW), both, piece_order(False)).astype(FULL)
    block_out = middle + block_sum
    conv_kernel_grad, conv_bias_grad = conv_grads[:CONV], conv_grads[CONV]
    skip_grad = jnp.sum(skip_sums[0].reshape(HEADS_HERE, HDIM), axis=1)
    bias_grad, log_decay_grad = head_sums[0, :HEADS_HERE, 0], head_sums[1, :HEADS_HERE, 0]
    unit_grad = dot_lhs_t(unit_rows, proj_grad)
    gain_first_grad = jnp.sum(unit_grad * weights.astype(FULL), axis=1)

    place = group_index * INNER_HERE
    kernel_wide = jnp.concatenate([jnp.zeros((CONV, INNER), FULL), conv_kernel_grad[:, INNER_HERE:]], axis=1)
    kernel_wide = lax.dynamic_update_slice_in_dim(kernel_wide, conv_kernel_grad[:, :INNER_HERE], place, 1)
    bias_wide = jnp.concatenate([jnp.zeros((INNER,), FULL), conv_bias_grad[INNER_HERE:]])
    bias_wide = lax.dynamic_update_slice_in_dim(bias_wide, conv_bias_grad[:INNER_HERE], place, 0)
    gain_wide = lax.dynamic_update_slice_in_dim(jnp.zeros((INNER,), FULL), gain_mixer_grad, place, 0)
    small_grad = jnp.concatenate(
        [gain_first_grad, gain_second_grad, gain_wide, bias_wide, kernel_wide.reshape(-1)]
    )
    small_grad = jnp.pad(small_grad.reshape(SHARDS * GROUPS, 178), ((0, 0), (0, 78))).reshape(SHARDS, 16, 128)
    router_rows = jnp.pad(router_grad.reshape(SHARDS, GROUPS, 96), ((0, 0), (0, 0), (0, 32)))
    head_grad = jnp.stack([bias_grad, log_decay_grad, skip_grad])
    head_rows = lax.dynamic_update_slice_in_dim(
        jnp.zeros((3, 128), FULL), head_grad, group_index * HEADS_HERE, 1
    )
    head_rows = jnp.pad(jnp.concatenate(hi_lo(head_rows)), ((0, 2), (0, 0)))
    aux_grad = jnp.concatenate(
        [
            small_grad.astype(LOW),
            router_rows.astype(LOW),
            jnp.broadcast_to(head_rows, (SHARDS, 8, 128)),
        ],
        axis=1,
    )
    normed_grad, column_sum, aux_sum = last_scatter(
        proj_grad, weights, unit_grad.astype(LOW).reshape(SHARDS, 96, PROJ_HERE), aux_grad
    )
    input_from_norm, unused = norm_back(inputs, first_inverse, gain_first, normed_grad)
    hidden_grad = middle_grad + input_from_norm

    shared_back = up_sum[:, 2 * FF_EXP :].astype(LOW).reshape(GROUPS, 12, 2 * SH_HERE)
    aux_side = jnp.concatenate(
        [
            aux_sum[:16].reshape(GROUPS, 2, 128),
            aux_sum[16:24].reshape(GROUPS, 1, 128),
            jnp.broadcast_to(aux_sum[24:27] + aux_sum[27:30], (GROUPS, 3, 128)),
            jnp.zeros((GROUPS, 2, 128), FULL),
        ],
        axis=1,
    )
    dense, shared_back, aux_back = columns_back(
        column_sum.astype(LOW).reshape(GROUPS, 12, PROJ_HERE), shared_back, aux_side
    )
    owner = lax.axis_index("fsdp") * GROUPS + group_index
    own_gain = lax.dynamic_slice_in_dim(gain_first, owner * 12, 12)[:, None]
    small_rows = [values[None] for values in (small_params, small_first, small_second)]
    router_rows = [values.reshape(1, 96) for values in (router_weight, router_first, router_second)]
    news = update(
        (dense, shared_back, aux_back, owned_sum, up_sum, down_sum, own_gain),
        (
            (proj_weight, proj_first, proj_second),
            (shared_up, shared_up_first, shared_up_second),
            (out_weight, out_first, out_second),
            (shared_down, shared_down_first, shared_down_second),
            (experts_up, experts_up_first, experts_up_second),
            (experts_down, experts_down_first, experts_down_second),
            small_rows,
            router_rows,
            (head_params, head_first, head_second),
        ),
    )
    proj_new, shared_up_new, out_new, shared_down_new, up_new, down_new, small_new, router_new, head_new = news
    small_new = [values[0] for values in small_new]
    router_new = [values.reshape(12, EXPERTS) for values in router_new]
    return (
        block_out[None],
        hidden_grad[None],
        *head_new,
        *small_new,
        *proj_new,
        *out_new,
        *router_new,
        *up_new,
        *down_new,
        *shared_up_new,
        *shared_down_new,
    )


def solution(mesh):
    return jax.shard_map(
        local,
        mesh=mesh,
        in_specs=(
            P("fsdp", "seq", None),
            P("fsdp", "seq", None),
            P("fsdp", "seq", None),
            P(),
            P(),
            P(),
            P(("fsdp", "seq")),
            P(("fsdp", "seq")),
            P(("fsdp", "seq")),
            P(("fsdp", "seq"), None),
            P(("fsdp", "seq"), None),
            P(("fsdp", "seq"), None),
            P(("fsdp", "seq"), None),
            P(("fsdp", "seq"), None),
            P(("fsdp", "seq"), None),
            P(("fsdp", "seq"), None),
            P(("fsdp", "seq"), None),
            P(("fsdp", "seq"), None),
            P("fsdp", "seq", None),
            P("fsdp", "seq", None),
            P("fsdp", "seq", None),
            P("fsdp", "seq", None),
            P("fsdp", "seq", None),
            P("fsdp", "seq", None),
            P(("fsdp", "seq"), None),
            P(("fsdp", "seq"), None),
            P(("fsdp", "seq"), None),
            P(("fsdp", "seq"), None),
            P(("fsdp", "seq"), None),
            P(("fsdp", "seq"), None),
        ),
        out_specs=(
            P("fsdp", "seq", None),
            P("fsdp", "seq", None),
            P(),
            P(),
            P(),
            P(("fsdp", "seq")),
            P(("fsdp", "seq")),
            P(("fsdp", "seq")),
            P(("fsdp", "seq"), None),
            P(("fsdp", "seq"), None),
            P(("fsdp", "seq"), None),
            P(("fsdp", "seq"), None),
            P(("fsdp", "seq"), None),
            P(("fsdp", "seq"), None),
            P(("fsdp", "seq"), None),
            P(("fsdp", "seq"), None),
            P(("fsdp", "seq"), None),
            P("fsdp", "seq", None),
            P("fsdp", "seq", None),
            P("fsdp", "seq", None),
            P("fsdp", "seq", None),
            P("fsdp", "seq", None),
            P("fsdp", "seq", None),
            P(("fsdp", "seq"), None),
            P(("fsdp", "seq"), None),
            P(("fsdp", "seq"), None),
            P(("fsdp", "seq"), None),
            P(("fsdp", "seq"), None),
            P(("fsdp", "seq"), None),
        ),
        check_vma=False,
    )
```

```python
import functools

import jax
import jax.numpy as jnp
from jax import lax
from jax.experimental import pallas as pl
from jax.experimental.pallas import tpu as pltpu
from jax.sharding import PartitionSpec as P

D = 1536
HEADS = 48
HDIM = 64
STATE = 128
CONV = 4
FF_EXP = 512
FF_SH = 1024
TOPK = 6
EXPERTS = 8
STEP = 5
INNER = 3072
CHANNELS = 3328
SMALL = 22784
GROUPS = 8
SHARDS = 16
HEADS_HERE = HEADS // GROUPS
INNER_HERE = INNER // GROUPS
SH_HERE = FF_SH // GROUPS
SEQ_LEN = 1024
PIECE = SEQ_LEN // GROUPS
CONV_HERE = INNER_HERE + 2 * STATE
PROJ_HERE = INNER_HERE + CONV_HERE + 128
SMALL_COLS = 15
ROUTER_AT = 100


NORM_EPSILON = 1e-05
BETA_FIRST = 0.9
BETA_SECOND = 0.95
ADAM_EPSILON = 1e-08
RATE_MATRIX = 0.04
RATE_DOWN = 0.1
RATE_SMALL = 0.3
RATE_HEAD = 1.0
WEIGHT_DECAY = 0.1
HIGHEST = lax.Precision.HIGHEST
LOW = jnp.bfloat16
FULL = jnp.float32
MESH = pl.DeviceIdType.MESH


def hi_lo(values):
    high = values.astype(LOW)
    return high, (values - high.astype(FULL)).astype(LOW)


BUSY = pl.CostEstimate(flops=30_000_000_000, bytes_accessed=4_000_000, transcendentals=0)


def seq_axis():
    me = lax.axis_index("seq")
    side, level = lax.rem(me, 2), lax.div(me, 2)

    def slot(up, other):
        return lax.rem(level + up + 4, 4) * 2 + (1 - side if other else side)

    return me, slot, lambda up, other: {"seq": slot(up, other)}


def fsdp_axis():
    me = lax.axis_index("fsdp")
    core, rest = lax.rem(me, 2), lax.div(me, 2)
    side, level = lax.rem(rest, 2), lax.div(rest, 2)

    def slot(up, other):
        return lax.rem(level + up + 4, 4) * 2 + (1 - side if other else side)

    return core, slot, lambda up, other: {"fsdp": slot(up, other) * 2 + core}, {"fsdp": rest * 2 + 1 - core}


def meet(devices):
    barrier = pltpu.get_barrier_semaphore()
    for device in devices:
        pl.semaphore_signal(barrier, inc=1, device_id=device, device_id_type=MESH)
    pl.semaphore_wait(barrier, len(devices))


def ring_peers(device):
    return [device(0, True), device(1, False), device(-1, False)]


def sender(send_sem, recv_sem, started):
    def send(source, target, device):
        index = len(started)
        copy = pltpu.make_async_remote_copy(
            src_ref=source,
            dst_ref=target,
            send_sem=send_sem.at[index],
            recv_sem=recv_sem.at[index],
            device_id=device,
            device_id_type=MESH,
        )
        copy.start()
        started.append(copy)
        return copy

    return send


def take_turns(*programs):
    waiting = list(programs)
    while waiting:
        for program in list(waiting):
            if next(program, None) is None:
                waiting.remove(program)


def follow(order, ring, shards):
    for which in order:
        for program in [ring] if which == "z" else shards:
            next(program, None)


def ring_gather(source, place, slot, device, send, arrived, split=True):
    rows = source.shape[0]
    halves = ((pl.ds(0, rows // 2),), (pl.ds(rows // 2, rows // 2),)) if split else ((), None)
    own = place(slot(0, False), ())
    to_side = send(source, own, device(0, True))
    up = send(source, own, device(1, False))
    down = send(source, own, device(-1, False))
    arrived(source, own)
    yield True
    far, two = [], []

    def pass_on(copy, up, other, index):
        copy.wait_recv()
        if halves[index] is not None:
            part = place(slot(-up, other), halves[index])
            far.append(send(part, part, device(up, False)))
        block = place(slot(-up, other), ())
        arrived(block, block)

    def far_here(index, other):
        if halves[index % 2] is not None:
            far.pop(0).wait_recv()
            part = place(slot(2, other), halves[index % 2])
            arrived(part, part)

    pass_on(up, 1, False, 0)
    yield True
    pass_on(down, -1, False, 1)
    yield True
    to_side.wait_recv()
    block = place(slot(0, True), ())
    two.append(send(block, block, device(1, False)))
    two.append(send(block, block, device(-1, False)))
    arrived(block, block)
    yield True
    for index in range(2):
        far_here(index, False)
        yield True
    pass_on(two[0], 1, True, 0)
    yield True
    pass_on(two[1], -1, True, 1)
    yield True
    for index in range(2):
        far_here(index, True)
        yield True


def nothing(source, target):
    return None


def side_start(side_ref, side_out, per_peer, send_sem, recv_sem, local_sem):
    me = lax.axis_index("seq")
    copies = []
    for step in range(1, GROUPS):
        other = lax.rem(me + step, GROUPS)
        copy = pltpu.make_async_remote_copy(
            src_ref=side_ref.at[other] if per_peer else side_ref,
            dst_ref=side_out.at[me],
            send_sem=send_sem.at[step],
            recv_sem=recv_sem.at[step],
            device_id={"seq": other},
            device_id_type=MESH,
        )
        copy.start()
        copies.append(copy)
    keep = pltpu.make_async_copy(side_ref.at[me] if per_peer else side_ref, side_out.at[me], local_sem)
    keep.start()
    return copies, keep


def side_end(copies, keep):
    for copy in copies:
        copy.wait_recv()
    for copy in copies:
        copy.wait_send()
    keep.wait()


def all_peers():
    me = lax.axis_index("seq")
    return [{"seq": lax.rem(me + step, GROUPS)} for step in range(1, GROUPS)]


def gather_kernel(x_ref, side_ref, out_ref, side_out, send_sem, recv_sem, local_sem, s_send, s_recv, s_local):
    me, slot, device = seq_axis()
    meet(all_peers())
    started = []
    send = sender(send_sem, recv_sem, started)
    program = ring_gather(x_ref, lambda at, cut: out_ref.at[(at, *cut)], slot, device, send, nothing)
    next(program)
    sides = side_start(side_ref, side_out, False, s_send, s_recv, s_local)
    keep = pltpu.make_async_copy(x_ref, out_ref.at[me], local_sem)
    keep.start()
    take_turns(program)
    side_end(*sides)
    for copy in started:
        copy.wait_send()
    keep.wait()


def any_spec():
    return pl.BlockSpec(memory_space=pl.ANY)


def vmem_spec():
    return pl.BlockSpec(memory_space=pltpu.VMEM)


def dma_sems(count):
    return pltpu.SemaphoreType.DMA((count,))


def seq_gather(piece, side, name, collective_id):
    rows, width = piece.shape
    gathered, sides = pl.pallas_call(
        gather_kernel,
        out_shape=(
            jax.ShapeDtypeStruct((GROUPS, rows, width), piece.dtype),
            jax.ShapeDtypeStruct((GROUPS, 8, 128), FULL),
        ),
        in_specs=[any_spec()] * 2,
        out_specs=(any_spec(), any_spec()),
        scratch_shapes=[
            dma_sems(9),
            dma_sems(9),
            pltpu.SemaphoreType.DMA,
            dma_sems(GROUPS),
            dma_sems(GROUPS),
            pltpu.SemaphoreType.DMA,
        ],
        compiler_params=pltpu.CompilerParams(collective_id=collective_id, has_side_effects=True),
        cost_estimate=BUSY,
        name=name,
    )(piece, side)
    return gathered.reshape(GROUPS * rows, width), sides


def shard_gather(source, target, send_sem, recv_sem, started, crossing, split=True):
    core, slot, device, twin = fsdp_axis()
    send = sender(send_sem, recv_sem, started)

    def place(at, cut):
        return target.at[(at * 2 + core, *cut)]

    def arrived(origin, block):
        crossing.append(send(origin, block, twin))

    return ring_gather(source, place, slot, device, send, arrived, split)


START_COUNT = 2


def start_kernel(x_ref, *rest):
    sources, x_out, targets = rest[:START_COUNT], rest[START_COUNT], rest[START_COUNT + 1 : 2 * START_COUNT + 1]
    x_send, x_recv, keeps, *sems = rest[2 * START_COUNT + 1 :]
    me, slot, device = seq_axis()
    core, f_slot, f_device, twin = fsdp_axis()
    meet(ring_peers(device) + ring_peers(f_device) + [twin])
    mine = f_slot(0, False) * 2 + core
    x_started, started, crossing, kept = [], [], [], []
    x_sender = sender(x_send, x_recv, x_started)
    program = ring_gather(x_ref, lambda at, cut: x_out.at[(at, *cut)], slot, device, x_sender, nothing)
    shards = []
    for index, (source, target) in enumerate(zip(sources, targets)):
        copies = []
        started.append(copies)
        shards.append(
            shard_gather(
                source, target, sems[2 * index], sems[2 * index + 1], copies, crossing, source.shape[0] % 32 == 0
            )
        )
        keep = pltpu.make_async_copy(source, target.at[mine], keeps.at[index])
        keep.start()
        kept.append(keep)
    keep = pltpu.make_async_copy(x_ref, x_out.at[me], keeps.at[START_COUNT])
    keep.start()
    kept.append(keep)
    follow("yzyyyzzyyzyyyyzzzzzz", program, shards)
    take_turns(program, *shards)
    for copy in crossing:
        copy.wait_recv()
    for copies in (x_started, *started):
        for copy in copies:
            copy.wait_send()
    for keep in kept:
        keep.wait()


def start_gather(piece, *shards):
    rows, width = piece.shape
    out = pl.pallas_call(
        start_kernel,
        out_shape=(jax.ShapeDtypeStruct((GROUPS, rows, width), LOW),)
        + tuple(jax.ShapeDtypeStruct((SHARDS, *shard.shape), LOW) for shard in shards),
        in_specs=[any_spec()] * (1 + START_COUNT),
        out_specs=(any_spec(),) * (1 + START_COUNT),
        scratch_shapes=[dma_sems(9)] * 2 + [dma_sems(START_COUNT + 1)] + [dma_sems(19)] * (2 * START_COUNT),
        compiler_params=pltpu.CompilerParams(collective_id=2, has_side_effects=True),
        cost_estimate=BUSY,
        name="rows_first",
    )(piece, *shards)
    return [out[0].reshape(GROUPS * rows, width)] + [
        full.reshape(SHARDS * shard.shape[0], -1) for full, shard in zip(out[1:], shards)
    ]


def staged(source, target, sem):
    copies = [pltpu.make_async_copy(source, target, sem)]
    copies[0].start()

    def ready():
        if copies:
            copies.pop().wait()
        return target

    return ready


def ring_scatter(block, slot, device, send, result, buffers, raw=None, near_first=False):
    raw = raw or block
    in_low, in_high, sum_up, sum_down, land_low, land_high, part_out, part_in = buffers
    rows = part_out.shape[0]
    half = rows // 2
    first, second = pl.ds(0, half), pl.ds(half, half)
    everything = pl.ds(0, rows)
    landing = {}

    def begin_far(turn, other):
        far = raw(2, other)
        return [
            send(far(first), in_low.at[turn], device(1, False)),
            send(far(second), in_high.at[turn], device(-1, False)),
        ]

    def begin_near(turn, other):
        landing[turn] = [
            send(raw(1, other)(second), land_low.at[turn, second], device(1, False)),
            send(raw(-1, other)(first), land_high.at[turn, first], device(-1, False)),
        ]

    def begin(turn, other):
        copies = begin_far(turn, other)
        begin_near(turn, other)
        return copies

    def middle(turn, other, copies):
        copies[0].wait_recv()
        sum_up[turn] = (in_low[turn].astype(FULL) + block(1, other)(first)[...].astype(FULL)).astype(LOW)
        landing[turn].append(send(sum_up.at[turn], land_low.at[turn, first], device(1, False)))
        copies[1].wait_recv()
        sum_down[turn] = (in_high[turn].astype(FULL) + block(-1, other)(second)[...].astype(FULL)).astype(LOW)
        landing[turn].append(send(sum_down.at[turn], land_high.at[turn, second], device(-1, False)))

    def total(turn, other):
        for copy in landing[turn]:
            copy.wait_recv()
        return (
            block(0, other)(everything)[...].astype(FULL)
            + land_low[turn].astype(FULL)
            + land_high[turn].astype(FULL)
        )

    if near_first:
        begin_near(0, True)
        yield True
        copies = begin_far(0, True)
    else:
        copies = begin(0, True)
    yield True
    middle(0, True, copies)
    yield True
    copies = begin(1, False)
    yield True
    part_out[...] = total(0, True).astype(LOW)
    to_side = send(part_out, part_in, device(0, True))
    yield True
    middle(1, False, copies)
    yield True
    result[...] = total(1, False)
    yield True
    to_side.wait_recv()
    result[...] += part_in[...].astype(FULL)


def scatter_buffers(rows, width):
    half = rows // 2
    return (
        [pltpu.VMEM((2, half, width), LOW)] * 4
        + [pltpu.VMEM((2, rows, width), LOW)] * 2
        + [pltpu.VMEM((rows, width), LOW)] * 2
    )


def block_of(x_ref, slot):
    def block(up, other):
        return lambda cut: x_ref.at[slot(up, other), cut]

    return block


def block_ready(ready, slot):
    def block(up, other):
        return lambda cut: ready().at[slot(up, other), cut]

    return block


def mixed_kernel(x_ref, side_ref, u_ref, d_ref, out_ref, side_out, u_out, d_out, *rest):
    buffers, (send_sem, recv_sem, s_send, s_recv, s_local) = rest[:8], rest[8:13]
    u_send, u_recv, d_send, d_recv, keeps, x_vmem, x_sem = rest[13:]
    me, slot, device = seq_axis()
    core, f_slot, f_device, twin = fsdp_axis()
    x_ready = staged(x_ref, x_vmem, x_sem)
    meet(all_peers() + ring_peers(f_device) + [twin])
    started, u_started, d_started, crossing = [], [], [], []
    send = sender(send_sem, recv_sem, started)
    program = ring_scatter(
        block_ready(x_ready, slot), slot, device, send, out_ref, buffers, block_of(x_ref, slot)
    )
    next(program)
    sides = side_start(side_ref, side_out, True, s_send, s_recv, s_local)
    mine = f_slot(0, False) * 2 + core
    kept = []
    for index, (source, block) in enumerate(((u_ref, u_out.at[mine]), (d_ref, d_out.at[mine]))):
        keep = pltpu.make_async_copy(source, block, keeps.at[index])
        keep.start()
        kept.append(keep)
    shards = [
        shard_gather(u_ref, u_out, u_send, u_recv, u_started, crossing),
        shard_gather(d_ref, d_out, d_send, d_recv, d_started, crossing),
    ]
    follow("yzyyzyyyzyyzyyzz", program, shards)
    take_turns(program, *shards)
    side_end(*sides)
    for copy in crossing:
        copy.wait_recv()
    for copy in started + u_started + d_started:
        copy.wait_send()
    for keep in kept:
        keep.wait()


def mixed_scatter(parts, side, up_piece, down_piece):
    groups, rows, width = parts.shape
    summed, sides, up_all, down_all = pl.pallas_call(
        mixed_kernel,
        out_shape=(
            jax.ShapeDtypeStruct((rows, width), FULL),
            jax.ShapeDtypeStruct((GROUPS, 8, 128), FULL),
            jax.ShapeDtypeStruct((SHARDS, *up_piece.shape), LOW),
            jax.ShapeDtypeStruct((SHARDS, *down_piece.shape), LOW),
        ),
        in_specs=[any_spec(), vmem_spec(), any_spec(), any_spec()],
        out_specs=(vmem_spec(), vmem_spec(), any_spec(), any_spec()),
        scratch_shapes=scatter_buffers(rows, width)
        + [dma_sems(13), dma_sems(13), dma_sems(GROUPS), dma_sems(GROUPS), pltpu.SemaphoreType.DMA]
        + [dma_sems(19)] * 4
        + [dma_sems(2), pltpu.VMEM(parts.shape, LOW), pltpu.SemaphoreType.DMA],
        compiler_params=pltpu.CompilerParams(
            collective_id=4, has_side_effects=True, vmem_limit_bytes=52 << 20
        ),
        cost_estimate=BUSY,
        name="mixer_out",
    )(parts, side, up_piece, down_piece)
    return summed, sides, up_all.reshape(-1, up_piece.shape[1]), down_all.reshape(-1, down_piece.shape[1])


def shard_scratch(grads):
    depth, columns = grads.shape[1:]
    return (
        scatter_buffers(depth, columns)
        + [pltpu.VMEM((GROUPS, depth, columns), LOW)]
        + [dma_sems(13), dma_sems(13), dma_sems(8), dma_sems(8)]
    )


SHARD_SCRATCH = 13


def shard_scatters(arrays, started):
    core, slot, device, twin = fsdp_axis()
    order = [(2, True), (1, True), (-1, True), (2, False), (1, False), (-1, False), (0, True), (0, False)]
    programs, senders = [], []
    for pick, value, target, scratch in arrays:
        buffers, (core_in, send_sem, recv_sem, c_send, c_recv) = scratch[:8], scratch[8:]
        crossing, copies, arriving = [], [], {}
        started.extend([crossing, copies])
        senders.append((pick, core_in, sender(c_send, c_recv, crossing), arriving))

        def block(up, other, value=value, core_in=core_in, arriving=arriving):
            at = slot(up, other)
            if (up, other) in arriving:
                arriving.pop((up, other)).wait_recv()
                core_in[at] = (core_in[at].astype(FULL) + value(at * 2 + core)[...].astype(FULL)).astype(LOW)
            return lambda cut: core_in.at[at, cut]

        programs.append(ring_scatter(block, slot, device, sender(send_sem, recv_sem, copies), target, buffers))
    for key in order:
        for pick, core_in, send_core, arriving in senders:
            at = slot(*key)
            arriving[key] = send_core(pick(at * 2 + 1 - core), core_in.at[at], twin)
    return programs


def blocks_of(ref):
    return lambda at: ref.at[at]


def ready_blocks(ready):
    return lambda at: ready().at[at]


def shard_peers():
    core, slot, device, twin = fsdp_axis()
    return ring_peers(device) + [twin]


def last_kernel(g_any, p_any, w_any, a_ref, x_out, w_out, a_out, x_ref, w_ref, g_ref, p_ref, stages, *rest):
    x_buffers, (x_send, x_recv) = rest[:8], rest[8:10]
    me, slot, device = seq_axis()
    g_ready = staged(g_any, g_ref, stages.at[0])
    p_ready = staged(p_any, p_ref, stages.at[1])
    w_ready = staged(w_any, w_ref, stages.at[2])
    done = set()

    def part_of(up, other):
        at = slot(up, other)
        if (up, other) not in done:
            done.add((up, other))
            here = pl.ds(pl.multiple_of(at * PIECE, PIECE), PIECE)
            g_ready(), p_ready()
            for part in range(D // 512):
                cols = slice(part * 512, (part + 1) * 512)
                x_ref[at, :, cols] = dot_rhs_t(g_ref[here, :], p_ref[cols, :]).astype(LOW)
        return lambda cut: x_ref.at[at, cut]

    meet(ring_peers(device) + shard_peers())
    x_started, started = [], []
    program = ring_scatter(part_of, slot, device, sender(x_send, x_recv, x_started), x_out, x_buffers)
    main, small = shard_scatters(
        [
            (blocks_of(w_any), ready_blocks(w_ready), w_out, rest[10 : 10 + SHARD_SCRATCH]),
            (blocks_of(a_ref), blocks_of(a_ref), a_out, rest[10 + SHARD_SCRATCH :]),
        ],
        started,
    )
    follow("zyzyzyyzyzyzyz", program, [main, small])
    take_turns(program, main, small)
    for copies in (x_started, *started):
        for copy in copies:
            copy.wait_send()


def last_scatter(proj_grad, weights, grads, small):
    rows, width = PIECE, D
    return pl.pallas_call(
        last_kernel,
        out_shape=(
            jax.ShapeDtypeStruct((rows, width), FULL),
            jax.ShapeDtypeStruct(grads.shape[1:], FULL),
            jax.ShapeDtypeStruct(small.shape[1:], FULL),
        ),
        in_specs=[any_spec(), any_spec(), any_spec(), vmem_spec()],
        out_specs=(vmem_spec(),) * 3,
        scratch_shapes=[
            pltpu.VMEM((GROUPS, rows, width), LOW),
            pltpu.VMEM(grads.shape, LOW),
            pltpu.VMEM(proj_grad.shape, LOW),
            pltpu.VMEM(weights.shape, LOW),
            dma_sems(3),
        ]
        + scatter_buffers(rows, width)
        + [dma_sems(13), dma_sems(13)]
        + shard_scratch(grads)
        + shard_scratch(small),
        compiler_params=pltpu.CompilerParams(
            collective_id=8, has_side_effects=True, vmem_limit_bytes=52 << 20
        ),
        cost_estimate=BUSY,
        name="rows_last",
    )(proj_grad, weights, grads, small)


def middle_kernel(x_ref, side_ref, u_ref, x_out, side_out, u_out, *rest):
    x_send, x_recv, x_local, s_send, s_recv, s_local = rest[:6]
    me, slot, device = seq_axis()
    meet(all_peers() + shard_peers())
    x_started, started = [], []
    send = sender(x_send, x_recv, x_started)
    program = ring_gather(x_ref, lambda at, cut: x_out.at[(at, *cut)], slot, device, send, nothing)
    next(program)
    [shard] = shard_scatters([(blocks_of(u_ref), blocks_of(u_ref), u_out, rest[6:])], started)
    sides = side_start(side_ref, side_out, False, s_send, s_recv, s_local)
    keep = pltpu.make_async_copy(x_ref, x_out.at[me], x_local)
    keep.start()
    follow("yyyzzyzyzzyyzzzz", program, [shard])
    take_turns(program, shard)
    side_end(*sides)
    for copies in (x_started, *started):
        for copy in copies:
            copy.wait_send()
    keep.wait()


def middle_gather(piece, side, up_grads):
    rows, width = piece.shape
    gathered, sides, up_sum = pl.pallas_call(
        middle_kernel,
        out_shape=(
            jax.ShapeDtypeStruct((GROUPS, rows, width), piece.dtype),
            jax.ShapeDtypeStruct((GROUPS, 8, 128), FULL),
            jax.ShapeDtypeStruct(up_grads.shape[1:], FULL),
        ),
        in_specs=[any_spec(), any_spec(), vmem_spec()],
        out_specs=(any_spec(), any_spec(), vmem_spec()),
        scratch_shapes=[
            dma_sems(9),
            dma_sems(9),
            pltpu.SemaphoreType.DMA,
            dma_sems(GROUPS),
            dma_sems(GROUPS),
            pltpu.SemaphoreType.DMA,
        ]
        + shard_scratch(up_grads),
        compiler_params=pltpu.CompilerParams(
            collective_id=7, has_side_effects=True, vmem_limit_bytes=52 << 20
        ),
        cost_estimate=BUSY,
        name="rows_mixer",
    )(piece, side, up_grads)
    return gathered.reshape(GROUPS * rows, width), sides, up_sum


UNITS = FF_EXP + SH_HERE
HIDDEN_COLS = 2 * UNITS


def experts_kernel(
    x_ref,
    side_ref,
    cot_any,
    up_any,
    shared_any,
    down_any,
    shared_down_any,
    back_out,
    side_back,
    block_any,
    up_grad_any,
    down_grad_any,
    shared_grad_any,
    cot_ref,
    up_ref,
    shared_ref,
    down_ref,
    shared_down_ref,
    block_ref,
    up_grad_ref,
    down_grad_ref,
    shared_grad_ref,
    rows_ref,
    sides_in,
    parts_ref,
    gu_ref,
    act_ref,
    side_send,
    *rest,
):
    buffers, rest = rest[:8], rest[8:]
    g_send, g_recv, g_local, s_send, s_recv, s_local, r_send, r_recv, b_send, b_recv, b_local, moves = rest
    me, slot, device = seq_axis()
    moving = []

    def move(source, target):
        copy = pltpu.make_async_copy(source, target, moves.at[len(moving)])
        copy.start()
        moving.append(copy)

    for source, target in (
        (up_any, up_ref),
        (down_any, down_ref),
        (cot_any, cot_ref),
        (shared_any, shared_ref),
        (shared_down_any, shared_down_ref),
    ):
        move(source, target)
    meet(all_peers())
    started = []
    gather = ring_gather(
        x_ref, lambda at, cut: rows_ref.at[(at, *cut)], slot, device, sender(g_send, g_recv, started), nothing
    )
    next(gather)
    sides = side_start(side_ref, sides_in, False, s_send, s_recv, s_local)
    keep = pltpu.make_async_copy(x_ref, rows_ref.at[me], g_local)
    keep.start()
    keep.wait()
    for copy in moving:
        copy.wait()
    side_end(*sides)

    def unit_step(hidden, cot, weights, downs, width, gu_at, half, scale):
        gate = dot(hidden, weights[:, gu_at : gu_at + width])
        lift = dot(hidden, weights[:, gu_at + half : gu_at + half + width])
        back = dot_rhs_t(cot, downs)
        gate_sig = sigmoid(gate)
        gate_silu = gate * gate_sig
        act = (gate_silu * lift).astype(LOW).astype(FULL)
        product = back * act
        if scale is not None:
            scale = jnp.concatenate([scale] * (width // 128), axis=1)
            act = act * scale
            back = back * scale
        gate_grad = back * lift * (gate_sig * (1.0 + gate * (1.0 - gate_sig)))
        return product, act.astype(LOW), gate_grad.astype(LOW), (back * gate_silu).astype(LOW)

    def joined(blocks):
        return blocks[0] if len(blocks) == 1 else jnp.concatenate(blocks, axis=0)

    def process(*keys):
        slots = [slot(*key) for key in keys]
        rows = [pl.ds(pl.multiple_of(at * PIECE, PIECE), PIECE) for at in slots]

        def put(ref, cols, values):
            for index, here in enumerate(rows):
                ref[here, cols] = values[index * PIECE : (index + 1) * PIECE]

        hidden = joined([rows_ref[at] for at in slots])
        cot = joined([cot_ref[at] for at in slots])
        scale = joined([jnp.broadcast_to(sides_in[at, pl.ds(me, 1), :], (128, 128)).T for at in slots])
        folded = None
        for begin in range(0, FF_EXP, 256):
            cols = slice(begin, begin + 256)
            product, act, gate_grad, lift_grad = unit_step(
                hidden, cot, up_ref, down_ref[cols, :], 256, begin, FF_EXP, scale
            )
            put(act_ref, cols, act)
            put(gu_ref, cols, gate_grad)
            put(gu_ref, slice(FF_EXP + begin, FF_EXP + begin + 256), lift_grad)
            product = product[:, :128] + product[:, 128:]
            folded = product if folded is None else folded + product
        unused, act, gate_grad, lift_grad = unit_step(
            hidden, cot, shared_ref, shared_down_ref[...], SH_HERE, 0, SH_HERE, None
        )
        put(act_ref, slice(FF_EXP, UNITS), act)
        put(gu_ref, slice(2 * FF_EXP, 2 * FF_EXP + SH_HERE), gate_grad)
        put(gu_ref, slice(2 * FF_EXP + SH_HERE, HIDDEN_COLS), lift_grad)
        sums = lax.dot_general(
            jnp.ones((8, 128), FULL),
            folded,
            (((1,), (1,)), ((), ())),
            precision=HIGHEST,
            preferred_element_type=FULL,
        )
        for index, at in enumerate(slots):
            side_send[at] = sums[:, index * PIECE : (index + 1) * PIECE]
        grads = joined([gu_ref[here, :] for here in rows])
        for begin in range(0, D, 512):
            cols = slice(begin, begin + 512)
            total = dot_rhs_t(grads[:, : 2 * FF_EXP], up_ref[cols, :])
            total = (total + dot_rhs_t(grads[:, 2 * FF_EXP :], shared_ref[cols, :])).astype(LOW)
            for index, at in enumerate(slots):
                parts_ref[at, :, cols] = total[index * PIECE : (index + 1) * PIECE]

    summed = []
    process((0, False))
    next(gather)
    next(gather)
    process((-1, False), (1, False))
    next(gather)
    next(gather)
    next(gather)
    process((0, True), (2, False))
    next(gather)
    next(gather)
    process((-1, True), (1, True))
    scatter = ring_scatter(
        block_of(parts_ref, slot),
        slot,
        device,
        sender(r_send, r_recv, summed),
        back_out,
        buffers,
        near_first=True,
    )
    next(scatter)
    take_turns(gather)
    process((2, True))

    next(scatter)
    backs = side_start(side_send, side_back, True, b_send, b_recv, b_local)

    def block_step(at, carry):
        rows = pl.ds(pl.multiple_of(at * PIECE, PIECE), PIECE)
        for begin in range(0, D, 512):
            cols = slice(begin, begin + 512)
            total = dot(act_ref[rows, :FF_EXP], down_ref[:, cols])
            total = total + dot(act_ref[rows, FF_EXP:], shared_down_ref[:, cols])
            block_ref[at, :, cols] = total.astype(LOW)
        return carry

    def up_step(part, carry):
        rows = pl.ds(pl.multiple_of(part * 256, 256), 256)
        left = rows_ref[:, :, rows].reshape(SEQ_LEN, 256).T
        for begin in range(0, HIDDEN_COLS, 640):
            cols = slice(begin, begin + 640)
            up_grad_ref[rows, cols] = dot(left, gu_ref[:, cols]).astype(LOW)
        return carry

    lax.fori_loop(0, 4, block_step, 0)
    next(scatter)
    next(scatter)
    lax.fori_loop(4, 8, block_step, 0)
    moving.clear()
    move(block_ref, block_any)
    next(scatter)
    lax.fori_loop(0, 3, up_step, 0)
    next(scatter)
    lax.fori_loop(3, 6, up_step, 0)
    move(up_grad_ref, up_grad_any)
    next(scatter)
    for row in range(0, UNITS, 128):
        left = act_ref[:, row : row + 128].T
        for begin in range(0, D, 512):
            cols = slice(begin, begin + 512)
            grads = dot(left, cot_ref[:, :, cols].reshape(SEQ_LEN, 512)).astype(LOW)
            if row < FF_EXP:
                down_grad_ref[row : row + 128, cols] = grads
            else:
                shared_grad_ref[:, cols] = grads
    move(down_grad_ref, down_grad_any)
    move(shared_grad_ref, shared_grad_any)
    take_turns(scatter)
    for copy in moving:
        copy.wait()
    side_end(*backs)
    for copy in started + summed:
        copy.wait_send()


def experts(piece, side, rows_cot, up, shared, down, shared_down):
    return pl.pallas_call(
        experts_kernel,
        out_shape=(
            jax.ShapeDtypeStruct((PIECE, D), FULL),
            jax.ShapeDtypeStruct((GROUPS, 8, 128), FULL),
            jax.ShapeDtypeStruct((GROUPS, PIECE, D), LOW),
            jax.ShapeDtypeStruct((D, HIDDEN_COLS), LOW),
            jax.ShapeDtypeStruct((FF_EXP, D), LOW),
            jax.ShapeDtypeStruct((SH_HERE, D), LOW),
        ),
        in_specs=[vmem_spec()] * 2 + [any_spec()] * 5,
        out_specs=(vmem_spec(),) * 2 + (any_spec(),) * 4,
        scratch_shapes=[
            pltpu.VMEM((GROUPS, PIECE, D), LOW),
            pltpu.VMEM((D, 2 * FF_EXP), LOW),
            pltpu.VMEM((D, 2 * SH_HERE), LOW),
            pltpu.VMEM((FF_EXP, D), LOW),
            pltpu.VMEM((SH_HERE, D), LOW),
            pltpu.VMEM((GROUPS, PIECE, D), LOW),
            pltpu.VMEM((D, HIDDEN_COLS), LOW),
            pltpu.VMEM((FF_EXP, D), LOW),
            pltpu.VMEM((SH_HERE, D), LOW),
            pltpu.VMEM((GROUPS, PIECE, D), LOW),
            pltpu.VMEM((GROUPS, 8, 128), FULL),
            pltpu.VMEM((GROUPS, PIECE, D), LOW),
            pltpu.VMEM((SEQ_LEN, HIDDEN_COLS), LOW),
            pltpu.VMEM((SEQ_LEN, UNITS), LOW),
            pltpu.VMEM((GROUPS, 8, 128), FULL),
        ]
        + scatter_buffers(PIECE, D)
        + [dma_sems(9), dma_sems(9), pltpu.SemaphoreType.DMA]
        + [dma_sems(GROUPS), dma_sems(GROUPS), pltpu.SemaphoreType.DMA]
        + [dma_sems(13), dma_sems(13)]
        + [dma_sems(GROUPS), dma_sems(GROUPS), pltpu.SemaphoreType.DMA]
        + [dma_sems(5)],
        compiler_params=pltpu.CompilerParams(
            collective_id=5, has_side_effects=True, vmem_limit_bytes=52 << 20
        ),
        cost_estimate=BUSY,
        name="experts",
    )(piece, side, rows_cot, up, shared, down, shared_down)


def swap_start(x_ref, out_ref, send_sem, recv_sem, local_sem):
    return side_start(x_ref, out_ref, True, send_sem, recv_sem, local_sem)


def columns_kernel(x_ref, x_out, x_send, x_recv, x_local):
    meet(all_peers())
    side_end(*swap_start(x_ref, x_out, x_send, x_recv, x_local))


def columns_out(blocks):
    return pl.pallas_call(
        columns_kernel,
        out_shape=jax.ShapeDtypeStruct(blocks.shape, blocks.dtype),
        in_specs=[any_spec()],
        out_specs=any_spec(),
        scratch_shapes=[dma_sems(GROUPS), dma_sems(GROUPS), pltpu.SemaphoreType.DMA],
        compiler_params=pltpu.CompilerParams(collective_id=1, has_side_effects=True),
        cost_estimate=BUSY,
        name="columns_out",
    )(blocks)


def back_kernel(x_ref, u_ref, side_ref, x_out, u_out, side_out, *sems):
    meet(all_peers())
    swaps = [
        swap_start(x_ref, x_out, *sems[:3]),
        swap_start(u_ref, u_out, *sems[3:6]),
        swap_start(side_ref, side_out, *sems[6:]),
    ]
    for swap in swaps:
        side_end(*swap)


def columns_back(blocks, shared, side):
    return pl.pallas_call(
        back_kernel,
        out_shape=(
            jax.ShapeDtypeStruct(blocks.shape, blocks.dtype),
            jax.ShapeDtypeStruct(shared.shape, shared.dtype),
            jax.ShapeDtypeStruct(side.shape, side.dtype),
        ),
        in_specs=[any_spec()] * 3,
        out_specs=(any_spec(),) * 3,
        scratch_shapes=[dma_sems(GROUPS), dma_sems(GROUPS), pltpu.SemaphoreType.DMA] * 3,
        compiler_params=pltpu.CompilerParams(collective_id=10, has_side_effects=True),
        cost_estimate=BUSY,
        name="columns_back",
    )(blocks, shared, side)


TILE = 256
TILES = SEQ_LEN // TILE
PAIRS = HEADS_HERE // 2


def scan_lanes(values, backward):
    length = values.shape[1]
    lane = lax.broadcasted_iota(jnp.int32, values.shape, 1)
    step = 1
    while step < length:
        if backward:
            values = values + jnp.where(lane < length - step, pltpu.roll(values, length - step, 1), 0.0)
        else:
            values = values + jnp.where(lane >= step, pltpu.roll(values, step, 1), 0.0)
        step *= 2
    return values


def sigmoid(values):
    return 1.0 / (1.0 + jnp.exp(-values))


def conv_taps(padded, taps, at):
    total = taps[0:1, at] * padded[5 : 5 + SEQ_LEN]
    for tap in range(1, CONV):
        total = total + taps[tap : tap + 1, at] * padded[5 + tap : 5 + tap + SEQ_LEN]
    return total


def scores_and_columns(b_state, c_state, cum_rows, scores, columns):
    for low in range(TILES):
        for far in range(low + 1):
            scores[low * TILE : (low + 1) * TILE, far * TILE : (far + 1) * TILE] = dot_rhs_t(
                c_state[low * TILE : (low + 1) * TILE], b_state[far * TILE : (far + 1) * TILE]
            )
    turned = jnp.concatenate([cum_rows, jnp.zeros((120, SEQ_LEN), FULL)], axis=0).T
    for head in range(HEADS_HERE):
        columns[head] = jnp.broadcast_to(turned[:, head : head + 1], (SEQ_LEN, 128))


def decay_tile(columns, cum_ref, head, low, far):
    column = columns[head, low * TILE : (low + 1) * TILE]
    row = cum_ref[pl.ds(head, 1), far * TILE : (far + 1) * TILE]
    return jnp.exp(jnp.minimum(jnp.concatenate([column] * (TILE // 128), axis=1) - row, 0.0))


def lower_tile():
    shape = (TILE, TILE)
    return lax.broadcasted_iota(jnp.int32, shape, 0) >= lax.broadcasted_iota(jnp.int32, shape, 1)


def mixer_forward_kernel(
    unit_any,
    first_ref,
    weight_any,
    out_weight_ref,
    taps_ref,
    bias_ref,
    head_ref,
    gain_ref,
    skip_ref,
    cot_ref,
    shared_ref,
    shared_down_ref,
    proj_any,
    act_any,
    mixed_any,
    gated_any,
    part_any,
    side_ref,
    cum_ref,
    step_ref,
    cot_out,
    shared_out,
    shared_down_out,
    unit_ref,
    weight_ref,
    proj_ref,
    act_ref,
    mixed_ref,
    gated_ref,
    part_ref,
    padded,
    scores,
    columns,
    scaled_ref,
    c_send,
    c_recv,
    c_local,
    moves,
    u_send,
    u_recv,
    d_send,
    d_recv,
    keeps,
):
    moving = []

    def move(source, target):
        copy = pltpu.make_async_copy(source, target, moves.at[len(moving)])
        copy.start()
        moving.append(copy)

    move(weight_any, weight_ref)
    move(unit_any, unit_ref)
    me, slot, device = seq_axis()
    core, f_slot, f_device, twin = fsdp_axis()
    meet(ring_peers(device) + ring_peers(f_device) + [twin])
    mine = f_slot(0, False) * 2 + core
    started, u_started, d_started, crossing, kept = [], [], [], [], []
    program = ring_gather(
        cot_ref, lambda at, cut: cot_out.at[(at, *cut)], slot, device, sender(c_send, c_recv, started), nothing
    )
    next(program)
    keep = pltpu.make_async_copy(cot_ref, cot_out.at[me], c_local)
    keep.start()
    shards = [
        shard_gather(shared_ref, shared_out, u_send, u_recv, u_started, crossing),
        shard_gather(shared_down_ref, shared_down_out, d_send, d_recv, d_started, crossing, False),
    ]
    for index, (source, block) in enumerate(
        ((shared_ref, shared_out.at[mine]), (shared_down_ref, shared_down_out.at[mine]))
    ):
        kept.append(pltpu.make_async_copy(source, block, keeps.at[index]))
        kept[-1].start()
    follow("y", program, shards)
    for copy in moving:
        copy.wait()
    moving.clear()

    def rows_step(tile, carry):
        here = pl.ds(pl.multiple_of(tile * TILE, TILE), TILE)
        normed = (unit_ref[here, :].astype(FULL) * first_ref[...]).astype(LOW)
        for part in range(PROJ_HERE // 384):
            at = slice(part * 384, (part + 1) * 384)
            proj_ref[here, at] = dot(normed, weight_ref[:, at]).astype(LOW)
        return carry

    lax.fori_loop(0, TILES, rows_step, 0)
    move(proj_ref, proj_any)
    follow("yyyzz", program, shards)
    padded[0:8] = jnp.zeros((8, 128), FULL)
    for part in range(CONV_HERE // 128):
        at = slice(part * 128, (part + 1) * 128)
        padded[8:] = proj_ref[:, INNER_HERE + part * 128 : INNER_HERE + (part + 1) * 128].astype(FULL)
        before = bias_ref[0:1, at] + conv_taps(padded, taps_ref, at)
        act_ref[:, at] = (before * sigmoid(before)).astype(LOW)
    rates = proj_ref[:, INNER_HERE + CONV_HERE :].astype(FULL).T[:8] + head_ref[0][:, :1]
    step_ref[...] = jnp.maximum(rates, 0.0) + jnp.log1p(jnp.exp(-jnp.abs(rates)))
    cum_ref[...] = scan_lanes(step_ref[...] * head_ref[1][:, :1], False)
    scores_and_columns(
        act_ref[:, INNER_HERE : INNER_HERE + STATE],
        act_ref[:, INNER_HERE + STATE :],
        cum_ref[...],
        scores,
        columns,
    )
    move(act_ref, act_any)
    follow("yyz", program, shards)

    def pair_step(pair, carry):
        at = pl.ds(pl.multiple_of(pair * 128, 128), 128)
        for low in range(TILES):
            here = slice(low * TILE, (low + 1) * TILE)
            sums = [None, None]
            for far in range(low + 1):
                there = slice(far * TILE, (far + 1) * TILE)
                for half in range(2):
                    head = pair * 2 + half
                    weight = scores[here, there] * decay_tile(columns, cum_ref, head, low, far)
                    weight = weight * step_ref[pl.ds(head, 1), there]
                    if far == low:
                        weight = jnp.where(lower_tile(), weight, 0.0)
                    term = dot(weight.astype(LOW), act_ref[there, at])
                    sums[half] = term if far == 0 else sums[half] + term
            first = lax.broadcasted_iota(jnp.int32, (TILE, 128), 1) < HDIM
            x_tile = act_ref[here, at].astype(FULL)
            mixed = jnp.where(first, sums[0], sums[1]) + skip_ref[0:1, at] * x_tile
            gate = proj_ref[here, at].astype(FULL)
            gated = (mixed * (gate * sigmoid(gate))).astype(LOW)
            mixed_ref[here, at] = mixed
            gated_ref[here, at] = gated
            scaled_ref[here, at] = (gated.astype(FULL) * gain_ref[0:1, at]).astype(LOW)
        return carry

    lax.fori_loop(0, PAIRS, pair_step, 0)
    move(mixed_ref, mixed_any)
    move(gated_ref, gated_any)
    follow("yyyyzzzz", program, shards)

    def out_step(tile, carry):
        here = pl.ds(pl.multiple_of(tile * TILE, TILE), TILE)
        for part in range(D // 512):
            at = slice(part * 512, (part + 1) * 512)
            part_ref[here, at] = dot(scaled_ref[here, :], out_weight_ref[:, at]).astype(LOW)
        return carry

    lax.fori_loop(0, TILES, out_step, 0)
    move(part_ref, part_any)
    wide = gated_ref[...].astype(FULL)
    squares = lax.dot_general(
        jnp.ones((8, INNER_HERE), FULL),
        wide * wide,
        (((1,), (1,)), ((), ())),
        precision=HIGHEST,
        preferred_element_type=FULL,
    )
    for piece in range(GROUPS):
        side_ref[piece] = squares[:, piece * PIECE : (piece + 1) * PIECE]
    take_turns(program, *shards)
    for copy in moving + kept:
        copy.wait()
    for copy in crossing:
        copy.wait_recv()
    for copy in started + u_started + d_started:
        copy.wait_send()
    keep.wait()


def mixer_forward(unit_rows, gain_first, weights, out_weights, taps, bias, head_cols, gain, skip, piece, shared, shared_down):
    return pl.pallas_call(
        mixer_forward_kernel,
        out_shape=(
            jax.ShapeDtypeStruct((SEQ_LEN, PROJ_HERE), LOW),
            jax.ShapeDtypeStruct((SEQ_LEN, CONV_HERE), LOW),
            jax.ShapeDtypeStruct((SEQ_LEN, INNER_HERE), FULL),
            jax.ShapeDtypeStruct((SEQ_LEN, INNER_HERE), LOW),
            jax.ShapeDtypeStruct((SEQ_LEN, D), LOW),
            jax.ShapeDtypeStruct((GROUPS, 8, PIECE), FULL),
            jax.ShapeDtypeStruct((8, SEQ_LEN), FULL),
            jax.ShapeDtypeStruct((8, SEQ_LEN), FULL),
            jax.ShapeDtypeStruct((GROUPS, PIECE, D), LOW),
            jax.ShapeDtypeStruct((SHARDS, *shared.shape), LOW),
            jax.ShapeDtypeStruct((SHARDS, *shared_down.shape), LOW),
        ),
        in_specs=[any_spec(), vmem_spec(), any_spec()] + [vmem_spec()] * 6 + [any_spec()] * 3,
        out_specs=(any_spec(),) * 5 + (vmem_spec(),) * 3 + (any_spec(),) * 3,
        scratch_shapes=[
            pltpu.VMEM((SEQ_LEN, D), LOW),
            pltpu.VMEM((D, PROJ_HERE), LOW),
            pltpu.VMEM((SEQ_LEN, PROJ_HERE), LOW),
            pltpu.VMEM((SEQ_LEN, CONV_HERE), LOW),
            pltpu.VMEM((SEQ_LEN, INNER_HERE), FULL),
            pltpu.VMEM((SEQ_LEN, INNER_HERE), LOW),
            pltpu.VMEM((SEQ_LEN, D), LOW),
            pltpu.VMEM((SEQ_LEN + 8, 128), FULL),
            pltpu.VMEM((SEQ_LEN, SEQ_LEN), FULL),
            pltpu.VMEM((HEADS_HERE, SEQ_LEN, 128), FULL),
            pltpu.VMEM((SEQ_LEN, INNER_HERE), LOW),
            dma_sems(9),
            dma_sems(9),
            pltpu.SemaphoreType.DMA,
            dma_sems(6),
        ]
        + [dma_sems(19)] * 4
        + [dma_sems(2)],
        compiler_params=pltpu.CompilerParams(
            collective_id=3, has_side_effects=True, vmem_limit_bytes=52 << 20
        ),
        cost_estimate=BUSY,
        name="mixer_forward",
    )(unit_rows, gain_first, weights, out_weights, taps, bias, head_cols, gain, skip, piece, shared, shared_down)


def mixer_backward_kernel(
    grad_ref,
    proj_ref,
    act_ref,
    mixed_ref,
    cum_ref,
    step_ref,
    taps_ref,
    bias_ref,
    head_ref,
    skip_ref,
    block_any,
    down_any,
    owned_any,
    out_ref,
    conv_ref,
    skip_grad_ref,
    head_grad_ref,
    block_out,
    down_out,
    owned_out,
    padded,
    trailing,
    scores,
    score_grad,
    columns,
    mixed_low,
    act_grad,
    size_rows,
    flow_rows,
    row_sums,
    mixed_back,
    block_ref,
    down_ref,
    owned_ref,
    stages,
    *rest,
):
    me, slot, device = seq_axis()
    block_ready_ref = staged(block_any, block_ref, stages.at[0])
    downs_ready = staged(down_any, down_ref, stages.at[1])
    owned_ready = staged(owned_any, owned_ref, stages.at[2])
    meet(ring_peers(device) + shard_peers())
    started = [[]]
    shards = shard_scatters(
        [
            (blocks_of(down_any), ready_blocks(downs_ready), down_out, rest[10 : 10 + SHARD_SCRATCH]),
            (blocks_of(owned_any), ready_blocks(owned_ready), owned_out, rest[10 + SHARD_SCRATCH :]),
        ],
        started,
    )
    send = sender(rest[8], rest[9], started[0])
    program = ring_scatter(
        block_ready(block_ready_ref, slot), slot, device, send, block_out, rest[:8], block_of(block_any, slot)
    )
    next(program)
    scores_and_columns(
        act_ref[:, INNER_HERE : INNER_HERE + STATE],
        act_ref[:, INNER_HERE + STATE :],
        cum_ref[...],
        scores,
        columns,
    )
    size_rows[...] = jnp.zeros((8, SEQ_LEN), FULL)
    flow_rows[...] = jnp.zeros((8, SEQ_LEN), FULL)
    for part in range(PAIRS):
        at = slice(part * 128, (part + 1) * 128)
        gate = proj_ref[:, at].astype(FULL)
        gate_sig = sigmoid(gate)
        grad = grad_ref[:, at].astype(FULL)
        mixed_grad = grad * (gate * gate_sig)
        out_ref[:, at] = (grad * mixed_ref[:, at] * (gate_sig * (1.0 + gate * (1.0 - gate_sig)))).astype(LOW)
        x_tile = act_ref[:, at].astype(FULL)
        skip_grad_ref[:, at] = jnp.broadcast_to(jnp.sum(mixed_grad * x_tile, axis=0, keepdims=True), (8, 128))
        mixed_low[:, at] = mixed_grad.astype(LOW)
        act_grad[:, at] = skip_ref[0:1, at] * mixed_grad
    follow("zzy", program, shards)

    def pair_step(pair):
        at = slice(pair * 128, (pair + 1) * 128)
        first = lax.broadcasted_iota(jnp.int32, (TILE, 128), 1) < HDIM
        for half in range(2):
            head = pair * 2 + half
            mine = first if half == 0 else jnp.logical_not(first)
            for low in range(TILES):
                here = slice(low * TILE, (low + 1) * TILE)
                grad = jnp.where(mine, mixed_low[here, at], jnp.zeros((TILE, 128), LOW))
                turned = mixed_low[here, at].T[half * HDIM : (half + 1) * HDIM]
                sums = jnp.zeros((TILE, 128), FULL)
                for far in range(low + 1):
                    there = slice(far * TILE, (far + 1) * TILE)
                    decay = decay_tile(columns, cum_ref, head, low, far)
                    if far == low:
                        decay = jnp.where(lower_tile(), decay, 0.0)
                    step = step_ref[pl.ds(head, 1), there]
                    scaled = dot_rhs_t(grad, act_ref[there, at]) * decay
                    product = scaled * scores[here, there]
                    size_rows[pl.ds(head, 1), there] += jnp.sum(product, axis=0, keepdims=True)
                    flow = product * step
                    for part in range(TILE // 128):
                        sums = sums + flow[:, part * 128 : (part + 1) * 128]
                    add = scaled * step
                    if half == 0 and pair == 0:
                        score_grad[here, there] = add
                    else:
                        score_grad[here, there] += add
                    weight = (scores[here, there] * decay * step).astype(LOW)
                    mixed_back[half * HDIM : (half + 1) * HDIM, there] += dot(turned, weight)
                row_sums[...] = sums
                flow_rows[pl.ds(head, 1), here] = lax.dot_general(
                    jnp.ones((8, 128), FULL),
                    row_sums[...],
                    (((1,), (1,)), ((), ())),
                    precision=HIGHEST,
                    preferred_element_type=FULL,
                )[:1]

    for pair in range(PAIRS):
        mixed_back[...] = jnp.zeros((128, SEQ_LEN), FULL)
        pair_step(pair)
        act_grad[:, pair * 128 : (pair + 1) * 128] += mixed_back[...].T
        follow(("yyz", "yz", "y")[pair], program, shards)

    b_at, c_at = INNER_HERE, INNER_HERE + STATE
    mixed_back[...] = jnp.zeros((128, SEQ_LEN), FULL)
    for low in range(TILES):
        here = slice(low * TILE, (low + 1) * TILE)
        for far in range(low + 1):
            there = slice(far * TILE, (far + 1) * TILE)
            high, rest = hi_lo(score_grad[here, there])
            b_tile, c_tile = act_ref[there, b_at:c_at], act_ref[here, c_at:]
            c_term = dot(high, b_tile) + dot(rest, b_tile)
            if far == 0:
                c_turned = c_tile.T
            mixed_back[:, there] += dot(c_turned, high) + dot(c_turned, rest)
            if far == 0:
                act_grad[here, c_at:] = c_term
            else:
                act_grad[here, c_at:] += c_term
    act_grad[:, b_at:c_at] = mixed_back[...].T

    step, size = step_ref[...], size_rows[...]
    decay_rate = head_ref[1][:, :1]
    back = scan_lanes(flow_rows[...] - step * size, True)
    rates = proj_ref[:, INNER_HERE + CONV_HERE :].astype(FULL).T[:8] + head_ref[0][:, :1]
    rate_grad = (size + back * decay_rate) * sigmoid(rates)
    real = lax.broadcasted_iota(jnp.int32, (8, SEQ_LEN), 0) < HEADS_HERE
    rate_grad = jnp.where(real, rate_grad, 0.0)
    head_grad_ref[0] = jnp.broadcast_to(jnp.sum(rate_grad, axis=1, keepdims=True), (8, 128))
    head_grad_ref[1] = jnp.broadcast_to(jnp.sum(back * step * decay_rate, axis=1, keepdims=True), (8, 128))
    turned = jnp.concatenate([rate_grad, jnp.zeros((120, SEQ_LEN), FULL)], axis=0).T
    out_ref[:, INNER_HERE + CONV_HERE :] = turned.astype(LOW)

    padded[0:8] = jnp.zeros((8, 128), FULL)
    trailing[SEQ_LEN:] = jnp.zeros((8, 128), FULL)
    for part in range(CONV_HERE // 128):
        at = slice(part * 128, (part + 1) * 128)
        wide = slice(INNER_HERE + part * 128, INNER_HERE + (part + 1) * 128)
        padded[8:] = proj_ref[:, wide].astype(FULL)
        before = bias_ref[0:1, at] + conv_taps(padded, taps_ref, at)
        gate = sigmoid(before)
        grad = act_grad[:, at] * (gate * (1.0 + before * (1.0 - gate)))
        trailing[:SEQ_LEN] = grad
        conv_ref[CONV : CONV + 1, at] = jnp.sum(grad, axis=0, keepdims=True)
        total = None
        for tap in range(CONV):
            conv_ref[tap : tap + 1, at] = jnp.sum(
                trailing[:SEQ_LEN] * padded[5 + tap : 5 + tap + SEQ_LEN], axis=0, keepdims=True
            )
            shift = CONV - 1 - tap
            term = taps_ref[tap : tap + 1, at] * trailing[shift : shift + SEQ_LEN]
            total = term if total is None else total + term
        out_ref[:, wide] = total.astype(LOW)
    conv_ref[CONV + 1 :] = jnp.zeros((3, CONV_HERE), FULL)
    take_turns(program, *shards)
    for copies in started:
        for copy in copies:
            copy.wait_send()


def mixer_backward(grad, projected, act, mixed, cum, step, taps, bias, head_cols, skip, blocks, downs, owned):
    return pl.pallas_call(
        mixer_backward_kernel,
        out_shape=(
            jax.ShapeDtypeStruct((SEQ_LEN, PROJ_HERE), LOW),
            jax.ShapeDtypeStruct((8, CONV_HERE), FULL),
            jax.ShapeDtypeStruct((8, INNER_HERE), FULL),
            jax.ShapeDtypeStruct((2, 8, 128), FULL),
            jax.ShapeDtypeStruct((PIECE, D), FULL),
            jax.ShapeDtypeStruct((32, D), FULL),
            jax.ShapeDtypeStruct((32, D), FULL),
        ),
        in_specs=[vmem_spec()] * 10 + [any_spec()] * 3,
        out_specs=(vmem_spec(),) * 7,
        scratch_shapes=[
            pltpu.VMEM((SEQ_LEN + 8, 128), FULL),
            pltpu.VMEM((SEQ_LEN + 8, 128), FULL),
            pltpu.VMEM((SEQ_LEN, SEQ_LEN), FULL),
            pltpu.VMEM((SEQ_LEN, SEQ_LEN), FULL),
            pltpu.VMEM((HEADS_HERE, SEQ_LEN, 128), FULL),
            pltpu.VMEM((SEQ_LEN, INNER_HERE), LOW),
            pltpu.VMEM((SEQ_LEN, CONV_HERE), FULL),
            pltpu.VMEM((8, SEQ_LEN), FULL),
            pltpu.VMEM((8, SEQ_LEN), FULL),
            pltpu.VMEM((TILE, 128), FULL),
            pltpu.VMEM((128, SEQ_LEN), FULL),
            pltpu.VMEM(blocks.shape, LOW),
            pltpu.VMEM(downs.shape, LOW),
            pltpu.VMEM(owned.shape, LOW),
            dma_sems(3),
        ]
        + scatter_buffers(PIECE, D)
        + [dma_sems(13), dma_sems(13)]
        + shard_scratch(downs)
        + shard_scratch(owned),
        compiler_params=pltpu.CompilerParams(
            collective_id=9, has_side_effects=True, vmem_limit_bytes=52 << 20
        ),
        cost_estimate=BUSY,
        name="mixer_backward",
    )(grad, projected, act, mixed, cum, step, taps, bias, head_cols, skip, blocks, downs, owned)


def adam_update(weight, old_first, old_second, gradient, step_rate, decay_rate):
    first_new = BETA_FIRST * old_first + (1.0 - BETA_FIRST) * gradient
    second_new = BETA_SECOND * old_second + (1.0 - BETA_SECOND) * gradient * gradient
    first_hat = first_new / (1.0 - BETA_FIRST**STEP)
    second_hat = second_new / (1.0 - BETA_SECOND**STEP)
    weight_new = weight - step_rate * (
        first_hat / (jnp.sqrt(second_hat) + ADAM_EPSILON) + decay_rate * weight
    )
    return (weight_new, first_new, second_new)


def update_kernel(dense_ref, shared_ref, aux_ref, owned_ref, up_ref, down_ref, gain_ref, *refs):
    olds = [refs[3 * index : 3 * index + 3] for index in range(9)]
    news = [refs[27 + 3 * index : 27 + 3 * index + 3] for index in range(9)]

    def step(index, gradient, rate, decay, at=()):
        old, new = olds[index], news[index]
        values = adam_update(old[0][at], old[1][at], old[2][at], gradient, rate, decay)
        for ref, value in zip(new, values):
            ref[at] = value

    rows = slice(None)
    state, rates = None, None
    place_row = lax.broadcasted_iota(jnp.int32, (128, 128), 0)
    place_col = lax.broadcasted_iota(jnp.int32, (128, 128), 1)
    for group in range(GROUPS):
        block = dense_ref[group].astype(FULL)
        for half in range(2):
            begin = half * INNER + group * INNER_HERE
            gradient = block[:, half * INNER_HERE : (half + 1) * INNER_HERE] * gain_ref[...]
            step(0, gradient, RATE_MATRIX, WEIGHT_DECAY, (rows, slice(begin, begin + INNER_HERE)))
            begin = half * FF_SH + group * SH_HERE
            gradient = shared_ref[group, :, half * SH_HERE : (half + 1) * SH_HERE].astype(FULL)
            step(1, gradient, RATE_MATRIX, WEIGHT_DECAY, (rows, slice(begin, begin + SH_HERE)))
        part = block[:, 2 * INNER_HERE : 2 * INNER_HERE + 2 * STATE]
        state = part if group == 0 else state + part
        moved = jnp.logical_and(place_row < HEADS_HERE, place_col == place_row + group * HEADS_HERE)
        part = dot(dense_ref[group, :, INNER_HERE + CONV_HERE : PROJ_HERE], moved.astype(LOW))
        rates = part if group == 0 else rates + part
    state, rates = state * gain_ref[...], rates * gain_ref[...]
    step(0, state, RATE_MATRIX, WEIGHT_DECAY, (rows, slice(2 * INNER, 2 * INNER + 2 * STATE)))
    step(0, rates[:, :HEADS], RATE_MATRIX, WEIGHT_DECAY, (rows, slice(INNER + CHANNELS, INNER + CHANNELS + HEADS)))
    step(2, owned_ref[:24], RATE_MATRIX, WEIGHT_DECAY, (slice(0, 24),))
    step(3, owned_ref[24:], RATE_MATRIX, WEIGHT_DECAY, (slice(0, 8),))

    def expert_step(index, sums, width, rate):
        def turn(count, carry):
            for row in range(8):
                at = count * 8 + row
                step(index, sums[pl.ds(at, 1), :width], rate, WEIGHT_DECAY, (at,))
            return carry

        lax.fori_loop(0, sums.shape[0] // 8, turn, 0)

    expert_step(4, up_ref, 2 * FF_EXP, RATE_MATRIX)
    expert_step(5, down_ref, D, RATE_DOWN)
    aux = aux_ref[0]
    for group in range(1, GROUPS):
        aux = aux + aux_ref[group]
    small = jnp.concatenate([aux[0:1, :89], aux[1:2, :89]], axis=1)
    step(6, small, RATE_SMALL, 0.0, (slice(0, 1),))
    step(7, aux[:, ROUTER_AT : ROUTER_AT + 12], RATE_MATRIX, WEIGHT_DECAY, (slice(0, 8),))
    step(8, aux[3:6, :HEADS], RATE_HEAD, 0.0, (slice(0, 3),))


def update(sums, triples):
    olds = [values for triple in triples for values in triple]
    news = pl.pallas_call(
        update_kernel,
        out_shape=tuple(jax.ShapeDtypeStruct(values.shape, FULL) for values in olds),
        in_specs=[vmem_spec()] * (7 + len(olds)),
        out_specs=(vmem_spec(),) * len(olds),
        compiler_params=pltpu.CompilerParams(vmem_limit_bytes=56 << 20),
        name="update",
    )(*sums, *olds)
    return [news[3 * index : 3 * index + 3] for index in range(len(triples))]


def route_combine(logit_values, onehot):
    picked = jnp.sum(logit_values[:, None, :] * onehot, axis=-1)
    route_probs = jax.nn.softmax(picked, axis=-1)
    return jnp.sum(route_probs[:, :, None] * onehot, axis=1)


def inverse_rms(values):
    return lax.rsqrt(jnp.mean(values * values, axis=-1, keepdims=True) + NORM_EPSILON)


def norm_back(values, inverse, gain, grad):
    shared = grad * gain
    inner = jnp.mean(values * shared, axis=-1, keepdims=True)
    grad_in = inverse * shared - values * (inverse * inverse * inverse * inner)
    return grad_in, jnp.sum(values * inverse * grad, axis=0)


def silu_slope(values, gate):
    return gate * (1.0 + values * (1.0 - gate))


def dot(left, right):
    return jnp.dot(left, right, preferred_element_type=FULL)


def dot_lhs_t(left, right):
    return lax.dot_general(left, right, (((0,), (0,)), ((), ())), preferred_element_type=FULL)


def dot_rhs_t(left, right):
    return lax.dot_general(left, right, (((1,), (1,)), ((), ())), preferred_element_type=FULL)


def side_rows(values):
    return jnp.pad(values, ((0, 0), (0, 7), (0, 0)))


def piece_order(forward):
    order = []
    for shard in range(SHARDS):
        for group in range(GROUPS):
            owner = shard * GROUPS + group
            user = ((shard % 2) * GROUPS + group) * GROUPS + shard // 2
            order.append((owner, user) if forward else (user, owner))
    return order


def local(
    hidden,
    cotangent,
    routes,
    head_params,
    head_first,
    head_second,
    small_params,
    small_first,
    small_second,
    proj_weight,
    proj_first,
    proj_second,
    out_weight,
    out_first,
    out_second,
    router_weight,
    router_first,
    router_second,
    experts_up,
    experts_up_first,
    experts_up_second,
    experts_down,
    experts_down_first,
    experts_down_second,
    shared_up,
    shared_up_first,
    shared_up_second,
    shared_down,
    shared_down_first,
    shared_down_second,
):
    group_index = lax.axis_index("seq")
    both = ("fsdp", "seq")
    inputs = hidden[0]
    out_grad = cotangent[0]

    proj_low = proj_weight.astype(LOW)
    misc = jnp.concatenate(
        [router_weight.astype(LOW), jnp.pad(small_params.astype(LOW), (0, 2)).reshape(12, SMALL_COLS)],
        axis=1,
    )
    columns = jnp.concatenate(
        [
            proj_low[:, :INNER].reshape(12, GROUPS, INNER_HERE),
            proj_low[:, INNER : 2 * INNER].reshape(12, GROUPS, INNER_HERE),
            jnp.broadcast_to(proj_low[:, None, 2 * INNER : INNER + CHANNELS], (12, GROUPS, 2 * STATE)),
            proj_low[:, INNER + CHANNELS :].reshape(12, GROUPS, HEADS_HERE),
            jnp.broadcast_to(misc[:, None], (12, GROUPS, 8 + SMALL_COLS)),
            jnp.zeros((12, GROUPS, 128 - HEADS_HERE - 8 - SMALL_COLS), LOW),
            shared_up.astype(LOW).reshape(12, 2, GROUPS, SH_HERE)[:, 0],
            shared_up.astype(LOW).reshape(12, 2, GROUPS, SH_HERE)[:, 1],
        ],
        axis=2,
    )
    columns = columns_out(columns.transpose(1, 0, 2)).reshape(96, -1)
    owned = jnp.concatenate([out_weight.astype(LOW), shared_down.astype(LOW)], axis=0)
    owned = lax.ppermute(owned, both, piece_order(True))

    first_inverse = inverse_rms(inputs)
    unit_rows, weights, out_here = start_gather(
        (inputs * first_inverse).astype(LOW), columns[:, :PROJ_HERE], owned[:24]
    )

    misc_at = INNER_HERE + CONV_HERE + HEADS_HERE
    misc = weights[:, misc_at : misc_at + EXPERTS + SMALL_COLS]
    router_full = misc[:, :EXPERTS]
    small_vec = (
        misc[:, EXPERTS:].reshape(SHARDS * GROUPS, 12 * SMALL_COLS)[:, :178].reshape(SMALL).astype(FULL)
    )
    gain_first, gain_second = small_vec[:D], small_vec[D : 2 * D]
    gain_mixer = lax.dynamic_slice_in_dim(small_vec, 2 * D + group_index * INNER_HERE, INNER_HERE)
    bias_all = small_vec[2 * D + INNER : 2 * D + INNER + CHANNELS]
    kernel_all = small_vec[2 * D + INNER + CHANNELS :].reshape(CONV, CHANNELS)
    conv_bias = jnp.concatenate(
        [lax.dynamic_slice_in_dim(bias_all, group_index * INNER_HERE, INNER_HERE), bias_all[INNER:]]
    )
    conv_kernel = jnp.concatenate(
        [
            lax.dynamic_slice_in_dim(kernel_all, group_index * INNER_HERE, INNER_HERE, 1),
            kernel_all[:, INNER:],
        ],
        axis=1,
    )
    head_local = lax.dynamic_slice_in_dim(head_params, group_index * HEADS_HERE, HEADS_HERE, 1)

    head_cols = jnp.stack([head_local[0], -jnp.exp(head_local[1])])
    head_cols = jnp.broadcast_to(jnp.pad(head_cols, ((0, 0), (0, 2)))[:, :, None], (2, 8, 128))
    skip_wide = jnp.repeat(head_local[2], HDIM)[None]
    projected, act, mixed, gated, out_part, square_side, cum_rows, step_rows, rows_cot, shared_here, shared_down_here = mixer_forward(
        unit_rows,
        gain_first[None],
        weights,
        out_here,
        conv_kernel,
        conv_bias[None],
        head_cols,
        gain_mixer[None],
        skip_wide,
        out_grad.astype(LOW),
        columns[:, PROJ_HERE:],
        owned[24:],
    )
    shared_here, shared_down_here = shared_here.reshape(D, 2 * SH_HERE), shared_down_here.reshape(SH_HERE, D)
    rows_cot = rows_cot.reshape(SEQ_LEN, D)
    raw_out, squares, up_here, down_here = mixed_scatter(
        out_part.reshape(GROUPS, PIECE, D),
        square_side,
        experts_up.reshape(96, 2 * FF_EXP).astype(LOW),
        experts_down.reshape(32, D).astype(LOW),
    )
    mixer_inverse = lax.rsqrt(jnp.sum(squares[:, 0], axis=0)[:, None] / INNER + NORM_EPSILON)
    middle = inputs + mixer_inverse * raw_out

    second_inverse = inverse_rms(middle)
    normed_two = (middle * second_inverse * gain_second).astype(LOW)
    logits = dot(normed_two, router_full)
    onehot = (routes[0][:, :, None] == jnp.arange(EXPERTS, dtype=jnp.int32)).astype(FULL)
    combine, route_pull = jax.vjp(lambda values: route_combine(values, onehot), logits)
    back_sum, combine_sides, block_part, up_total_grad, down_total_grad, shared_down_total_grad = experts(
        normed_two, combine.T, rows_cot.reshape(GROUPS, PIECE, D), up_here, shared_here, down_here, shared_down_here
    )

    logits_grad = route_pull(combine_sides[:, 0].T)[0].astype(LOW)
    normed_two_grad = back_sum + dot_rhs_t(logits_grad, router_full)
    router_grad = dot_lhs_t(logits_grad, normed_two)
    middle_from_norm, gain_second_grad = norm_back(middle, second_inverse, gain_second, normed_two_grad)
    middle_grad = out_grad + middle_from_norm
    mixer_grad = middle_grad.astype(LOW)
    mixer_inner = jnp.sum(mixer_grad.astype(FULL) * raw_out, axis=1, keepdims=True) / INNER
    mixer_fix = mixer_inverse * mixer_inverse * mixer_inverse * mixer_inner
    rows_mixer, stats, up_sum = middle_gather(
        mixer_grad,
        jnp.pad(jnp.concatenate([mixer_inverse, mixer_fix], axis=1).T, ((0, 6), (0, 0))),
        up_total_grad.reshape(SHARDS, 96, 2 * FF_EXP + 2 * SH_HERE),
    )

    rows_inverse = stats[:, 0].reshape(SEQ_LEN, 1)
    rows_fix = stats[:, 1].reshape(SEQ_LEN, 1)
    gated = gated.astype(FULL)
    gated_normed = (gated * rows_inverse * gain_mixer).astype(LOW)
    out_total_grad = dot_lhs_t(gated_normed, rows_mixer).astype(LOW)
    gated_normed_grad = dot_rhs_t(rows_mixer, out_here)
    gain_mixer_grad = jnp.sum(gated * rows_inverse * gated_normed_grad, axis=0)
    gated_grad = (rows_inverse * gain_mixer * gated_normed_grad - gated * rows_fix).astype(LOW)
    owned_grad = jnp.concatenate(
        [out_total_grad.reshape(SHARDS, 24, D), shared_down_total_grad.reshape(SHARDS, 8, D)], axis=1
    )

    proj_grad, conv_grads, skip_sums, head_sums, block_sum, down_sum, owned_sum = mixer_backward(
        gated_grad,
        projected,
        act,
        mixed,
        cum_rows,
        step_rows,
        conv_kernel,
        conv_bias[None],
        head_cols,
        skip_wide,
        block_part,
        down_total_grad.reshape(SHARDS, 32, D),
        owned_grad,
    )
    owned_sum = lax.ppermute(owned_sum.astype(LOW), both, piece_order(False)).astype(FULL)
    block_out = middle + block_sum
    conv_kernel_grad, conv_bias_grad = conv_grads[:CONV], conv_grads[CONV]
    skip_grad = jnp.sum(skip_sums[0].reshape(HEADS_HERE, HDIM), axis=1)
    bias_grad, log_decay_grad = head_sums[0, :HEADS_HERE, 0], head_sums[1, :HEADS_HERE, 0]
    unit_grad = dot_lhs_t(unit_rows, proj_grad)
    gain_first_grad = jnp.sum(unit_grad * weights.astype(FULL), axis=1)

    place = group_index * INNER_HERE
    kernel_wide = jnp.concatenate([jnp.zeros((CONV, INNER), FULL), conv_kernel_grad[:, INNER_HERE:]], axis=1)
    kernel_wide = lax.dynamic_update_slice_in_dim(kernel_wide, conv_kernel_grad[:, :INNER_HERE], place, 1)
    bias_wide = jnp.concatenate([jnp.zeros((INNER,), FULL), conv_bias_grad[INNER_HERE:]])
    bias_wide = lax.dynamic_update_slice_in_dim(bias_wide, conv_bias_grad[:INNER_HERE], place, 0)
    gain_wide = lax.dynamic_update_slice_in_dim(jnp.zeros((INNER,), FULL), gain_mixer_grad, place, 0)
    small_grad = jnp.concatenate(
        [gain_first_grad, gain_second_grad, gain_wide, bias_wide, kernel_wide.reshape(-1)]
    )
    small_grad = jnp.pad(small_grad.reshape(SHARDS * GROUPS, 2, 89), ((0, 0), (0, 6), (0, 39)))
    router_rows = router_grad.reshape(EXPERTS, SHARDS * GROUPS, 12).transpose(1, 0, 2)
    small_grad = (small_grad + jnp.pad(router_rows, ((0, 0), (0, 0), (ROUTER_AT, 116 - ROUTER_AT)))).astype(LOW)
    head_grad = jnp.stack([bias_grad, log_decay_grad, skip_grad])
    head_rows = lax.dynamic_update_slice_in_dim(
        jnp.zeros((3, 128), FULL), head_grad, group_index * HEADS_HERE, 1
    )
    head_rows = jnp.pad(jnp.concatenate(hi_lo(head_rows)), ((0, 2), (0, 0)))
    aux_grad = jnp.concatenate(
        [
            small_grad.reshape(SHARDS, 64, 128),
            jnp.broadcast_to(jnp.pad(head_rows, ((0, 24), (0, 0))), (SHARDS, 32, 128)),
        ],
        axis=1,
    )
    normed_grad, column_sum, aux_sum = last_scatter(
        proj_grad, weights, unit_grad.astype(LOW).reshape(SHARDS, 96, PROJ_HERE), aux_grad
    )
    input_from_norm, unused = norm_back(inputs, first_inverse, gain_first, normed_grad)
    hidden_grad = middle_grad + input_from_norm

    shared_back = up_sum[:, 2 * FF_EXP :].astype(LOW).reshape(GROUPS, 12, 2 * SH_HERE)
    head_side = jnp.pad(aux_sum[64:67] + aux_sum[67:70], ((3, 2), (0, 0)))
    aux_side = aux_sum[:64].reshape(GROUPS, 8, 128) + head_side
    dense, shared_back, aux_back = columns_back(
        column_sum.astype(LOW).reshape(GROUPS, 12, PROJ_HERE), shared_back, aux_side
    )
    owner = lax.axis_index("fsdp") * GROUPS + group_index
    own_gain = lax.dynamic_slice_in_dim(gain_first, owner * 12, 12)[:, None]
    small_rows = [values[None] for values in (small_params, small_first, small_second)]
    router_rows = [values.T for values in (router_weight, router_first, router_second)]
    news = update(
        (dense, shared_back, aux_back, owned_sum, up_sum, down_sum, own_gain),
        (
            (proj_weight, proj_first, proj_second),
            (shared_up, shared_up_first, shared_up_second),
            (out_weight, out_first, out_second),
            (shared_down, shared_down_first, shared_down_second),
            (experts_up, experts_up_first, experts_up_second),
            (experts_down, experts_down_first, experts_down_second),
            small_rows,
            router_rows,
            (head_params, head_first, head_second),
        ),
    )
    proj_new, shared_up_new, out_new, shared_down_new, up_new, down_new, small_new, router_new, head_new = news
    small_new = [values[0] for values in small_new]
    router_new = [values.T for values in router_new]
    return (
        block_out[None],
        hidden_grad[None],
        *head_new,
        *small_new,
        *proj_new,
        *out_new,
        *router_new,
        *up_new,
        *down_new,
        *shared_up_new,
        *shared_down_new,
    )


def solution(mesh):
    return jax.shard_map(
        local,
        mesh=mesh,
        in_specs=(
            P("fsdp", "seq", None),
            P("fsdp", "seq", None),
            P("fsdp", "seq", None),
            P(),
            P(),
            P(),
            P(("fsdp", "seq")),
            P(("fsdp", "seq")),
            P(("fsdp", "seq")),
            P(("fsdp", "seq"), None),
            P(("fsdp", "seq"), None),
            P(("fsdp", "seq"), None),
            P(("fsdp", "seq"), None),
            P(("fsdp", "seq"), None),
            P(("fsdp", "seq"), None),
            P(("fsdp", "seq"), None),
            P(("fsdp", "seq"), None),
            P(("fsdp", "seq"), None),
            P("fsdp", "seq", None),
            P("fsdp", "seq", None),
            P("fsdp", "seq", None),
            P("fsdp", "seq", None),
            P("fsdp", "seq", None),
            P("fsdp", "seq", None),
            P(("fsdp", "seq"), None),
            P(("fsdp", "seq"), None),
            P(("fsdp", "seq"), None),
            P(("fsdp", "seq"), None),
            P(("fsdp", "seq"), None),
            P(("fsdp", "seq"), None),
        ),
        out_specs=(
            P("fsdp", "seq", None),
            P("fsdp", "seq", None),
            P(),
            P(),
            P(),
            P(("fsdp", "seq")),
            P(("fsdp", "seq")),
            P(("fsdp", "seq")),
            P(("fsdp", "seq"), None),
            P(("fsdp", "seq"), None),
            P(("fsdp", "seq"), None),
            P(("fsdp", "seq"), None),
            P(("fsdp", "seq"), None),
            P(("fsdp", "seq"), None),
            P(("fsdp", "seq"), None),
            P(("fsdp", "seq"), None),
            P(("fsdp", "seq"), None),
            P("fsdp", "seq", None),
            P("fsdp", "seq", None),
            P("fsdp", "seq", None),
            P("fsdp", "seq", None),
            P("fsdp", "seq", None),
            P("fsdp", "seq", None),
            P(("fsdp", "seq"), None),
            P(("fsdp", "seq"), None),
            P(("fsdp", "seq"), None),
            P(("fsdp", "seq"), None),
            P(("fsdp", "seq"), None),
            P(("fsdp", "seq"), None),
        ),
        check_vma=False,
    )
```

```python
import functools

import jax
import jax.numpy as jnp
from jax import lax
from jax.experimental import pallas as pl
from jax.experimental.pallas import tpu as pltpu
from jax.sharding import PartitionSpec as P

D = 1536
HEADS = 48
HDIM = 64
STATE = 128
CONV = 4
FF_EXP = 512
FF_SH = 1024
TOPK = 6
EXPERTS = 8
STEP = 5
INNER = 3072
CHANNELS = 3328
SMALL = 22784
GROUPS = 8
SHARDS = 16
HEADS_HERE = HEADS // GROUPS
INNER_HERE = INNER // GROUPS
SH_HERE = FF_SH // GROUPS
SEQ_LEN = 1024
PIECE = SEQ_LEN // GROUPS
CONV_HERE = INNER_HERE + 2 * STATE
PROJ_HERE = INNER_HERE + CONV_HERE + 128
SMALL_COLS = 15
ROUTER_AT = 100


NORM_EPSILON = 1e-05
BETA_FIRST = 0.9
BETA_SECOND = 0.95
ADAM_EPSILON = 1e-08
RATE_MATRIX = 0.04
RATE_DOWN = 0.1
RATE_SMALL = 0.3
RATE_HEAD = 1.0
WEIGHT_DECAY = 0.1
HIGHEST = lax.Precision.HIGHEST
LOW = jnp.bfloat16
FULL = jnp.float32
MESH = pl.DeviceIdType.MESH


def hi_lo(values):
    high = values.astype(LOW)
    return high, (values - high.astype(FULL)).astype(LOW)


BUSY = pl.CostEstimate(flops=30_000_000_000, bytes_accessed=4_000_000, transcendentals=0)


def seq_axis():
    me = lax.axis_index("seq")
    side, level = lax.rem(me, 2), lax.div(me, 2)

    def slot(up, other):
        return lax.rem(level + up + 4, 4) * 2 + (1 - side if other else side)

    return me, slot, lambda up, other: {"seq": slot(up, other)}


def fsdp_axis():
    me = lax.axis_index("fsdp")
    core, rest = lax.rem(me, 2), lax.div(me, 2)
    side, level = lax.rem(rest, 2), lax.div(rest, 2)

    def slot(up, other):
        return lax.rem(level + up + 4, 4) * 2 + (1 - side if other else side)

    return core, slot, lambda up, other: {"fsdp": slot(up, other) * 2 + core}, {"fsdp": rest * 2 + 1 - core}


def meet(devices):
    barrier = pltpu.get_barrier_semaphore()
    for device in devices:
        pl.semaphore_signal(barrier, inc=1, device_id=device, device_id_type=MESH)
    pl.semaphore_wait(barrier, len(devices))


def ring_peers(device):
    return [device(0, True), device(1, False), device(-1, False)]


def sender(send_sem, recv_sem, started):
    def send(source, target, device):
        index = len(started)
        copy = pltpu.make_async_remote_copy(
            src_ref=source,
            dst_ref=target,
            send_sem=send_sem.at[index],
            recv_sem=recv_sem.at[index],
            device_id=device,
            device_id_type=MESH,
        )
        copy.start()
        started.append(copy)
        return copy

    return send


def take_turns(*programs):
    waiting = list(programs)
    while waiting:
        for program in list(waiting):
            if next(program, None) is None:
                waiting.remove(program)


def follow(order, ring, shards):
    for which in order:
        for program in [ring] if which == "z" else shards:
            next(program, None)


def ring_gather(source, place, slot, device, send, arrived, split=True):
    rows = source.shape[0]
    halves = ((pl.ds(0, rows // 2),), (pl.ds(rows // 2, rows // 2),)) if split else ((), None)
    own = place(slot(0, False), ())
    to_side = send(source, own, device(0, True))
    up = send(source, own, device(1, False))
    down = send(source, own, device(-1, False))
    arrived(source, own)
    yield True
    far, two = [], []

    def pass_on(copy, up, other, index):
        copy.wait_recv()
        if halves[index] is not None:
            part = place(slot(-up, other), halves[index])
            far.append(send(part, part, device(up, False)))
        block = place(slot(-up, other), ())
        arrived(block, block)

    def far_here(index, other):
        if halves[index % 2] is not None:
            far.pop(0).wait_recv()
            part = place(slot(2, other), halves[index % 2])
            arrived(part, part)

    pass_on(up, 1, False, 0)
    yield True
    pass_on(down, -1, False, 1)
    yield True
    to_side.wait_recv()
    block = place(slot(0, True), ())
    two.append(send(block, block, device(1, False)))
    two.append(send(block, block, device(-1, False)))
    arrived(block, block)
    yield True
    for index in range(2):
        far_here(index, False)
        yield True
    pass_on(two[0], 1, True, 0)
    yield True
    pass_on(two[1], -1, True, 1)
    yield True
    for index in range(2):
        far_here(index, True)
        yield True


def nothing(source, target):
    return None


def side_start(side_ref, side_out, per_peer, send_sem, recv_sem, local_sem):
    me = lax.axis_index("seq")
    copies = []
    for step in range(1, GROUPS):
        other = lax.rem(me + step, GROUPS)
        copy = pltpu.make_async_remote_copy(
            src_ref=side_ref.at[other] if per_peer else side_ref,
            dst_ref=side_out.at[me],
            send_sem=send_sem.at[step],
            recv_sem=recv_sem.at[step],
            device_id={"seq": other},
            device_id_type=MESH,
        )
        copy.start()
        copies.append(copy)
    keep = pltpu.make_async_copy(side_ref.at[me] if per_peer else side_ref, side_out.at[me], local_sem)
    keep.start()
    return copies, keep


def side_end(copies, keep):
    for copy in copies:
        copy.wait_recv()
    for copy in copies:
        copy.wait_send()
    keep.wait()


def all_peers():
    me = lax.axis_index("seq")
    return [{"seq": lax.rem(me + step, GROUPS)} for step in range(1, GROUPS)]


def gather_kernel(x_ref, side_ref, out_ref, side_out, send_sem, recv_sem, local_sem, s_send, s_recv, s_local):
    me, slot, device = seq_axis()
    meet(all_peers())
    started = []
    send = sender(send_sem, recv_sem, started)
    program = ring_gather(x_ref, lambda at, cut: out_ref.at[(at, *cut)], slot, device, send, nothing)
    next(program)
    sides = side_start(side_ref, side_out, False, s_send, s_recv, s_local)
    keep = pltpu.make_async_copy(x_ref, out_ref.at[me], local_sem)
    keep.start()
    take_turns(program)
    side_end(*sides)
    for copy in started:
        copy.wait_send()
    keep.wait()


def any_spec():
    return pl.BlockSpec(memory_space=pl.ANY)


def vmem_spec():
    return pl.BlockSpec(memory_space=pltpu.VMEM)


def dma_sems(count):
    return pltpu.SemaphoreType.DMA((count,))


def seq_gather(piece, side, name, collective_id):
    rows, width = piece.shape
    gathered, sides = pl.pallas_call(
        gather_kernel,
        out_shape=(
            jax.ShapeDtypeStruct((GROUPS, rows, width), piece.dtype),
            jax.ShapeDtypeStruct((GROUPS, 8, 128), FULL),
        ),
        in_specs=[any_spec()] * 2,
        out_specs=(any_spec(), any_spec()),
        scratch_shapes=[
            dma_sems(9),
            dma_sems(9),
            pltpu.SemaphoreType.DMA,
            dma_sems(GROUPS),
            dma_sems(GROUPS),
            pltpu.SemaphoreType.DMA,
        ],
        compiler_params=pltpu.CompilerParams(collective_id=collective_id, has_side_effects=True),
        cost_estimate=BUSY,
        name=name,
    )(piece, side)
    return gathered.reshape(GROUPS * rows, width), sides


def shard_gather(source, target, send_sem, recv_sem, started, crossing, split=True):
    core, slot, device, twin = fsdp_axis()
    send = sender(send_sem, recv_sem, started)

    def place(at, cut):
        return target.at[(at * 2 + core, *cut)]

    def arrived(origin, block):
        crossing.append(send(origin, block, twin))

    return ring_gather(source, place, slot, device, send, arrived, split)


START_COUNT = 2


def start_kernel(x_ref, *rest):
    sources, x_out, targets = rest[:START_COUNT], rest[START_COUNT], rest[START_COUNT + 1 : 2 * START_COUNT + 1]
    x_send, x_recv, keeps, *sems = rest[2 * START_COUNT + 1 :]
    me, slot, device = seq_axis()
    core, f_slot, f_device, twin = fsdp_axis()
    meet(ring_peers(device) + ring_peers(f_device) + [twin])
    mine = f_slot(0, False) * 2 + core
    x_started, started, crossing, kept = [], [], [], []
    x_sender = sender(x_send, x_recv, x_started)
    program = ring_gather(x_ref, lambda at, cut: x_out.at[(at, *cut)], slot, device, x_sender, nothing)
    shards = []
    for index, (source, target) in enumerate(zip(sources, targets)):
        copies = []
        started.append(copies)
        shards.append(
            shard_gather(
                source, target, sems[2 * index], sems[2 * index + 1], copies, crossing, source.shape[0] % 32 == 0
            )
        )
        keep = pltpu.make_async_copy(source, target.at[mine], keeps.at[index])
        keep.start()
        kept.append(keep)
    keep = pltpu.make_async_copy(x_ref, x_out.at[me], keeps.at[START_COUNT])
    keep.start()
    kept.append(keep)
    follow("yzyyyzzyyzyyyyzzzzzz", program, shards)
    take_turns(program, *shards)
    for copy in crossing:
        copy.wait_recv()
    for copies in (x_started, *started):
        for copy in copies:
            copy.wait_send()
    for keep in kept:
        keep.wait()


def start_gather(piece, *shards):
    rows, width = piece.shape
    out = pl.pallas_call(
        start_kernel,
        out_shape=(jax.ShapeDtypeStruct((GROUPS, rows, width), LOW),)
        + tuple(jax.ShapeDtypeStruct((SHARDS, *shard.shape), LOW) for shard in shards),
        in_specs=[any_spec()] * (1 + START_COUNT),
        out_specs=(any_spec(),) * (1 + START_COUNT),
        scratch_shapes=[dma_sems(9)] * 2 + [dma_sems(START_COUNT + 1)] + [dma_sems(19)] * (2 * START_COUNT),
        compiler_params=pltpu.CompilerParams(collective_id=2, has_side_effects=True),
        cost_estimate=BUSY,
        name="rows_first",
    )(piece, *shards)
    return [out[0].reshape(GROUPS * rows, width)] + [
        full.reshape(SHARDS * shard.shape[0], -1) for full, shard in zip(out[1:], shards)
    ]


def staged(source, target, sem):
    copies = [pltpu.make_async_copy(source, target, sem)]
    copies[0].start()

    def ready():
        if copies:
            copies.pop().wait()
        return target

    return ready


def ring_scatter(block, slot, device, send, result, buffers, raw=None, near_first=False):
    raw = raw or block
    in_low, in_high, sum_up, sum_down, land_low, land_high, part_out, part_in = buffers
    rows = part_out.shape[0]
    half = rows // 2
    first, second = pl.ds(0, half), pl.ds(half, half)
    everything = pl.ds(0, rows)
    landing = {}

    def begin_far(turn, other):
        far = raw(2, other)
        return [
            send(far(first), in_low.at[turn], device(1, False)),
            send(far(second), in_high.at[turn], device(-1, False)),
        ]

    def begin_near(turn, other):
        landing[turn] = [
            send(raw(1, other)(second), land_low.at[turn, second], device(1, False)),
            send(raw(-1, other)(first), land_high.at[turn, first], device(-1, False)),
        ]

    def begin(turn, other):
        copies = begin_far(turn, other)
        begin_near(turn, other)
        return copies

    def middle(turn, other, copies):
        copies[0].wait_recv()
        sum_up[turn] = (in_low[turn].astype(FULL) + block(1, other)(first)[...].astype(FULL)).astype(LOW)
        landing[turn].append(send(sum_up.at[turn], land_low.at[turn, first], device(1, False)))
        copies[1].wait_recv()
        sum_down[turn] = (in_high[turn].astype(FULL) + block(-1, other)(second)[...].astype(FULL)).astype(LOW)
        landing[turn].append(send(sum_down.at[turn], land_high.at[turn, second], device(-1, False)))

    def total(turn, other):
        for copy in landing[turn]:
            copy.wait_recv()
        return (
            block(0, other)(everything)[...].astype(FULL)
            + land_low[turn].astype(FULL)
            + land_high[turn].astype(FULL)
        )

    if near_first:
        begin_near(0, True)
        yield True
        copies = begin_far(0, True)
    else:
        copies = begin(0, True)
    yield True
    middle(0, True, copies)
    yield True
    copies = begin(1, False)
    yield True
    part_out[...] = total(0, True).astype(LOW)
    to_side = send(part_out, part_in, device(0, True))
    yield True
    middle(1, False, copies)
    yield True
    result[...] = total(1, False)
    yield True
    to_side.wait_recv()
    result[...] += part_in[...].astype(FULL)


def scatter_buffers(rows, width):
    half = rows // 2
    return (
        [pltpu.VMEM((2, half, width), LOW)] * 4
        + [pltpu.VMEM((2, rows, width), LOW)] * 2
        + [pltpu.VMEM((rows, width), LOW)] * 2
    )


def block_of(x_ref, slot):
    def block(up, other):
        return lambda cut: x_ref.at[slot(up, other), cut]

    return block


def block_ready(ready, slot):
    def block(up, other):
        return lambda cut: ready().at[slot(up, other), cut]

    return block


def mixed_kernel(x_ref, side_ref, u_ref, d_ref, out_ref, side_out, u_out, d_out, *rest):
    buffers, (send_sem, recv_sem, s_send, s_recv, s_local) = rest[:8], rest[8:13]
    u_send, u_recv, d_send, d_recv, keeps, x_vmem, x_sem = rest[13:]
    me, slot, device = seq_axis()
    core, f_slot, f_device, twin = fsdp_axis()
    x_ready = staged(x_ref, x_vmem, x_sem)
    meet(all_peers() + ring_peers(f_device) + [twin])
    started, u_started, d_started, crossing = [], [], [], []
    send = sender(send_sem, recv_sem, started)
    program = ring_scatter(
        block_ready(x_ready, slot), slot, device, send, out_ref, buffers, block_of(x_ref, slot)
    )
    next(program)
    sides = side_start(side_ref, side_out, True, s_send, s_recv, s_local)
    mine = f_slot(0, False) * 2 + core
    kept = []
    for index, (source, block) in enumerate(((u_ref, u_out.at[mine]), (d_ref, d_out.at[mine]))):
        keep = pltpu.make_async_copy(source, block, keeps.at[index])
        keep.start()
        kept.append(keep)
    shards = [
        shard_gather(u_ref, u_out, u_send, u_recv, u_started, crossing),
        shard_gather(d_ref, d_out, d_send, d_recv, d_started, crossing),
    ]
    follow("yzyyzyyyzyyzyyzz", program, shards)
    take_turns(program, *shards)
    side_end(*sides)
    for copy in crossing:
        copy.wait_recv()
    for copy in started + u_started + d_started:
        copy.wait_send()
    for keep in kept:
        keep.wait()


def mixed_scatter(parts, side, up_piece, down_piece):
    groups, rows, width = parts.shape
    summed, sides, up_all, down_all = pl.pallas_call(
        mixed_kernel,
        out_shape=(
            jax.ShapeDtypeStruct((rows, width), FULL),
            jax.ShapeDtypeStruct((GROUPS, 8, 128), FULL),
            jax.ShapeDtypeStruct((SHARDS, *up_piece.shape), LOW),
            jax.ShapeDtypeStruct((SHARDS, *down_piece.shape), LOW),
        ),
        in_specs=[any_spec(), vmem_spec(), any_spec(), any_spec()],
        out_specs=(vmem_spec(), vmem_spec(), any_spec(), any_spec()),
        scratch_shapes=scatter_buffers(rows, width)
        + [dma_sems(13), dma_sems(13), dma_sems(GROUPS), dma_sems(GROUPS), pltpu.SemaphoreType.DMA]
        + [dma_sems(19)] * 4
        + [dma_sems(2), pltpu.VMEM(parts.shape, LOW), pltpu.SemaphoreType.DMA],
        compiler_params=pltpu.CompilerParams(
            collective_id=4, has_side_effects=True, vmem_limit_bytes=52 << 20
        ),
        cost_estimate=BUSY,
        name="mixer_out",
    )(parts, side, up_piece, down_piece)
    return summed, sides, up_all.reshape(-1, up_piece.shape[1]), down_all.reshape(-1, down_piece.shape[1])


def shard_scratch(grads):
    depth, columns = grads.shape[1:]
    return (
        scatter_buffers(depth, columns)
        + [pltpu.VMEM((GROUPS, depth, columns), LOW)]
        + [dma_sems(13), dma_sems(13), dma_sems(8), dma_sems(8)]
    )


SHARD_SCRATCH = 13


def shard_scatters(arrays, started):
    core, slot, device, twin = fsdp_axis()
    order = [(2, True), (1, True), (-1, True), (2, False), (1, False), (-1, False), (0, True), (0, False)]
    programs, senders = [], []
    for pick, value, target, scratch in arrays:
        buffers, (core_in, send_sem, recv_sem, c_send, c_recv) = scratch[:8], scratch[8:]
        crossing, copies, arriving = [], [], {}
        started.extend([crossing, copies])
        senders.append((pick, core_in, sender(c_send, c_recv, crossing), arriving))

        def block(up, other, value=value, core_in=core_in, arriving=arriving):
            at = slot(up, other)
            if (up, other) in arriving:
                arriving.pop((up, other)).wait_recv()
                core_in[at] = (core_in[at].astype(FULL) + value(at * 2 + core)[...].astype(FULL)).astype(LOW)
            return lambda cut: core_in.at[at, cut]

        programs.append(ring_scatter(block, slot, device, sender(send_sem, recv_sem, copies), target, buffers))
    for key in order:
        for pick, core_in, send_core, arriving in senders:
            at = slot(*key)
            arriving[key] = send_core(pick(at * 2 + 1 - core), core_in.at[at], twin)
    return programs


def blocks_of(ref):
    return lambda at: ref.at[at]


def ready_blocks(ready):
    return lambda at: ready().at[at]


def shard_peers():
    core, slot, device, twin = fsdp_axis()
    return ring_peers(device) + [twin]


def last_kernel(g_any, p_any, w_any, a_ref, x_out, w_out, a_out, x_ref, w_ref, g_ref, p_ref, stages, *rest):
    x_buffers, (x_send, x_recv) = rest[:8], rest[8:10]
    me, slot, device = seq_axis()
    g_ready = staged(g_any, g_ref, stages.at[0])
    p_ready = staged(p_any, p_ref, stages.at[1])
    w_ready = staged(w_any, w_ref, stages.at[2])
    done = set()

    def part_of(up, other):
        at = slot(up, other)
        if (up, other) not in done:
            done.add((up, other))
            here = pl.ds(pl.multiple_of(at * PIECE, PIECE), PIECE)
            g_ready(), p_ready()
            for part in range(D // 512):
                cols = slice(part * 512, (part + 1) * 512)
                x_ref[at, :, cols] = dot_rhs_t(g_ref[here, :], p_ref[cols, :]).astype(LOW)
        return lambda cut: x_ref.at[at, cut]

    meet(ring_peers(device) + shard_peers())
    x_started, started = [], []
    program = ring_scatter(part_of, slot, device, sender(x_send, x_recv, x_started), x_out, x_buffers)
    main, small = shard_scatters(
        [
            (blocks_of(w_any), ready_blocks(w_ready), w_out, rest[10 : 10 + SHARD_SCRATCH]),
            (blocks_of(a_ref), blocks_of(a_ref), a_out, rest[10 + SHARD_SCRATCH :]),
        ],
        started,
    )
    follow("zyzyzyyzyzyzyz", program, [main, small])
    take_turns(program, main, small)
    for copies in (x_started, *started):
        for copy in copies:
            copy.wait_send()


def last_scatter(proj_grad, weights, grads, small):
    rows, width = PIECE, D
    return pl.pallas_call(
        last_kernel,
        out_shape=(
            jax.ShapeDtypeStruct((rows, width), FULL),
            jax.ShapeDtypeStruct(grads.shape[1:], FULL),
            jax.ShapeDtypeStruct(small.shape[1:], FULL),
        ),
        in_specs=[any_spec(), any_spec(), any_spec(), vmem_spec()],
        out_specs=(vmem_spec(),) * 3,
        scratch_shapes=[
            pltpu.VMEM((GROUPS, rows, width), LOW),
            pltpu.VMEM(grads.shape, LOW),
            pltpu.VMEM(proj_grad.shape, LOW),
            pltpu.VMEM(weights.shape, LOW),
            dma_sems(3),
        ]
        + scatter_buffers(rows, width)
        + [dma_sems(13), dma_sems(13)]
        + shard_scratch(grads)
        + shard_scratch(small),
        compiler_params=pltpu.CompilerParams(
            collective_id=8, has_side_effects=True, vmem_limit_bytes=52 << 20
        ),
        cost_estimate=BUSY,
        name="rows_last",
    )(proj_grad, weights, grads, small)


def middle_kernel(x_ref, side_ref, u_ref, x_out, side_out, u_out, *rest):
    x_send, x_recv, x_local, s_send, s_recv, s_local = rest[:6]
    me, slot, device = seq_axis()
    meet(all_peers() + shard_peers())
    x_started, started = [], []
    send = sender(x_send, x_recv, x_started)
    program = ring_gather(x_ref, lambda at, cut: x_out.at[(at, *cut)], slot, device, send, nothing)
    next(program)
    [shard] = shard_scatters([(blocks_of(u_ref), blocks_of(u_ref), u_out, rest[6:])], started)
    sides = side_start(side_ref, side_out, False, s_send, s_recv, s_local)
    keep = pltpu.make_async_copy(x_ref, x_out.at[me], x_local)
    keep.start()
    follow("yyyzzyzyzzyyzzzz", program, [shard])
    take_turns(program, shard)
    side_end(*sides)
    for copies in (x_started, *started):
        for copy in copies:
            copy.wait_send()
    keep.wait()


def middle_gather(piece, side, up_grads):
    rows, width = piece.shape
    gathered, sides, up_sum = pl.pallas_call(
        middle_kernel,
        out_shape=(
            jax.ShapeDtypeStruct((GROUPS, rows, width), piece.dtype),
            jax.ShapeDtypeStruct((GROUPS, 8, 128), FULL),
            jax.ShapeDtypeStruct(up_grads.shape[1:], FULL),
        ),
        in_specs=[any_spec(), any_spec(), vmem_spec()],
        out_specs=(any_spec(), any_spec(), vmem_spec()),
        scratch_shapes=[
            dma_sems(9),
            dma_sems(9),
            pltpu.SemaphoreType.DMA,
            dma_sems(GROUPS),
            dma_sems(GROUPS),
            pltpu.SemaphoreType.DMA,
        ]
        + shard_scratch(up_grads),
        compiler_params=pltpu.CompilerParams(
            collective_id=7, has_side_effects=True, vmem_limit_bytes=52 << 20
        ),
        cost_estimate=BUSY,
        name="rows_mixer",
    )(piece, side, up_grads)
    return gathered.reshape(GROUPS * rows, width), sides, up_sum


UNITS = FF_EXP + SH_HERE
HIDDEN_COLS = 2 * UNITS


def experts_kernel(
    x_ref,
    side_ref,
    cot_any,
    up_any,
    shared_any,
    down_any,
    shared_down_any,
    back_out,
    side_back,
    block_any,
    up_grad_any,
    down_grad_any,
    shared_grad_any,
    cot_ref,
    up_ref,
    shared_ref,
    down_ref,
    shared_down_ref,
    block_ref,
    up_grad_ref,
    down_grad_ref,
    shared_grad_ref,
    rows_ref,
    sides_in,
    parts_ref,
    gu_ref,
    act_ref,
    side_send,
    *rest,
):
    buffers, rest = rest[:8], rest[8:]
    g_send, g_recv, g_local, s_send, s_recv, s_local, r_send, r_recv, b_send, b_recv, b_local, moves = rest
    me, slot, device = seq_axis()
    moving = []

    def move(source, target):
        copy = pltpu.make_async_copy(source, target, moves.at[len(moving)])
        copy.start()
        moving.append(copy)

    for source, target in (
        (up_any, up_ref),
        (down_any, down_ref),
        (cot_any, cot_ref),
        (shared_any, shared_ref),
        (shared_down_any, shared_down_ref),
    ):
        move(source, target)
    meet(all_peers())
    started = []
    gather = ring_gather(
        x_ref, lambda at, cut: rows_ref.at[(at, *cut)], slot, device, sender(g_send, g_recv, started), nothing
    )
    next(gather)
    sides = side_start(side_ref, sides_in, False, s_send, s_recv, s_local)
    keep = pltpu.make_async_copy(x_ref, rows_ref.at[me], g_local)
    keep.start()
    keep.wait()
    for copy in moving:
        copy.wait()
    side_end(*sides)

    def unit_step(hidden, cot, weights, downs, width, gu_at, half, scale):
        gate = dot(hidden, weights[:, gu_at : gu_at + width])
        lift = dot(hidden, weights[:, gu_at + half : gu_at + half + width])
        back = dot_rhs_t(cot, downs)
        gate_sig = sigmoid(gate)
        gate_silu = gate * gate_sig
        act = (gate_silu * lift).astype(LOW).astype(FULL)
        product = back * act
        if scale is not None:
            scale = jnp.concatenate([scale] * (width // 128), axis=1)
            act = act * scale
            back = back * scale
        gate_grad = back * lift * (gate_sig * (1.0 + gate * (1.0 - gate_sig)))
        return product, act.astype(LOW), gate_grad.astype(LOW), (back * gate_silu).astype(LOW)

    def joined(blocks):
        return blocks[0] if len(blocks) == 1 else jnp.concatenate(blocks, axis=0)

    def process(*keys):
        slots = [slot(*key) for key in keys]
        rows = [pl.ds(pl.multiple_of(at * PIECE, PIECE), PIECE) for at in slots]

        def put(ref, cols, values):
            for index, here in enumerate(rows):
                ref[here, cols] = values[index * PIECE : (index + 1) * PIECE]

        hidden = joined([rows_ref[at] for at in slots])
        cot = joined([cot_ref[at] for at in slots])
        scale = joined([jnp.broadcast_to(sides_in[at, pl.ds(me, 1), :], (128, 128)).T for at in slots])
        folded = None
        for begin in range(0, FF_EXP, 256):
            cols = slice(begin, begin + 256)
            product, act, gate_grad, lift_grad = unit_step(
                hidden, cot, up_ref, down_ref[cols, :], 256, begin, FF_EXP, scale
            )
            put(act_ref, cols, act)
            put(gu_ref, cols, gate_grad)
            put(gu_ref, slice(FF_EXP + begin, FF_EXP + begin + 256), lift_grad)
            product = product[:, :128] + product[:, 128:]
            folded = product if folded is None else folded + product
        unused, act, gate_grad, lift_grad = unit_step(
            hidden, cot, shared_ref, shared_down_ref[...], SH_HERE, 0, SH_HERE, None
        )
        put(act_ref, slice(FF_EXP, UNITS), act)
        put(gu_ref, slice(2 * FF_EXP, 2 * FF_EXP + SH_HERE), gate_grad)
        put(gu_ref, slice(2 * FF_EXP + SH_HERE, HIDDEN_COLS), lift_grad)
        sums = lax.dot_general(
            jnp.ones((8, 128), FULL),
            folded,
            (((1,), (1,)), ((), ())),
            precision=HIGHEST,
            preferred_element_type=FULL,
        )
        for index, at in enumerate(slots):
            side_send[at] = sums[:, index * PIECE : (index + 1) * PIECE]
        grads = joined([gu_ref[here, :] for here in rows])
        for begin in range(0, D, 512):
            cols = slice(begin, begin + 512)
            total = dot_rhs_t(grads[:, : 2 * FF_EXP], up_ref[cols, :])
            total = (total + dot_rhs_t(grads[:, 2 * FF_EXP :], shared_ref[cols, :])).astype(LOW)
            for index, at in enumerate(slots):
                parts_ref[at, :, cols] = total[index * PIECE : (index + 1) * PIECE]

    summed = []
    process((0, False))
    next(gather)
    next(gather)
    process((-1, False), (1, False))
    next(gather)
    next(gather)
    next(gather)
    process((0, True), (2, False))
    next(gather)
    next(gather)
    process((-1, True), (1, True))
    scatter = ring_scatter(
        block_of(parts_ref, slot),
        slot,
        device,
        sender(r_send, r_recv, summed),
        back_out,
        buffers,
        near_first=True,
    )
    next(scatter)
    take_turns(gather)
    process((2, True))

    next(scatter)
    backs = side_start(side_send, side_back, True, b_send, b_recv, b_local)

    def block_step(at, carry):
        rows = pl.ds(pl.multiple_of(at * PIECE, PIECE), PIECE)
        for begin in range(0, D, 512):
            cols = slice(begin, begin + 512)
            total = dot(act_ref[rows, :FF_EXP], down_ref[:, cols])
            total = total + dot(act_ref[rows, FF_EXP:], shared_down_ref[:, cols])
            block_ref[at, :, cols] = total.astype(LOW)
        return carry

    def up_step(part, carry):
        rows = pl.ds(pl.multiple_of(part * 256, 256), 256)
        left = rows_ref[:, :, rows].reshape(SEQ_LEN, 256).T
        for begin in range(0, HIDDEN_COLS, 640):
            cols = slice(begin, begin + 640)
            up_grad_ref[rows, cols] = dot(left, gu_ref[:, cols]).astype(LOW)
        return carry

    lax.fori_loop(0, 4, block_step, 0)
    next(scatter)
    next(scatter)
    lax.fori_loop(4, 8, block_step, 0)
    moving.clear()
    move(block_ref, block_any)
    next(scatter)
    lax.fori_loop(0, 3, up_step, 0)
    next(scatter)
    lax.fori_loop(3, 6, up_step, 0)
    move(up_grad_ref, up_grad_any)
    next(scatter)
    for row in range(0, UNITS, 128):
        left = act_ref[:, row : row + 128].T
        for begin in range(0, D, 512):
            cols = slice(begin, begin + 512)
            grads = dot(left, cot_ref[:, :, cols].reshape(SEQ_LEN, 512)).astype(LOW)
            if row < FF_EXP:
                down_grad_ref[row : row + 128, cols] = grads
            else:
                shared_grad_ref[:, cols] = grads
    move(down_grad_ref, down_grad_any)
    move(shared_grad_ref, shared_grad_any)
    take_turns(scatter)
    for copy in moving:
        copy.wait()
    side_end(*backs)
    for copy in started + summed:
        copy.wait_send()


def experts(piece, side, rows_cot, up, shared, down, shared_down):
    return pl.pallas_call(
        experts_kernel,
        out_shape=(
            jax.ShapeDtypeStruct((PIECE, D), FULL),
            jax.ShapeDtypeStruct((GROUPS, 8, 128), FULL),
            jax.ShapeDtypeStruct((GROUPS, PIECE, D), LOW),
            jax.ShapeDtypeStruct((D, HIDDEN_COLS), LOW),
            jax.ShapeDtypeStruct((FF_EXP, D), LOW),
            jax.ShapeDtypeStruct((SH_HERE, D), LOW),
        ),
        in_specs=[vmem_spec()] * 2 + [any_spec()] * 5,
        out_specs=(vmem_spec(),) * 2 + (any_spec(),) * 4,
        scratch_shapes=[
            pltpu.VMEM((GROUPS, PIECE, D), LOW),
            pltpu.VMEM((D, 2 * FF_EXP), LOW),
            pltpu.VMEM((D, 2 * SH_HERE), LOW),
            pltpu.VMEM((FF_EXP, D), LOW),
            pltpu.VMEM((SH_HERE, D), LOW),
            pltpu.VMEM((GROUPS, PIECE, D), LOW),
            pltpu.VMEM((D, HIDDEN_COLS), LOW),
            pltpu.VMEM((FF_EXP, D), LOW),
            pltpu.VMEM((SH_HERE, D), LOW),
            pltpu.VMEM((GROUPS, PIECE, D), LOW),
            pltpu.VMEM((GROUPS, 8, 128), FULL),
            pltpu.VMEM((GROUPS, PIECE, D), LOW),
            pltpu.VMEM((SEQ_LEN, HIDDEN_COLS), LOW),
            pltpu.VMEM((SEQ_LEN, UNITS), LOW),
            pltpu.VMEM((GROUPS, 8, 128), FULL),
        ]
        + scatter_buffers(PIECE, D)
        + [dma_sems(9), dma_sems(9), pltpu.SemaphoreType.DMA]
        + [dma_sems(GROUPS), dma_sems(GROUPS), pltpu.SemaphoreType.DMA]
        + [dma_sems(13), dma_sems(13)]
        + [dma_sems(GROUPS), dma_sems(GROUPS), pltpu.SemaphoreType.DMA]
        + [dma_sems(5)],
        compiler_params=pltpu.CompilerParams(
            collective_id=5, has_side_effects=True, vmem_limit_bytes=52 << 20
        ),
        cost_estimate=BUSY,
        name="experts",
    )(piece, side, rows_cot, up, shared, down, shared_down)


def swap_start(x_ref, out_ref, send_sem, recv_sem, local_sem):
    return side_start(x_ref, out_ref, True, send_sem, recv_sem, local_sem)


def columns_kernel(x_ref, x_out, x_send, x_recv, x_local):
    meet(all_peers())
    side_end(*swap_start(x_ref, x_out, x_send, x_recv, x_local))


def columns_out(blocks):
    return pl.pallas_call(
        columns_kernel,
        out_shape=jax.ShapeDtypeStruct(blocks.shape, blocks.dtype),
        in_specs=[any_spec()],
        out_specs=any_spec(),
        scratch_shapes=[dma_sems(GROUPS), dma_sems(GROUPS), pltpu.SemaphoreType.DMA],
        compiler_params=pltpu.CompilerParams(collective_id=1, has_side_effects=True),
        cost_estimate=BUSY,
        name="columns_out",
    )(blocks)


def back_kernel(x_ref, u_ref, side_ref, x_out, u_out, side_out, *sems):
    meet(all_peers())
    swaps = [
        swap_start(x_ref, x_out, *sems[:3]),
        swap_start(u_ref, u_out, *sems[3:6]),
        swap_start(side_ref, side_out, *sems[6:]),
    ]
    for swap in swaps:
        side_end(*swap)


def columns_back(blocks, shared, side):
    return pl.pallas_call(
        back_kernel,
        out_shape=(
            jax.ShapeDtypeStruct(blocks.shape, blocks.dtype),
            jax.ShapeDtypeStruct(shared.shape, shared.dtype),
            jax.ShapeDtypeStruct(side.shape, side.dtype),
        ),
        in_specs=[any_spec()] * 3,
        out_specs=(any_spec(),) * 3,
        scratch_shapes=[dma_sems(GROUPS), dma_sems(GROUPS), pltpu.SemaphoreType.DMA] * 3,
        compiler_params=pltpu.CompilerParams(collective_id=10, has_side_effects=True),
        cost_estimate=BUSY,
        name="columns_back",
    )(blocks, shared, side)


TILE = 256
TILES = SEQ_LEN // TILE
PAIRS = HEADS_HERE // 2


def scan_lanes(values, backward):
    length = values.shape[1]
    lane = lax.broadcasted_iota(jnp.int32, values.shape, 1)
    step = 1
    while step < length:
        if backward:
            values = values + jnp.where(lane < length - step, pltpu.roll(values, length - step, 1), 0.0)
        else:
            values = values + jnp.where(lane >= step, pltpu.roll(values, step, 1), 0.0)
        step *= 2
    return values


def sigmoid(values):
    return 1.0 / (1.0 + jnp.exp(-values))


def conv_taps(padded, taps, at):
    total = taps[0:1, at] * padded[5 : 5 + SEQ_LEN]
    for tap in range(1, CONV):
        total = total + taps[tap : tap + 1, at] * padded[5 + tap : 5 + tap + SEQ_LEN]
    return total


def scores_and_columns(b_state, c_state, cum_rows, scores, columns):
    for low in range(TILES):
        for far in range(low + 1):
            scores[low * TILE : (low + 1) * TILE, far * TILE : (far + 1) * TILE] = dot_rhs_t(
                c_state[low * TILE : (low + 1) * TILE], b_state[far * TILE : (far + 1) * TILE]
            )
    turned = jnp.concatenate([cum_rows, jnp.zeros((120, SEQ_LEN), FULL)], axis=0).T
    for head in range(HEADS_HERE):
        columns[head] = jnp.broadcast_to(turned[:, head : head + 1], (SEQ_LEN, 128))


def decay_tile(columns, cum_ref, head, low, far):
    column = columns[head, low * TILE : (low + 1) * TILE]
    row = cum_ref[pl.ds(head, 1), far * TILE : (far + 1) * TILE]
    return jnp.exp(jnp.minimum(jnp.concatenate([column] * (TILE // 128), axis=1) - row, 0.0))


def lower_tile():
    shape = (TILE, TILE)
    return lax.broadcasted_iota(jnp.int32, shape, 0) >= lax.broadcasted_iota(jnp.int32, shape, 1)


def mixer_forward_kernel(
    unit_any,
    first_ref,
    weight_any,
    out_weight_ref,
    taps_ref,
    bias_ref,
    head_ref,
    gain_ref,
    skip_ref,
    cot_ref,
    shared_ref,
    shared_down_ref,
    proj_any,
    act_any,
    mixed_any,
    gated_any,
    part_any,
    side_ref,
    cum_ref,
    step_ref,
    cot_out,
    shared_out,
    shared_down_out,
    unit_ref,
    weight_ref,
    proj_ref,
    act_ref,
    mixed_ref,
    gated_ref,
    part_ref,
    padded,
    scores,
    columns,
    scaled_ref,
    c_send,
    c_recv,
    c_local,
    moves,
    u_send,
    u_recv,
    d_send,
    d_recv,
    keeps,
):
    moving = []

    def move(source, target):
        copy = pltpu.make_async_copy(source, target, moves.at[len(moving)])
        copy.start()
        moving.append(copy)

    move(weight_any, weight_ref)
    move(unit_any, unit_ref)
    me, slot, device = seq_axis()
    core, f_slot, f_device, twin = fsdp_axis()
    meet(ring_peers(device) + ring_peers(f_device) + [twin])
    mine = f_slot(0, False) * 2 + core
    started, u_started, d_started, crossing, kept = [], [], [], [], []
    program = ring_gather(
        cot_ref, lambda at, cut: cot_out.at[(at, *cut)], slot, device, sender(c_send, c_recv, started), nothing
    )
    next(program)
    keep = pltpu.make_async_copy(cot_ref, cot_out.at[me], c_local)
    keep.start()
    shards = [
        shard_gather(shared_ref, shared_out, u_send, u_recv, u_started, crossing),
        shard_gather(shared_down_ref, shared_down_out, d_send, d_recv, d_started, crossing, False),
    ]
    for index, (source, block) in enumerate(
        ((shared_ref, shared_out.at[mine]), (shared_down_ref, shared_down_out.at[mine]))
    ):
        kept.append(pltpu.make_async_copy(source, block, keeps.at[index]))
        kept[-1].start()
    follow("y", program, shards)
    for copy in moving:
        copy.wait()
    moving.clear()

    def rows_step(tile, carry):
        here = pl.ds(pl.multiple_of(tile * TILE, TILE), TILE)
        normed = (unit_ref[here, :].astype(FULL) * first_ref[...]).astype(LOW)
        for part in range(PROJ_HERE // 384):
            at = slice(part * 384, (part + 1) * 384)
            proj_ref[here, at] = dot(normed, weight_ref[:, at]).astype(LOW)
        return carry

    lax.fori_loop(0, TILES, rows_step, 0)
    move(proj_ref, proj_any)
    follow("yyyzzz", program, shards)
    padded[0:8] = jnp.zeros((8, 128), FULL)
    for part in range(CONV_HERE // 128):
        at = slice(part * 128, (part + 1) * 128)
        padded[8:] = proj_ref[:, INNER_HERE + part * 128 : INNER_HERE + (part + 1) * 128].astype(FULL)
        before = bias_ref[0:1, at] + conv_taps(padded, taps_ref, at)
        act_ref[:, at] = (before * sigmoid(before)).astype(LOW)
    rates = proj_ref[:, INNER_HERE + CONV_HERE :].astype(FULL).T[:8] + head_ref[0][:, :1]
    step_ref[...] = jnp.maximum(rates, 0.0) + jnp.log1p(jnp.exp(-jnp.abs(rates)))
    cum_ref[...] = scan_lanes(step_ref[...] * head_ref[1][:, :1], False)
    scores_and_columns(
        act_ref[:, INNER_HERE : INNER_HERE + STATE],
        act_ref[:, INNER_HERE + STATE :],
        cum_ref[...],
        scores,
        columns,
    )
    move(act_ref, act_any)
    follow("yy", program, shards)

    def pair_step(pair, carry):
        at = pl.ds(pl.multiple_of(pair * 128, 128), 128)
        for low in range(TILES):
            here = slice(low * TILE, (low + 1) * TILE)
            sums = [None, None]
            for far in range(low + 1):
                there = slice(far * TILE, (far + 1) * TILE)
                for half in range(2):
                    head = pair * 2 + half
                    weight = scores[here, there] * decay_tile(columns, cum_ref, head, low, far)
                    weight = weight * step_ref[pl.ds(head, 1), there]
                    if far == low:
                        weight = jnp.where(lower_tile(), weight, 0.0)
                    term = dot(weight.astype(LOW), act_ref[there, at])
                    sums[half] = term if far == 0 else sums[half] + term
            first = lax.broadcasted_iota(jnp.int32, (TILE, 128), 1) < HDIM
            x_tile = act_ref[here, at].astype(FULL)
            mixed = jnp.where(first, sums[0], sums[1]) + skip_ref[0:1, at] * x_tile
            gate = proj_ref[here, at].astype(FULL)
            gated = (mixed * (gate * sigmoid(gate))).astype(LOW)
            mixed_ref[here, at] = mixed
            gated_ref[here, at] = gated
            scaled_ref[here, at] = (gated.astype(FULL) * gain_ref[0:1, at]).astype(LOW)
        return carry

    lax.fori_loop(0, PAIRS, pair_step, 0)
    move(mixed_ref, mixed_any)
    move(gated_ref, gated_any)
    follow("yyyyzzzz", program, shards)

    def out_step(tile, carry):
        here = pl.ds(pl.multiple_of(tile * TILE, TILE), TILE)
        for part in range(D // 512):
            at = slice(part * 512, (part + 1) * 512)
            part_ref[here, at] = dot(scaled_ref[here, :], out_weight_ref[:, at]).astype(LOW)
        return carry

    lax.fori_loop(0, TILES, out_step, 0)
    move(part_ref, part_any)
    wide = gated_ref[...].astype(FULL)
    squares = lax.dot_general(
        jnp.ones((8, INNER_HERE), FULL),
        wide * wide,
        (((1,), (1,)), ((), ())),
        precision=HIGHEST,
        preferred_element_type=FULL,
    )
    for piece in range(GROUPS):
        side_ref[piece] = squares[:, piece * PIECE : (piece + 1) * PIECE]
    take_turns(program, *shards)
    for copy in moving + kept:
        copy.wait()
    for copy in crossing:
        copy.wait_recv()
    for copy in started + u_started + d_started:
        copy.wait_send()
    keep.wait()


def mixer_forward(unit_rows, gain_first, weights, out_weights, taps, bias, head_cols, gain, skip, piece, shared, shared_down):
    return pl.pallas_call(
        mixer_forward_kernel,
        out_shape=(
            jax.ShapeDtypeStruct((SEQ_LEN, PROJ_HERE), LOW),
            jax.ShapeDtypeStruct((SEQ_LEN, CONV_HERE), LOW),
            jax.ShapeDtypeStruct((SEQ_LEN, INNER_HERE), FULL),
            jax.ShapeDtypeStruct((SEQ_LEN, INNER_HERE), LOW),
            jax.ShapeDtypeStruct((SEQ_LEN, D), LOW),
            jax.ShapeDtypeStruct((GROUPS, 8, PIECE), FULL),
            jax.ShapeDtypeStruct((8, SEQ_LEN), FULL),
            jax.ShapeDtypeStruct((8, SEQ_LEN), FULL),
            jax.ShapeDtypeStruct((GROUPS, PIECE, D), LOW),
            jax.ShapeDtypeStruct((SHARDS, *shared.shape), LOW),
            jax.ShapeDtypeStruct((SHARDS, *shared_down.shape), LOW),
        ),
        in_specs=[any_spec(), vmem_spec(), any_spec()] + [vmem_spec()] * 6 + [any_spec()] * 3,
        out_specs=(any_spec(),) * 5 + (vmem_spec(),) * 3 + (any_spec(),) * 3,
        scratch_shapes=[
            pltpu.VMEM((SEQ_LEN, D), LOW),
            pltpu.VMEM((D, PROJ_HERE), LOW),
            pltpu.VMEM((SEQ_LEN, PROJ_HERE), LOW),
            pltpu.VMEM((SEQ_LEN, CONV_HERE), LOW),
            pltpu.VMEM((SEQ_LEN, INNER_HERE), FULL),
            pltpu.VMEM((SEQ_LEN, INNER_HERE), LOW),
            pltpu.VMEM((SEQ_LEN, D), LOW),
            pltpu.VMEM((SEQ_LEN + 8, 128), FULL),
            pltpu.VMEM((SEQ_LEN, SEQ_LEN), FULL),
            pltpu.VMEM((HEADS_HERE, SEQ_LEN, 128), FULL),
            pltpu.VMEM((SEQ_LEN, INNER_HERE), LOW),
            dma_sems(9),
            dma_sems(9),
            pltpu.SemaphoreType.DMA,
            dma_sems(6),
        ]
        + [dma_sems(19)] * 4
        + [dma_sems(2)],
        compiler_params=pltpu.CompilerParams(
            collective_id=3, has_side_effects=True, vmem_limit_bytes=52 << 20
        ),
        cost_estimate=BUSY,
        name="mixer_forward",
    )(unit_rows, gain_first, weights, out_weights, taps, bias, head_cols, gain, skip, piece, shared, shared_down)


def mixer_backward_kernel(
    grad_ref,
    proj_ref,
    act_ref,
    mixed_ref,
    cum_ref,
    step_ref,
    taps_ref,
    bias_ref,
    head_ref,
    skip_ref,
    block_any,
    down_any,
    owned_any,
    out_ref,
    conv_ref,
    skip_grad_ref,
    head_grad_ref,
    block_out,
    down_out,
    owned_out,
    padded,
    trailing,
    scores,
    score_grad,
    columns,
    mixed_low,
    act_grad,
    size_rows,
    flow_rows,
    row_sums,
    mixed_back,
    block_ref,
    down_ref,
    owned_ref,
    stages,
    *rest,
):
    me, slot, device = seq_axis()
    block_ready_ref = staged(block_any, block_ref, stages.at[0])
    downs_ready = staged(down_any, down_ref, stages.at[1])
    owned_ready = staged(owned_any, owned_ref, stages.at[2])
    meet(ring_peers(device) + shard_peers())
    started = [[]]
    shards = shard_scatters(
        [
            (blocks_of(down_any), ready_blocks(downs_ready), down_out, rest[10 : 10 + SHARD_SCRATCH]),
            (blocks_of(owned_any), ready_blocks(owned_ready), owned_out, rest[10 + SHARD_SCRATCH :]),
        ],
        started,
    )
    send = sender(rest[8], rest[9], started[0])
    program = ring_scatter(
        block_ready(block_ready_ref, slot), slot, device, send, block_out, rest[:8], block_of(block_any, slot)
    )
    next(program)
    scores_and_columns(
        act_ref[:, INNER_HERE : INNER_HERE + STATE],
        act_ref[:, INNER_HERE + STATE :],
        cum_ref[...],
        scores,
        columns,
    )
    size_rows[...] = jnp.zeros((8, SEQ_LEN), FULL)
    flow_rows[...] = jnp.zeros((8, SEQ_LEN), FULL)
    for part in range(PAIRS):
        at = slice(part * 128, (part + 1) * 128)
        gate = proj_ref[:, at].astype(FULL)
        gate_sig = sigmoid(gate)
        grad = grad_ref[:, at].astype(FULL)
        mixed_grad = grad * (gate * gate_sig)
        out_ref[:, at] = (grad * mixed_ref[:, at] * (gate_sig * (1.0 + gate * (1.0 - gate_sig)))).astype(LOW)
        x_tile = act_ref[:, at].astype(FULL)
        skip_grad_ref[:, at] = jnp.broadcast_to(jnp.sum(mixed_grad * x_tile, axis=0, keepdims=True), (8, 128))
        mixed_low[:, at] = mixed_grad.astype(LOW)
        act_grad[:, at] = skip_ref[0:1, at] * mixed_grad
    follow("zzy", program, shards)

    def pair_step(pair):
        at = slice(pair * 128, (pair + 1) * 128)
        first = lax.broadcasted_iota(jnp.int32, (TILE, 128), 1) < HDIM
        for half in range(2):
            head = pair * 2 + half
            mine = first if half == 0 else jnp.logical_not(first)
            for low in range(TILES):
                here = slice(low * TILE, (low + 1) * TILE)
                grad = jnp.where(mine, mixed_low[here, at], jnp.zeros((TILE, 128), LOW))
                turned = mixed_low[here, at].T[half * HDIM : (half + 1) * HDIM]
                sums = jnp.zeros((TILE, 128), FULL)
                for far in range(low + 1):
                    there = slice(far * TILE, (far + 1) * TILE)
                    decay = decay_tile(columns, cum_ref, head, low, far)
                    if far == low:
                        decay = jnp.where(lower_tile(), decay, 0.0)
                    step = step_ref[pl.ds(head, 1), there]
                    scaled = dot_rhs_t(grad, act_ref[there, at]) * decay
                    product = scaled * scores[here, there]
                    size_rows[pl.ds(head, 1), there] += jnp.sum(product, axis=0, keepdims=True)
                    flow = product * step
                    for part in range(TILE // 128):
                        sums = sums + flow[:, part * 128 : (part + 1) * 128]
                    add = scaled * step
                    if half == 0 and pair == 0:
                        score_grad[here, there] = add
                    else:
                        score_grad[here, there] += add
                    weight = (scores[here, there] * decay * step).astype(LOW)
                    mixed_back[half * HDIM : (half + 1) * HDIM, there] += dot(turned, weight)
                row_sums[...] = sums
                flow_rows[pl.ds(head, 1), here] = lax.dot_general(
                    jnp.ones((8, 128), FULL),
                    row_sums[...],
                    (((1,), (1,)), ((), ())),
                    precision=HIGHEST,
                    preferred_element_type=FULL,
                )[:1]

    for pair in range(PAIRS):
        mixed_back[...] = jnp.zeros((128, SEQ_LEN), FULL)
        pair_step(pair)
        act_grad[:, pair * 128 : (pair + 1) * 128] += mixed_back[...].T
        follow(("yyz", "yz", "y")[pair], program, shards)

    b_at, c_at = INNER_HERE, INNER_HERE + STATE
    mixed_back[...] = jnp.zeros((128, SEQ_LEN), FULL)
    for low in range(TILES):
        here = slice(low * TILE, (low + 1) * TILE)
        for far in range(low + 1):
            there = slice(far * TILE, (far + 1) * TILE)
            high, rest = hi_lo(score_grad[here, there])
            b_tile, c_tile = act_ref[there, b_at:c_at], act_ref[here, c_at:]
            c_term = dot(high, b_tile) + dot(rest, b_tile)
            if far == 0:
                c_turned = c_tile.T
            mixed_back[:, there] += dot(c_turned, high) + dot(c_turned, rest)
            if far == 0:
                act_grad[here, c_at:] = c_term
            else:
                act_grad[here, c_at:] += c_term
    act_grad[:, b_at:c_at] = mixed_back[...].T

    step, size = step_ref[...], size_rows[...]
    decay_rate = head_ref[1][:, :1]
    back = scan_lanes(flow_rows[...] - step * size, True)
    rates = proj_ref[:, INNER_HERE + CONV_HERE :].astype(FULL).T[:8] + head_ref[0][:, :1]
    rate_grad = (size + back * decay_rate) * sigmoid(rates)
    real = lax.broadcasted_iota(jnp.int32, (8, SEQ_LEN), 0) < HEADS_HERE
    rate_grad = jnp.where(real, rate_grad, 0.0)
    head_grad_ref[0] = jnp.broadcast_to(jnp.sum(rate_grad, axis=1, keepdims=True), (8, 128))
    head_grad_ref[1] = jnp.broadcast_to(jnp.sum(back * step * decay_rate, axis=1, keepdims=True), (8, 128))
    turned = jnp.concatenate([rate_grad, jnp.zeros((120, SEQ_LEN), FULL)], axis=0).T
    out_ref[:, INNER_HERE + CONV_HERE :] = turned.astype(LOW)

    padded[0:8] = jnp.zeros((8, 128), FULL)
    trailing[SEQ_LEN:] = jnp.zeros((8, 128), FULL)
    for part in range(CONV_HERE // 128):
        at = slice(part * 128, (part + 1) * 128)
        wide = slice(INNER_HERE + part * 128, INNER_HERE + (part + 1) * 128)
        padded[8:] = proj_ref[:, wide].astype(FULL)
        before = bias_ref[0:1, at] + conv_taps(padded, taps_ref, at)
        gate = sigmoid(before)
        grad = act_grad[:, at] * (gate * (1.0 + before * (1.0 - gate)))
        trailing[:SEQ_LEN] = grad
        conv_ref[CONV : CONV + 1, at] = jnp.sum(grad, axis=0, keepdims=True)
        total = None
        for tap in range(CONV):
            conv_ref[tap : tap + 1, at] = jnp.sum(
                trailing[:SEQ_LEN] * padded[5 + tap : 5 + tap + SEQ_LEN], axis=0, keepdims=True
            )
            shift = CONV - 1 - tap
            term = taps_ref[tap : tap + 1, at] * trailing[shift : shift + SEQ_LEN]
            total = term if total is None else total + term
        out_ref[:, wide] = total.astype(LOW)
    conv_ref[CONV + 1 :] = jnp.zeros((3, CONV_HERE), FULL)
    take_turns(program, *shards)
    for copies in started:
        for copy in copies:
            copy.wait_send()


def mixer_backward(grad, projected, act, mixed, cum, step, taps, bias, head_cols, skip, blocks, downs, owned):
    return pl.pallas_call(
        mixer_backward_kernel,
        out_shape=(
            jax.ShapeDtypeStruct((SEQ_LEN, PROJ_HERE), LOW),
            jax.ShapeDtypeStruct((8, CONV_HERE), FULL),
            jax.ShapeDtypeStruct((8, INNER_HERE), FULL),
            jax.ShapeDtypeStruct((2, 8, 128), FULL),
            jax.ShapeDtypeStruct((PIECE, D), FULL),
            jax.ShapeDtypeStruct((32, D), FULL),
            jax.ShapeDtypeStruct((32, D), FULL),
        ),
        in_specs=[vmem_spec()] * 10 + [any_spec()] * 3,
        out_specs=(vmem_spec(),) * 7,
        scratch_shapes=[
            pltpu.VMEM((SEQ_LEN + 8, 128), FULL),
            pltpu.VMEM((SEQ_LEN + 8, 128), FULL),
            pltpu.VMEM((SEQ_LEN, SEQ_LEN), FULL),
            pltpu.VMEM((SEQ_LEN, SEQ_LEN), FULL),
            pltpu.VMEM((HEADS_HERE, SEQ_LEN, 128), FULL),
            pltpu.VMEM((SEQ_LEN, INNER_HERE), LOW),
            pltpu.VMEM((SEQ_LEN, CONV_HERE), FULL),
            pltpu.VMEM((8, SEQ_LEN), FULL),
            pltpu.VMEM((8, SEQ_LEN), FULL),
            pltpu.VMEM((TILE, 128), FULL),
            pltpu.VMEM((128, SEQ_LEN), FULL),
            pltpu.VMEM(blocks.shape, LOW),
            pltpu.VMEM(downs.shape, LOW),
            pltpu.VMEM(owned.shape, LOW),
            dma_sems(3),
        ]
        + scatter_buffers(PIECE, D)
        + [dma_sems(13), dma_sems(13)]
        + shard_scratch(downs)
        + shard_scratch(owned),
        compiler_params=pltpu.CompilerParams(
            collective_id=9, has_side_effects=True, vmem_limit_bytes=52 << 20
        ),
        cost_estimate=BUSY,
        name="mixer_backward",
    )(grad, projected, act, mixed, cum, step, taps, bias, head_cols, skip, blocks, downs, owned)


def adam_update(weight, old_first, old_second, gradient, step_rate, decay_rate):
    first_new = BETA_FIRST * old_first + (1.0 - BETA_FIRST) * gradient
    second_new = BETA_SECOND * old_second + (1.0 - BETA_SECOND) * gradient * gradient
    first_hat = first_new / (1.0 - BETA_FIRST**STEP)
    second_hat = second_new / (1.0 - BETA_SECOND**STEP)
    weight_new = weight - step_rate * (
        first_hat / (jnp.sqrt(second_hat) + ADAM_EPSILON) + decay_rate * weight
    )
    return (weight_new, first_new, second_new)


def update_kernel(dense_ref, shared_ref, aux_ref, owned_ref, up_ref, down_ref, gain_ref, *refs):
    olds = [refs[3 * index : 3 * index + 3] for index in range(9)]
    news = [refs[27 + 3 * index : 27 + 3 * index + 3] for index in range(9)]

    def step(index, gradient, rate, decay, at=()):
        old, new = olds[index], news[index]
        values = adam_update(old[0][at], old[1][at], old[2][at], gradient, rate, decay)
        for ref, value in zip(new, values):
            ref[at] = value

    rows = slice(None)
    state, rates = None, None
    place_row = lax.broadcasted_iota(jnp.int32, (128, 128), 0)
    place_col = lax.broadcasted_iota(jnp.int32, (128, 128), 1)
    for group in range(GROUPS):
        block = dense_ref[group].astype(FULL)
        for half in range(2):
            begin = half * INNER + group * INNER_HERE
            gradient = block[:, half * INNER_HERE : (half + 1) * INNER_HERE] * gain_ref[...]
            step(0, gradient, RATE_MATRIX, WEIGHT_DECAY, (rows, slice(begin, begin + INNER_HERE)))
            begin = half * FF_SH + group * SH_HERE
            gradient = shared_ref[group, :, half * SH_HERE : (half + 1) * SH_HERE].astype(FULL)
            step(1, gradient, RATE_MATRIX, WEIGHT_DECAY, (rows, slice(begin, begin + SH_HERE)))
        part = block[:, 2 * INNER_HERE : 2 * INNER_HERE + 2 * STATE]
        state = part if group == 0 else state + part
        moved = jnp.logical_and(place_row < HEADS_HERE, place_col == place_row + group * HEADS_HERE)
        part = dot(dense_ref[group, :, INNER_HERE + CONV_HERE : PROJ_HERE], moved.astype(LOW))
        rates = part if group == 0 else rates + part
    state, rates = state * gain_ref[...], rates * gain_ref[...]
    step(0, state, RATE_MATRIX, WEIGHT_DECAY, (rows, slice(2 * INNER, 2 * INNER + 2 * STATE)))
    step(0, rates[:, :HEADS], RATE_MATRIX, WEIGHT_DECAY, (rows, slice(INNER + CHANNELS, INNER + CHANNELS + HEADS)))
    step(2, owned_ref[:24], RATE_MATRIX, WEIGHT_DECAY, (slice(0, 24),))
    step(3, owned_ref[24:], RATE_MATRIX, WEIGHT_DECAY, (slice(0, 8),))

    def expert_step(index, sums, width, rate):
        def turn(count, carry):
            for row in range(8):
                at = count * 8 + row
                step(index, sums[pl.ds(at, 1), :width], rate, WEIGHT_DECAY, (at,))
            return carry

        lax.fori_loop(0, sums.shape[0] // 8, turn, 0)

    expert_step(4, up_ref, 2 * FF_EXP, RATE_MATRIX)
    expert_step(5, down_ref, D, RATE_DOWN)
    aux = aux_ref[0]
    for group in range(1, GROUPS):
        aux = aux + aux_ref[group]
    small = jnp.concatenate([aux[0:1, :89], aux[1:2, :89]], axis=1)
    step(6, small, RATE_SMALL, 0.0, (slice(0, 1),))
    step(7, aux[:, ROUTER_AT : ROUTER_AT + 12], RATE_MATRIX, WEIGHT_DECAY, (slice(0, 8),))
    step(8, aux[3:6, :HEADS], RATE_HEAD, 0.0, (slice(0, 3),))


def update(sums, triples):
    olds = [values for triple in triples for values in triple]
    news = pl.pallas_call(
        update_kernel,
        out_shape=tuple(jax.ShapeDtypeStruct(values.shape, FULL) for values in olds),
        in_specs=[vmem_spec()] * (7 + len(olds)),
        out_specs=(vmem_spec(),) * len(olds),
        compiler_params=pltpu.CompilerParams(vmem_limit_bytes=56 << 20),
        name="update",
    )(*sums, *olds)
    return [news[3 * index : 3 * index + 3] for index in range(len(triples))]


def route_combine(logit_values, onehot):
    picked = jnp.sum(logit_values[:, None, :] * onehot, axis=-1)
    route_probs = jax.nn.softmax(picked, axis=-1)
    return jnp.sum(route_probs[:, :, None] * onehot, axis=1)


def inverse_rms(values):
    return lax.rsqrt(jnp.mean(values * values, axis=-1, keepdims=True) + NORM_EPSILON)


def norm_back(values, inverse, gain, grad):
    shared = grad * gain
    inner = jnp.mean(values * shared, axis=-1, keepdims=True)
    grad_in = inverse * shared - values * (inverse * inverse * inverse * inner)
    return grad_in, jnp.sum(values * inverse * grad, axis=0)


def silu_slope(values, gate):
    return gate * (1.0 + values * (1.0 - gate))


def dot(left, right):
    return jnp.dot(left, right, preferred_element_type=FULL)


def dot_lhs_t(left, right):
    return lax.dot_general(left, right, (((0,), (0,)), ((), ())), preferred_element_type=FULL)


def dot_rhs_t(left, right):
    return lax.dot_general(left, right, (((1,), (1,)), ((), ())), preferred_element_type=FULL)


def side_rows(values):
    return jnp.pad(values, ((0, 0), (0, 7), (0, 0)))


def piece_order(forward):
    order = []
    for shard in range(SHARDS):
        for group in range(GROUPS):
            owner = shard * GROUPS + group
            user = ((shard % 2) * GROUPS + group) * GROUPS + shard // 2
            order.append((owner, user) if forward else (user, owner))
    return order


def local(
    hidden,
    cotangent,
    routes,
    head_params,
    head_first,
    head_second,
    small_params,
    small_first,
    small_second,
    proj_weight,
    proj_first,
    proj_second,
    out_weight,
    out_first,
    out_second,
    router_weight,
    router_first,
    router_second,
    experts_up,
    experts_up_first,
    experts_up_second,
    experts_down,
    experts_down_first,
    experts_down_second,
    shared_up,
    shared_up_first,
    shared_up_second,
    shared_down,
    shared_down_first,
    shared_down_second,
):
    group_index = lax.axis_index("seq")
    both = ("fsdp", "seq")
    inputs = hidden[0]
    out_grad = cotangent[0]

    proj_low = proj_weight.astype(LOW)
    misc = jnp.concatenate(
        [router_weight.astype(LOW), jnp.pad(small_params.astype(LOW), (0, 2)).reshape(12, SMALL_COLS)],
        axis=1,
    )
    columns = jnp.concatenate(
        [
            proj_low[:, :INNER].reshape(12, GROUPS, INNER_HERE),
            proj_low[:, INNER : 2 * INNER].reshape(12, GROUPS, INNER_HERE),
            jnp.broadcast_to(proj_low[:, None, 2 * INNER : INNER + CHANNELS], (12, GROUPS, 2 * STATE)),
            proj_low[:, INNER + CHANNELS :].reshape(12, GROUPS, HEADS_HERE),
            jnp.broadcast_to(misc[:, None], (12, GROUPS, 8 + SMALL_COLS)),
            jnp.zeros((12, GROUPS, 128 - HEADS_HERE - 8 - SMALL_COLS), LOW),
            shared_up.astype(LOW).reshape(12, 2, GROUPS, SH_HERE)[:, 0],
            shared_up.astype(LOW).reshape(12, 2, GROUPS, SH_HERE)[:, 1],
        ],
        axis=2,
    )
    columns = columns_out(columns.transpose(1, 0, 2)).reshape(96, -1)
    owned = jnp.concatenate([out_weight.astype(LOW), shared_down.astype(LOW)], axis=0)
    owned = lax.ppermute(owned, both, piece_order(True))

    first_inverse = inverse_rms(inputs)
    unit_rows, weights, out_here = start_gather(
        (inputs * first_inverse).astype(LOW), columns[:, :PROJ_HERE], owned[:24]
    )

    misc_at = INNER_HERE + CONV_HERE + HEADS_HERE
    misc = weights[:, misc_at : misc_at + EXPERTS + SMALL_COLS]
    router_full = misc[:, :EXPERTS]
    small_vec = (
        misc[:, EXPERTS:].reshape(SHARDS * GROUPS, 12 * SMALL_COLS)[:, :178].reshape(SMALL).astype(FULL)
    )
    gain_first, gain_second = small_vec[:D], small_vec[D : 2 * D]
    gain_mixer = lax.dynamic_slice_in_dim(small_vec, 2 * D + group_index * INNER_HERE, INNER_HERE)
    bias_all = small_vec[2 * D + INNER : 2 * D + INNER + CHANNELS]
    kernel_all = small_vec[2 * D + INNER + CHANNELS :].reshape(CONV, CHANNELS)
    conv_bias = jnp.concatenate(
        [lax.dynamic_slice_in_dim(bias_all, group_index * INNER_HERE, INNER_HERE), bias_all[INNER:]]
    )
    conv_kernel = jnp.concatenate(
        [
            lax.dynamic_slice_in_dim(kernel_all, group_index * INNER_HERE, INNER_HERE, 1),
            kernel_all[:, INNER:],
        ],
        axis=1,
    )
    head_local = lax.dynamic_slice_in_dim(head_params, group_index * HEADS_HERE, HEADS_HERE, 1)

    head_cols = jnp.stack([head_local[0], -jnp.exp(head_local[1])])
    head_cols = jnp.broadcast_to(jnp.pad(head_cols, ((0, 0), (0, 2)))[:, :, None], (2, 8, 128))
    skip_wide = jnp.repeat(head_local[2], HDIM)[None]
    projected, act, mixed, gated, out_part, square_side, cum_rows, step_rows, rows_cot, shared_here, shared_down_here = mixer_forward(
        unit_rows,
        gain_first[None],
        weights,
        out_here,
        conv_kernel,
        conv_bias[None],
        head_cols,
        gain_mixer[None],
        skip_wide,
        out_grad.astype(LOW),
        columns[:, PROJ_HERE:],
        owned[24:],
    )
    shared_here, shared_down_here = shared_here.reshape(D, 2 * SH_HERE), shared_down_here.reshape(SH_HERE, D)
    rows_cot = rows_cot.reshape(SEQ_LEN, D)
    raw_out, squares, up_here, down_here = mixed_scatter(
        out_part.reshape(GROUPS, PIECE, D),
        square_side,
        experts_up.reshape(96, 2 * FF_EXP).astype(LOW),
        experts_down.reshape(32, D).astype(LOW),
    )
    mixer_inverse = lax.rsqrt(jnp.sum(squares[:, 0], axis=0)[:, None] / INNER + NORM_EPSILON)
    middle = inputs + mixer_inverse * raw_out

    second_inverse = inverse_rms(middle)
    normed_two = (middle * second_inverse * gain_second).astype(LOW)
    logits = dot(normed_two, router_full)
    onehot = (routes[0][:, :, None] == jnp.arange(EXPERTS, dtype=jnp.int32)).astype(FULL)
    combine, route_pull = jax.vjp(lambda values: route_combine(values, onehot), logits)
    back_sum, combine_sides, block_part, up_total_grad, down_total_grad, shared_down_total_grad = experts(
        normed_two, combine.T, rows_cot.reshape(GROUPS, PIECE, D), up_here, shared_here, down_here, shared_down_here
    )

    logits_grad = route_pull(combine_sides[:, 0].T)[0].astype(LOW)
    normed_two_grad = back_sum + dot_rhs_t(logits_grad, router_full)
    router_grad = dot_lhs_t(logits_grad, normed_two)
    middle_from_norm, gain_second_grad = norm_back(middle, second_inverse, gain_second, normed_two_grad)
    middle_grad = out_grad + middle_from_norm
    mixer_grad = middle_grad.astype(LOW)
    mixer_inner = jnp.sum(mixer_grad.astype(FULL) * raw_out, axis=1, keepdims=True) / INNER
    mixer_fix = mixer_inverse * mixer_inverse * mixer_inverse * mixer_inner
    rows_mixer, stats, up_sum = middle_gather(
        mixer_grad,
        jnp.pad(jnp.concatenate([mixer_inverse, mixer_fix], axis=1).T, ((0, 6), (0, 0))),
        up_total_grad.reshape(SHARDS, 96, 2 * FF_EXP + 2 * SH_HERE),
    )

    rows_inverse = stats[:, 0].reshape(SEQ_LEN, 1)
    rows_fix = stats[:, 1].reshape(SEQ_LEN, 1)
    gated = gated.astype(FULL)
    gated_normed = (gated * rows_inverse * gain_mixer).astype(LOW)
    out_total_grad = dot_lhs_t(gated_normed, rows_mixer).astype(LOW)
    gated_normed_grad = dot_rhs_t(rows_mixer, out_here)
    gain_mixer_grad = jnp.sum(gated * rows_inverse * gated_normed_grad, axis=0)
    gated_grad = (rows_inverse * gain_mixer * gated_normed_grad - gated * rows_fix).astype(LOW)
    owned_grad = jnp.concatenate(
        [out_total_grad.reshape(SHARDS, 24, D), shared_down_total_grad.reshape(SHARDS, 8, D)], axis=1
    )

    proj_grad, conv_grads, skip_sums, head_sums, block_sum, down_sum, owned_sum = mixer_backward(
        gated_grad,
        projected,
        act,
        mixed,
        cum_rows,
        step_rows,
        conv_kernel,
        conv_bias[None],
        head_cols,
        skip_wide,
        block_part,
        down_total_grad.reshape(SHARDS, 32, D),
        owned_grad,
    )
    owned_sum = lax.ppermute(owned_sum.astype(LOW), both, piece_order(False)).astype(FULL)
    block_out = middle + block_sum
    conv_kernel_grad, conv_bias_grad = conv_grads[:CONV], conv_grads[CONV]
    skip_grad = jnp.sum(skip_sums[0].reshape(HEADS_HERE, HDIM), axis=1)
    bias_grad, log_decay_grad = head_sums[0, :HEADS_HERE, 0], head_sums[1, :HEADS_HERE, 0]
    unit_grad = dot_lhs_t(unit_rows, proj_grad)
    gain_first_grad = jnp.sum(unit_grad * weights.astype(FULL), axis=1)

    place = group_index * INNER_HERE
    kernel_wide = jnp.concatenate([jnp.zeros((CONV, INNER), FULL), conv_kernel_grad[:, INNER_HERE:]], axis=1)
    kernel_wide = lax.dynamic_update_slice_in_dim(kernel_wide, conv_kernel_grad[:, :INNER_HERE], place, 1)
    bias_wide = jnp.concatenate([jnp.zeros((INNER,), FULL), conv_bias_grad[INNER_HERE:]])
    bias_wide = lax.dynamic_update_slice_in_dim(bias_wide, conv_bias_grad[:INNER_HERE], place, 0)
    gain_wide = lax.dynamic_update_slice_in_dim(jnp.zeros((INNER,), FULL), gain_mixer_grad, place, 0)
    small_grad = jnp.concatenate(
        [gain_first_grad, gain_second_grad, gain_wide, bias_wide, kernel_wide.reshape(-1)]
    )
    small_grad = jnp.pad(small_grad.reshape(SHARDS * GROUPS, 2, 89), ((0, 0), (0, 6), (0, 39)))
    router_rows = router_grad.reshape(EXPERTS, SHARDS * GROUPS, 12).transpose(1, 0, 2)
    small_grad = (small_grad + jnp.pad(router_rows, ((0, 0), (0, 0), (ROUTER_AT, 116 - ROUTER_AT)))).astype(LOW)
    head_grad = jnp.stack([bias_grad, log_decay_grad, skip_grad])
    head_rows = lax.dynamic_update_slice_in_dim(
        jnp.zeros((3, 128), FULL), head_grad, group_index * HEADS_HERE, 1
    )
    head_rows = jnp.pad(jnp.concatenate(hi_lo(head_rows)), ((0, 2), (0, 0)))
    aux_grad = jnp.concatenate(
        [
            small_grad.reshape(SHARDS, 64, 128),
            jnp.broadcast_to(jnp.pad(head_rows, ((0, 24), (0, 0))), (SHARDS, 32, 128)),
        ],
        axis=1,
    )
    unit_low, owned_sum = lax.optimization_barrier((unit_grad.astype(LOW), owned_sum))
    normed_grad, column_sum, aux_sum = last_scatter(
        proj_grad, weights, unit_low.reshape(SHARDS, 96, PROJ_HERE), aux_grad
    )
    input_from_norm, unused = norm_back(inputs, first_inverse, gain_first, normed_grad)
    hidden_grad = middle_grad + input_from_norm

    shared_back = up_sum[:, 2 * FF_EXP :].astype(LOW).reshape(GROUPS, 12, 2 * SH_HERE)
    head_side = jnp.pad(aux_sum[64:67] + aux_sum[67:70], ((3, 2), (0, 0)))
    aux_side = aux_sum[:64].reshape(GROUPS, 8, 128) + head_side
    dense, shared_back, aux_back = columns_back(
        column_sum.astype(LOW).reshape(GROUPS, 12, PROJ_HERE), shared_back, aux_side
    )
    owner = lax.axis_index("fsdp") * GROUPS + group_index
    own_gain = lax.dynamic_slice_in_dim(gain_first, owner * 12, 12)[:, None]
    small_rows = [values[None] for values in (small_params, small_first, small_second)]
    router_rows = [values.T for values in (router_weight, router_first, router_second)]
    news = update(
        (dense, shared_back, aux_back, owned_sum, up_sum, down_sum, own_gain),
        (
            (proj_weight, proj_first, proj_second),
            (shared_up, shared_up_first, shared_up_second),
            (out_weight, out_first, out_second),
            (shared_down, shared_down_first, shared_down_second),
            (experts_up, experts_up_first, experts_up_second),
            (experts_down, experts_down_first, experts_down_second),
            small_rows,
            router_rows,
            (head_params, head_first, head_second),
        ),
    )
    proj_new, shared_up_new, out_new, shared_down_new, up_new, down_new, small_new, router_new, head_new = news
    small_new = [values[0] for values in small_new]
    router_new = [values.T for values in router_new]
    return (
        block_out[None],
        hidden_grad[None],
        *head_new,
        *small_new,
        *proj_new,
        *out_new,
        *router_new,
        *up_new,
        *down_new,
        *shared_up_new,
        *shared_down_new,
    )


def solution(mesh):
    return jax.shard_map(
        local,
        mesh=mesh,
        in_specs=(
            P("fsdp", "seq", None),
            P("fsdp", "seq", None),
            P("fsdp", "seq", None),
            P(),
            P(),
            P(),
            P(("fsdp", "seq")),
            P(("fsdp", "seq")),
            P(("fsdp", "seq")),
            P(("fsdp", "seq"), None),
            P(("fsdp", "seq"), None),
            P(("fsdp", "seq"), None),
            P(("fsdp", "seq"), None),
            P(("fsdp", "seq"), None),
            P(("fsdp", "seq"), None),
            P(("fsdp", "seq"), None),
            P(("fsdp", "seq"), None),
            P(("fsdp", "seq"), None),
            P("fsdp", "seq", None),
            P("fsdp", "seq", None),
            P("fsdp", "seq", None),
            P("fsdp", "seq", None),
            P("fsdp", "seq", None),
            P("fsdp", "seq", None),
            P(("fsdp", "seq"), None),
            P(("fsdp", "seq"), None),
            P(("fsdp", "seq"), None),
            P(("fsdp", "seq"), None),
            P(("fsdp", "seq"), None),
            P(("fsdp", "seq"), None),
        ),
        out_specs=(
            P("fsdp", "seq", None),
            P("fsdp", "seq", None),
            P(),
            P(),
            P(),
            P(("fsdp", "seq")),
            P(("fsdp", "seq")),
            P(("fsdp", "seq")),
            P(("fsdp", "seq"), None),
            P(("fsdp", "seq"), None),
            P(("fsdp", "seq"), None),
            P(("fsdp", "seq"), None),
            P(("fsdp", "seq"), None),
            P(("fsdp", "seq"), None),
            P(("fsdp", "seq"), None),
            P(("fsdp", "seq"), None),
            P(("fsdp", "seq"), None),
            P("fsdp", "seq", None),
            P("fsdp", "seq", None),
            P("fsdp", "seq", None),
            P("fsdp", "seq", None),
            P("fsdp", "seq", None),
            P("fsdp", "seq", None),
            P(("fsdp", "seq"), None),
            P(("fsdp", "seq"), None),
            P(("fsdp", "seq"), None),
            P(("fsdp", "seq"), None),
            P(("fsdp", "seq"), None),
            P(("fsdp", "seq"), None),
        ),
        check_vma=False,
    )
```
